32 devices in a mesh: orb: 8 (over y, x, core), pln: 4 (over z).
Axes of the slice: x: 2, y: 2, z: 4, core: 2. Of those that a mesh axis runs over, the one named last changes fastest.
Arguments:
- orbitals: bfloat16 [32, 32768], P('orb'), may hold values from -6 to 6
- occupations: float32 [32], P('orb'), may hold values from 0.5 to 2
- box_offsets: int32 [32, 3], P('orb'), may hold values from 0 to 96
- kernel_spectrum: float32 [256, 256, 256], P(None, 'pln', 'orb'), may hold values from 0.05 to 3.4, as said below
Outputs:
- hartree_terms: bfloat16 [32, 32768], P('orb', 'pln')
The draws below stay inside these ranges and needn't reach their ends.
Inputs may be any that keep to these rules, and one draw needn't show every extreme that they name: `box_offsets`: each orbital's box of 32 cells a side lies inside the fine grid. `kernel_spectrum`: positive and even: unchanged when any index k is replaced by (256 - k) mod 256.
All inputs are finite; a program needn't handle non-finite values.
Results may differ from the reference program's by a relative error of at most 0.003.
Values may be sent and summed in bfloat16 or wider, within the bound.
No kernel may reach another device: no remote copies, remote signals or barrier semaphores. Data moves between devices by JAX's collectives and lax.ppermute only.
A program may use at most 128 MiB of HBM per device.

```python
import math
import jax
import jax.numpy as jnp
from jax import lax

G = 128
BOX = 32
NORB = 32
M = 256
BOX3 = 32768


def draw_kernel_spectrum(key, part):
    half = M // 2 + 1
    steps = jnp.arange(M, dtype=jnp.int32)
    folded = jnp.minimum(steps, M - steps)
    rough = jnp.exp(jax.random.uniform(key, (half, half, half), jnp.float32, math.log(0.5), math.log(2.0)))
    strength = 8.0
    squares = (folded[:, None, None] ** 2 + folded[None, :, None] ** 2 + folded[None, None, :] ** 2).astype(jnp.float32)
    table = rough[folded[:, None, None], folded[None, :, None], folded[None, None, :]]
    return (0.1 * table * (1.0 + strength / (1.0 + squares / 4.0))).astype(jnp.float32)


def with_ends(entries, own_key, low, largest):
    spot = [jax.random.randint(jax.random.fold_in(own_key, axis), (), 0, length) for axis, length in enumerate(entries.shape)]
    widest = entries.shape.index(max(entries.shape))
    neighbour = spot[:widest] + [(spot[widest] + 1) % entries.shape[widest]] + spot[widest + 1:]
    return entries.at[tuple(spot)].set(low).at[tuple(neighbour)].set(largest)


def block_levels(key, shape, split, least, high):
    gain, own = 1.0, jax.random.fold_in(key, 6)
    for dim, shards_of in split:
        steps = jnp.exp(jax.random.uniform(jax.random.fold_in(own, dim), (shards_of,), jnp.float32, least / len(split), high / len(split)))
        gain = gain * jnp.repeat(steps, shape[dim] // shards_of).reshape([-1 if axis == dim else 1 for axis in range(len(shape))])
    return gain


def centred(rng, dims, scale, most, pieces=(), kind=jnp.bfloat16):
    factor_of = block_levels(rng, dims, pieces, -0.22, 0.18) if pieces else 1.0
    result = jax.random.normal(rng, dims, jnp.float32) * scale * factor_of
    return jnp.minimum(jnp.maximum(result, -most), most).astype(kind)


def setup_inputs(seed: int = 0) -> dict:
    streams_of = jax.random.split(jax.random.key(seed), 5)
    orbitals = centred(streams_of[0], (NORB, BOX3), 1.0, 6.0, ((0, 8),))
    occupations = jnp.clip(0.5 + 1.5 * jax.random.uniform(streams_of[1], (NORB,), jnp.float32) ** block_levels(streams_of[1], (NORB,), ((0, 8),), -0.2, 0.2), 0.5, 2.0)
    box_offsets = with_ends(jax.random.randint(streams_of[2], (NORB, 3), 0, G - BOX + 1), jax.random.fold_in(streams_of[2], 1), 0, G - BOX).astype(jnp.int32)
    kernel_spectrum = draw_kernel_spectrum(jax.random.fold_in(streams_of[4], 71), 0)
    return dict(orbitals=orbitals, occupations=occupations, box_offsets=box_offsets, kernel_spectrum=kernel_spectrum)


MAGIC_TAPS = (8.4334247333529341e-7, -1.2905572013420610e-5, 8.7629844762105596e-5, -3.0158038132690463e-4, 1.7472371367299390e-3, -9.4204703020108039e-3, 2.3738214637249424e-2, 6.1262589583120798e-2, 9.9404156978340040e-1, -6.0489528919698352e-2, -2.1030251609303814e-2, 1.3372634148547948e-2, -3.4412814449349386e-3, 4.9443227688689919e-4, -5.1859868811734329e-5, 2.7273449291197966e-6)
PRECISE = lax.Precision.HIGHEST


def magic_matrix(positions, width):
    taps = jnp.array(MAGIC_TAPS, dtype=jnp.float32)
    shifted = jnp.arange(width, dtype=jnp.int32)[None, :] - positions[:, None]
    hits = (shifted[:, :, None] == jnp.arange(-8, 8, dtype=jnp.int32)[None, None, :]).astype(jnp.float32)
    inside = ((positions >= 0) & (positions < width)).astype(jnp.float32)
    return jnp.sum(hits * taps, axis=2) * inside[:, None]


def expand(coef, filters):
    section = jnp.einsum('jk,kyx->jyx', filters, coef, precision=PRECISE)
    section = jnp.einsum('ak,jkx->jax', filters, section, precision=PRECISE)
    return jnp.einsum('bx,jax->jab', filters, section, precision=PRECISE)


def contract(weighted, filters):
    section = jnp.einsum('bx,jab->jax', filters, weighted, precision=PRECISE)
    section = jnp.einsum('ak,jax->jkx', filters, section, precision=PRECISE)
    return jnp.einsum('jk,jyx->kyx', filters, section, precision=PRECISE)


def reference(orbitals, occupations, box_offsets, kernel_spectrum):
    filters = magic_matrix(jnp.arange(BOX, dtype=jnp.int32), BOX)
    coefs = orbitals.astype(jnp.float32).reshape(NORB, BOX, BOX, BOX)

    def add_one(grid, item):
        coef, weight, corner = item
        psi = expand(coef, filters)
        where = (corner[0], corner[1], corner[2])
        current = lax.dynamic_slice(grid, where, (BOX, BOX, BOX))
        return lax.dynamic_update_slice(grid, current + weight * psi * psi, where), None

    density, _ = lax.scan(add_one, jnp.zeros((G, G, G), jnp.float32), (coefs, occupations, box_offsets.astype(jnp.int32)))
    padded = jnp.pad(density, ((0, G), (0, G), (0, G)))
    spectrum = jnp.fft.fftn(padded) * kernel_spectrum
    potential = jnp.real(jnp.fft.ifftn(spectrum))[:G, :G, :G].astype(jnp.float32)

    def apply_one(item):
        coef, corner = item
        psi = expand(coef, filters)
        local = lax.dynamic_slice(potential, (corner[0], corner[1], corner[2]), (BOX, BOX, BOX))
        return contract(local * psi, filters).reshape(BOX * BOX * BOX)

    terms = lax.map(apply_one, (coefs, box_offsets.astype(jnp.int32)))
    return terms.astype(jnp.bfloat16)
```

```python
import functools
import math

import jax
import jax.numpy as jnp
import numpy as np
from jax import lax
from jax.experimental import pallas as pl
from jax.experimental.pallas import tpu as pltpu
from jax.sharding import PartitionSpec as P

MAGIC_TAPS = (
    8.433424733352934e-07,
    -1.290557201342061e-05,
    8.76298447621056e-05,
    -0.00030158038132690465,
    0.001747237136729939,
    -0.009420470302010804,
    0.023738214637249424,
    0.0612625895831208,
    0.9940415697834004,
    -0.06048952891969835,
    -0.021030251609303816,
    0.013372634148547948,
    -0.0034412814449349387,
    0.0004944322768868992,
    -5.185986881173433e-05,
    2.7273449291197967e-06,
)
F32 = jnp.float32
BF16 = jnp.bfloat16
SUB = 8
VMEM_LIMIT = 48 * 1024 * 1024


def magic_filter(box):
    table = np.zeros((box, box))
    for row in range(box):
        for tap in range(-8, 8):
            if 0 <= row + tap < box:
                table[row, row + tap] = MAGIC_TAPS[tap + 8]
    return table.astype(np.float32).astype(np.float64)


def cas(product, doubled):
    angle = 2.0 * math.pi * (product % doubled) / doubled
    return np.cos(angle) + np.sin(angle)


def halves(table):
    high = np.asarray(table, np.float32).astype(jnp.bfloat16)
    low = (np.asarray(table, np.float64) - high.astype(np.float64)).astype(jnp.bfloat16)
    return high, low


def split(values):
    high = values.astype(BF16)
    low = (values - high.astype(F32)).astype(BF16)
    return high, low


def dot(left, right, dims=((1,), (0,))):
    return lax.dot_general(left, right, (dims, ((), ())), preferred_element_type=F32)


def table_dot(high, low, values):
    up, down = split(values)
    return dot(high, up) + dot(low, up) + dot(high, down)


def dot_table(values, high, low):
    up, down = split(values)
    return dot(up, high) + dot(up, low) + dot(down, high)


class Plan:
    def __init__(self, mesh, orbital_shape, kernel_shape):
        self.orb = mesh.shape["orb"]
        self.pln = mesh.shape["pln"]
        self.doubled = doubled = kernel_shape[0]
        self.grid = grid = doubled // 2
        self.box = box = round(orbital_shape[1] ** (1 / 3))
        self.per_group = grid // box
        self.groups = orbital_shape[0] // self.orb // self.per_group
        self.ky_block = kernel_shape[1] // self.pln
        self.kx_block = kernel_shape[2] // self.orb
        self.slots = SUB * -(-self.kx_block // (SUB * self.pln))
        self.half = self.pln // 2
        self.rows = self.orb * self.slots
        self.box_part = box // self.pln
        magic = magic_filter(box)
        eye = np.eye(SUB)
        depth = np.zeros((box, self.per_group, self.per_group, box))
        for n in range(self.per_group):
            depth[:, n, n, :] = magic.T
        depth = depth.reshape(grid, grid)
        self.depth = halves(depth)
        self.inner = halves(np.kron(eye, magic))
        self.outer = halves(np.kron(magic, eye))
        self.inner_back = halves(np.kron(eye, magic.T))
        self.outer_back = halves(np.kron(magic.T, eye))
        places = np.arange(grid)
        wave = np.zeros((self.pln, self.orb, self.slots, grid))
        for p in range(self.pln):
            for s in range(self.slots):
                within = p * self.slots + s
                if within < self.kx_block:
                    k = self.kx_block * np.arange(self.orb) + within
                    wave[p, :, s, :] = cas(k[:, None] * places[None, :], doubled)
        self.wave = wave.reshape(self.pln, self.rows, grid).astype(np.float32)
        along_z = cas(places[:, None] * np.arange(doubled)[None, :], doubled)
        self.forward_z = halves(along_z)
        self.inverse_z = halves(along_z.T / doubled)
        forward = np.zeros((self.pln, 2, grid, grid))
        weight = np.zeros((self.pln, 2, grid))
        for p in range(self.pln):
            group, index = divmod(p, self.half)
            base = grid * group
            for piece in range(self.half):
                block = (index - piece) % self.half
                for r in range(self.ky_block):
                    j = block * self.ky_block + r
                    row = piece * self.ky_block + r
                    angle = 2.0 * math.pi * ((base + j) * places % doubled) / doubled
                    forward[p, 0, row] = np.cos(angle)
                    forward[p, 1, row] = np.sin(angle)
                    weight[p, :, row] = 2.0
                    if j == 0:
                        edge = (base + grid) % doubled
                        forward[p, 1, row] = np.cos(2.0 * math.pi * (edge * places % doubled) / doubled)
                        weight[p, :, row] = 1.0
        inverse = forward * weight[..., None] / doubled**2
        self.forward_y = halves(forward.reshape(self.pln, doubled, grid))
        self.inverse_y = halves(inverse.reshape(self.pln, doubled, grid).transpose(0, 2, 1))


def lane_owner(shape, box):
    return lax.broadcasted_iota(jnp.int32, shape, len(shape) - 1) // box


def density_kernel(
    plan, where_ref, corner_ref, weight_ref, coef_ref, dh_ref, dl_ref, ih_ref, il_ref, oh_ref, ol_ref, wave_ref,
    send_ref, psi_ref, wave_out_ref, stage_ref,
):
    box, grid, count = plan.box, plan.grid, plan.per_group
    section = box * box
    group = pl.program_id(0)
    for p in range(box):
        stage_ref[count * p : count * (p + 1), :] = coef_ref[0, :, section * p : section * (p + 1)].astype(F32)
    coef = stage_ref[...].astype(BF16)
    doubled_coef = jnp.concatenate([coef, coef], axis=0)
    depth = jnp.concatenate([dh_ref[...], dl_ref[...]], axis=0)
    first = dot(doubled_coef, depth, ((0,), (0,)))
    span = SUB * box
    ih, il, oh, ol = ih_ref[...], il_ref[...], oh_ref[...], ol_ref[...]
    second = [table_dot(ih, il, first[span * t : span * (t + 1)]) for t in range(box // SUB)]
    second = jnp.concatenate(second, axis=0).reshape(box, box // SUB, SUB, grid)
    for t in range(box // SUB):
        third = table_dot(oh, ol, second[:, t].reshape(span, grid))
        psi_ref[0, :, SUB * t : SUB * (t + 1), :] = third.reshape(box, SUB, grid)
    owner = lane_owner((1, grid), box)
    whole_wave = wave_ref[where_ref[0]]
    wave = jnp.zeros_like(whole_wave)
    weight = jnp.zeros((1, grid), F32)
    for n in range(count):
        shift = lax.rem(box * n - corner_ref[group * count + n, 2] + grid, grid)
        wave = jnp.where(owner == n, pltpu.roll(whole_wave, shift, 1), wave)
        weight = jnp.where(owner == n, weight_ref[group * count + n], weight)
    wave_out_ref[0] = wave
    wave_both = jnp.concatenate(split(wave), axis=1)
    for pair in range(box // 2):
        columns = []
        for b in (2 * pair, 2 * pair + 1):
            psi = psi_ref[0, b]
            density = psi * psi * weight
            parts = [jnp.where(owner == n, density, 0.0) for n in range(count)]
            columns.append(jnp.concatenate(parts, axis=0).astype(BF16))
        both = jnp.concatenate(columns, axis=1)
        out = dot(wave_both, jnp.concatenate([both, both], axis=0))
        for o in range(plan.orb):
            rows = out[plan.slots * o : plan.slots * (o + 1)]
            tile = jnp.concatenate([rows[:, :grid], rows[:, grid:]], axis=0)
            send_ref[o, 0, 2 * plan.slots * pair : 2 * plan.slots * (pair + 1), :] = tile.astype(send_ref.dtype)


def solve_kernel(plan, where_ref, corner_ref, recv_ref, *refs):
    half, slots, grid, box, count = plan.half, plan.slots, plan.grid, plan.box, plan.per_group
    kernel_refs = refs[:half]
    edge_refs = refs[half : 2 * half]
    zh_ref, zl_ref, yh_ref, yl_ref, vh_ref, vl_ref, wh_ref, wl_ref, send_ref, field_ref = refs[2 * half :]
    index = where_ref[0]
    depth = box * slots
    owner = lane_owner((1, grid), box)
    field_ref[...] = jnp.zeros_like(field_ref)

    def start(number):
        return pl.multiple_of(corner_ref[number, 1] * slots, SUB)

    def place(group, carry):
        values = recv_ref[group].astype(F32)
        for n in range(count):
            number = group * count + n
            shift = lax.rem(corner_ref[number, 0] - box * n + grid, grid)
            moved = pltpu.roll(jnp.where(owner == n, values, 0.0), shift, 1)
            field_ref[pl.ds(start(number), depth), :] += moved
        return carry

    lax.fori_loop(0, plan.orb * plan.groups, place, 0)
    zh, zl, wh, wl = zh_ref[...], zl_ref[...], wh_ref[...], wl_ref[...]
    yh, yl, vh, vl = yh_ref[index], yl_ref[index], vh_ref[index], vl_ref[index]
    row = lax.broadcasted_iota(jnp.int32, (grid, 1), 0)
    edge_row = lax.rem(index, half) * plan.ky_block
    for s in range(slots):
        plane = field_ref[pl.ds(s, grid, stride=slots), :]
        modes = table_dot(yh, yl, dot_table(plane, zh, zl))
        kernel = jnp.concatenate([ref[:, s, :] for ref in kernel_refs], axis=0)
        edge = edge_refs[0][0, s : s + 1, :]
        for ref in edge_refs[1:]:
            edge = edge + ref[0, s : s + 1, :]
        other = jnp.where(row == edge_row, edge, kernel)
        modes = modes * jnp.concatenate([kernel, other], axis=0)
        plane = dot_table(table_dot(vh, vl, modes), wh, wl)
        field_ref[pl.ds(s, grid, stride=slots), :] = plane

    def cut(group, carry):
        values = jnp.zeros((depth, grid), F32)
        for n in range(count):
            number = group * count + n
            shift = lax.rem(box * n - corner_ref[number, 0] + grid, grid)
            rows = field_ref[pl.ds(start(number), depth), :]
            values = jnp.where(owner == n, pltpu.roll(rows, shift, 1), values)
        send_ref[group] = values.astype(send_ref.dtype)
        return carry

    lax.fori_loop(0, plan.orb * plan.groups, cut, 0)


def terms_kernel(
    plan, recv_ref, psi_ref, wave_ref, dh_ref, dl_ref, ih_ref, il_ref, oh_ref, ol_ref, send_ref, stage_ref,
):
    box, grid, count, slots = plan.box, plan.grid, plan.per_group, plan.slots
    owner = lane_owner((1, grid), box)
    high, low = split(wave_ref[0].T)
    wave = jnp.concatenate([high, low, high], axis=1)
    for pair in range(box // 2):
        columns = []
        for b in (2 * pair, 2 * pair + 1):
            columns.append(
                jnp.concatenate([recv_ref[o, 0, slots * b : slots * (b + 1), :].astype(F32) for o in range(plan.orb)], axis=0)
            )
        up, down = split(jnp.concatenate(columns, axis=1))
        out = dot(wave, jnp.concatenate([up, up, down], axis=0))
        for side, b in enumerate((2 * pair, 2 * pair + 1)):
            mine = out[:, grid * side : grid * (side + 1)]
            potential = jnp.zeros((box, grid), F32)
            for n in range(count):
                potential = jnp.where(owner == n, mine[box * n : box * (n + 1)], potential)
            stage_ref[b] = potential * psi_ref[0, b]
    span = SUB * box
    ih, il, oh, ol = ih_ref[...], il_ref[...], oh_ref[...], ol_ref[...]
    for t in range(box // SUB):
        values = stage_ref[SUB * t : SUB * (t + 1)].reshape(span, grid)
        stage_ref[SUB * t : SUB * (t + 1)] = table_dot(ih, il, values).reshape(SUB, box, grid)
    for t in range(box // SUB):
        values = stage_ref[:, SUB * t : SUB * (t + 1), :].reshape(span, grid)
        stage_ref[:, SUB * t : SUB * (t + 1), :] = table_dot(oh, ol, values).reshape(box, SUB, grid)
    up, down = split(stage_ref[...].reshape(box * box, grid))
    dh, dl = dh_ref[...], dl_ref[...]
    last = ((1,), (1,))
    out = dot(dh, up, last) + dot(dl, up, last) + dot(dh, down, last)
    part = plan.box_part * count
    for p in range(plan.pln):
        send_ref[p, 0] = out[part * p : part * (p + 1)].astype(send_ref.dtype)


def sum_kernel(plan, recv_ref, out_ref):
    total = recv_ref[0, 0].astype(F32)
    for p in range(1, plan.pln):
        total = total + recv_ref[p, 0].astype(F32)
    section = plan.box * plan.box
    count = plan.per_group
    for j in range(plan.box_part):
        out_ref[0, :, section * j : section * (j + 1)] = total[count * j : count * (j + 1)].astype(out_ref.dtype)


def whole_spec(array):
    rank = len(array.shape)
    return pl.BlockSpec(array.shape, lambda *_: (0,) * rank)


def per_device(plan, orbitals, occupations, box_offsets, kernel_spectrum):
    orb, pln, half, slots = plan.orb, plan.pln, plan.half, plan.slots
    groups, count, box, grid = plan.groups, plan.per_group, plan.box, plan.grid
    plane_index = lax.axis_index("pln")
    where = plane_index.astype(jnp.int32)[None]
    corners = lax.all_gather(box_offsets, "orb", axis=0, tiled=True)
    by_ky = jnp.transpose(kernel_spectrum, (1, 2, 0))

    def columns_for(target, rows):
        first = jnp.minimum(target * slots, max(plan.kx_block - slots, 0))
        return lax.dynamic_slice(by_ky, (0, first, 0), (rows, slots, plan.doubled))

    group_of, index = plane_index // half, plane_index % half
    pieces = [columns_for(plane_index, plan.ky_block)]
    for step in range(1, half):
        target = group_of * half + (index + step) % half
        pairs = [(g * half + i, g * half + (i + step) % half) for g in range(2) for i in range(half)]
        pieces.append(lax.ppermute(columns_for(target, plan.ky_block), "pln", pairs))
    edges = []
    for step in range(half):
        target = (1 - group_of) * half + step
        edges.append(lax.ppermute(columns_for(target, 1), "pln", [(0, half + step), (half, step)]))

    smem = pl.BlockSpec(memory_space=pltpu.SMEM)
    params = pltpu.CompilerParams(vmem_limit_bytes=VMEM_LIMIT)
    coefs = orbitals.reshape(groups, count, orbitals.shape[1])
    area = box * slots
    tables = [*plan.depth, *plan.inner, *plan.outer]
    send, psi, wave = pl.pallas_call(
        functools.partial(density_kernel, plan),
        grid=(groups,),
        in_specs=[smem, smem, smem, pl.BlockSpec((1, count, orbitals.shape[1]), lambda g: (g, 0, 0))]
        + [whole_spec(t) for t in tables]
        + [whole_spec(plan.wave)],
        out_specs=[
            pl.BlockSpec((orb, 1, area, grid), lambda g: (0, g, 0, 0)),
            pl.BlockSpec((1, box, box, grid), lambda g: (g, 0, 0, 0)),
            pl.BlockSpec((1, plan.rows, grid), lambda g: (g, 0, 0)),
        ],
        out_shape=[
            jax.ShapeDtypeStruct((orb, groups, area, grid), BF16),
            jax.ShapeDtypeStruct((groups, box, box, grid), F32),
            jax.ShapeDtypeStruct((groups, plan.rows, grid), F32),
        ],
        scratch_shapes=[pltpu.VMEM((grid, box * box), F32)],
        compiler_params=params,
        name="density",
    )(where, box_offsets, occupations, coefs, *tables, plan.wave)
    received = lax.all_to_all(send, "orb", split_axis=0, concat_axis=0, tiled=True)
    received = received.reshape(orb * groups, area, grid)
    tables = [*plan.forward_z, *plan.forward_y, *plan.inverse_y, *plan.inverse_z]
    blocks = [received, *pieces, *edges, *tables]
    send = pl.pallas_call(
        functools.partial(solve_kernel, plan),
        grid=(1,),
        in_specs=[smem, smem] + [whole_spec(t) for t in blocks],
        out_specs=pl.BlockSpec((orb * groups, area, grid), lambda g: (0, 0, 0)),
        out_shape=jax.ShapeDtypeStruct((orb * groups, area, grid), F32),
        scratch_shapes=[pltpu.VMEM((grid * slots, grid), F32)],
        compiler_params=params,
        name="solve",
    )(where, corners, *blocks)
    send = send.reshape(orb, groups, area, grid)
    received = lax.all_to_all(send, "orb", split_axis=0, concat_axis=0, tiled=True)
    tables = [*plan.depth, *plan.inner_back, *plan.outer_back]
    part = plan.box_part * count
    send = pl.pallas_call(
        functools.partial(terms_kernel, plan),
        grid=(groups,),
        in_specs=[
            pl.BlockSpec((orb, 1, area, grid), lambda g: (0, g, 0, 0)),
            pl.BlockSpec((1, box, box, grid), lambda g: (g, 0, 0, 0)),
            pl.BlockSpec((1, plan.rows, grid), lambda g: (g, 0, 0)),
        ]
        + [whole_spec(t) for t in tables],
        out_specs=pl.BlockSpec((pln, 1, part, box * box), lambda g: (0, g, 0, 0)),
        out_shape=jax.ShapeDtypeStruct((pln, groups, part, box * box), F32),
        scratch_shapes=[pltpu.VMEM((box, box, grid), F32)],
        compiler_params=params,
        name="terms",
    )(received, psi, wave, *tables)
    received = lax.all_to_all(send, "pln", split_axis=0, concat_axis=0, tiled=True)
    cells = plan.box_part * box * box
    result = pl.pallas_call(
        functools.partial(sum_kernel, plan),
        grid=(groups,),
        in_specs=[pl.BlockSpec((pln, 1, part, box * box), lambda g: (0, g, 0, 0))],
        out_specs=pl.BlockSpec((1, count, cells), lambda g: (g, 0, 0)),
        out_shape=jax.ShapeDtypeStruct((groups, count, cells), BF16),
        compiler_params=params,
        name="sum",
    )(received)
    return result.reshape(groups * count, cells)


def solution(mesh):
    in_specs = (P("orb", None), P("orb"), P("orb", None), P(None, "pln", "orb"))
    out_specs = P("orb", "pln")

    def whole(orbitals, occupations, box_offsets, kernel_spectrum):
        plan = Plan(mesh, orbitals.shape, kernel_spectrum.shape)
        return jax.shard_map(
            functools.partial(per_device, plan), mesh=mesh, in_specs=in_specs, out_specs=out_specs, check_vma=False
        )(orbitals, occupations, box_offsets, kernel_spectrum)

    return whole
```

```python
import functools
import math

import jax
import jax.numpy as jnp
import numpy as np
from jax import lax
from jax.experimental import pallas as pl
from jax.experimental.pallas import tpu as pltpu
from jax.sharding import PartitionSpec as P

MAGIC_TAPS = (
    8.433424733352934e-07,
    -1.290557201342061e-05,
    8.76298447621056e-05,
    -0.00030158038132690465,
    0.001747237136729939,
    -0.009420470302010804,
    0.023738214637249424,
    0.0612625895831208,
    0.9940415697834004,
    -0.06048952891969835,
    -0.021030251609303816,
    0.013372634148547948,
    -0.0034412814449349387,
    0.0004944322768868992,
    -5.185986881173433e-05,
    2.7273449291197967e-06,
)
F32 = jnp.float32
BF16 = jnp.bfloat16
SUB = 8
VMEM_LIMIT = 48 * 1024 * 1024


def magic_filter(box):
    table = np.zeros((box, box))
    for row in range(box):
        for tap in range(-8, 8):
            if 0 <= row + tap < box:
                table[row, row + tap] = MAGIC_TAPS[tap + 8]
    return table.astype(np.float32).astype(np.float64)


def cas(product, doubled):
    angle = 2.0 * math.pi * (product % doubled) / doubled
    return np.cos(angle) + np.sin(angle)


def halves(table):
    high = np.asarray(table, np.float32).astype(jnp.bfloat16)
    low = (np.asarray(table, np.float64) - high.astype(np.float64)).astype(jnp.bfloat16)
    return high, low


def split(values):
    high = values.astype(BF16)
    low = (values - high.astype(F32)).astype(BF16)
    return high, low


def dot(left, right, dims=((1,), (0,))):
    return lax.dot_general(left, right, (dims, ((), ())), preferred_element_type=F32)


def table_dot(high, low, values):
    up, down = split(values)
    return dot(high, up) + dot(low, up) + dot(high, down)


def dot_table(values, high, low):
    up, down = split(values)
    return dot(up, high) + dot(up, low) + dot(down, high)


class Plan:
    def __init__(self, mesh, orbital_shape, kernel_shape):
        self.orb = mesh.shape["orb"]
        self.pln = mesh.shape["pln"]
        self.doubled = doubled = kernel_shape[0]
        self.grid = grid = doubled // 2
        self.box = box = round(orbital_shape[1] ** (1 / 3))
        self.per_group = grid // box
        self.groups = orbital_shape[0] // self.orb // self.per_group
        self.ky_block = kernel_shape[1] // self.pln
        self.kx_block = kernel_shape[2] // self.orb
        self.slots = SUB * -(-self.kx_block // (SUB * self.pln))
        self.half = self.pln // 2
        self.rows = self.orb * self.slots
        self.area = box * self.slots
        self.box_part = box // self.pln
        magic = magic_filter(box)
        eye = np.eye(SUB)
        depth = np.zeros((box, self.per_group, self.per_group, box))
        for n in range(self.per_group):
            depth[:, n, n, :] = magic.T
        depth = depth.reshape(grid, grid)
        self.depth = halves(depth)
        self.inner = halves(np.kron(eye, magic))
        self.outer = halves(np.kron(magic, eye))
        self.inner_back = halves(np.kron(eye, magic.T))
        self.outer_back = halves(np.kron(magic.T, eye))
        places = np.arange(grid)
        wave = np.zeros((self.pln, self.orb, self.slots, grid))
        for p in range(self.pln):
            for s in range(self.slots):
                within = p * self.slots + s
                if within < self.kx_block:
                    k = self.kx_block * np.arange(self.orb) + within
                    wave[p, :, s, :] = cas(k[:, None] * places[None, :], doubled)
        self.wave = wave.reshape(self.pln, self.rows, grid).astype(np.float32)
        kz = np.concatenate([places, doubled - places])
        along_z = cas(places[:, None] * kz[None, :], doubled)
        along_z[:, grid] = 0.0
        self.forward_z = halves(along_z)
        self.inverse_z = halves(along_z.T / doubled)
        forward = np.zeros((self.pln, 2, grid, grid))
        weight = np.zeros((self.pln, 2, grid))
        for p in range(self.pln):
            group, index = divmod(p, self.half)
            base = grid * group
            for piece in range(self.half):
                block = (index - piece) % self.half
                for r in range(self.ky_block):
                    j = block * self.ky_block + r
                    row = piece * self.ky_block + r
                    angle = 2.0 * math.pi * ((base + j) * places % doubled) / doubled
                    forward[p, 0, row] = np.cos(angle)
                    forward[p, 1, row] = np.sin(angle)
                    weight[p, :, row] = 2.0
                    if j == 0:
                        edge = (base + grid) % doubled
                        forward[p, 1, row] = np.cos(2.0 * math.pi * (edge * places % doubled) / doubled)
                        weight[p, :, row] = 1.0
        inverse = forward * weight[..., None] / doubled**2
        self.forward_y = halves(forward.reshape(self.pln, doubled, grid))
        self.inverse_y = halves(inverse.reshape(self.pln, doubled, grid).transpose(0, 2, 1))


def lane_owner(shape, box):
    return lax.broadcasted_iota(jnp.int32, shape, len(shape) - 1) // box


def density_kernel(
    plan, where_ref, corner_ref, weight_ref, coef_ref, dh_ref, dl_ref, ih_ref, il_ref, oh_ref, ol_ref, wave_ref,
    send_ref, psi_ref, wave_out_ref, stage_ref,
):
    box, grid, count = plan.box, plan.grid, plan.per_group
    section = box * box
    group = pl.program_id(0)
    for p in range(box):
        stage_ref[count * p : count * (p + 1), :] = coef_ref[0, :, section * p : section * (p + 1)].astype(F32)
    coef = stage_ref[...].astype(BF16)
    doubled_coef = jnp.concatenate([coef, coef], axis=0)
    depth = jnp.concatenate([dh_ref[...], dl_ref[...]], axis=0)
    first = dot(doubled_coef, depth, ((0,), (0,)))
    span = SUB * box
    ih, il, oh, ol = ih_ref[...], il_ref[...], oh_ref[...], ol_ref[...]
    second = [table_dot(ih, il, first[span * t : span * (t + 1)]) for t in range(box // SUB)]
    second = jnp.concatenate(second, axis=0).reshape(box, box // SUB, SUB, grid)
    for t in range(box // SUB):
        third = table_dot(oh, ol, second[:, t].reshape(span, grid))
        psi_ref[0, :, SUB * t : SUB * (t + 1), :] = third.reshape(box, SUB, grid)
    owner = lane_owner((1, grid), box)
    whole_wave = wave_ref[where_ref[0]]
    wave = jnp.zeros_like(whole_wave)
    weight = jnp.zeros((1, grid), F32)
    for n in range(count):
        shift = lax.rem(box * n - corner_ref[group * count + n, 2] + grid, grid)
        wave = jnp.where(owner == n, pltpu.roll(whole_wave, shift, 1), wave)
        weight = jnp.where(owner == n, weight_ref[group * count + n], weight)
    wave_out_ref[0] = wave
    high, low = split(wave)
    wave_terms = jnp.concatenate([high, low, high], axis=1)
    kind = lax.broadcasted_iota(jnp.int32, (2 * SUB, 1), 0)
    corner = jnp.zeros((2 * SUB, grid), F32)
    for n in range(count):
        place = jnp.where(kind == 0, corner_ref[group * count + n, 0], corner_ref[group * count + n, 1])
        corner = jnp.where(owner == n, place.astype(F32), corner)
    for o in range(plan.orb):
        send_ref[o, 0, plan.area :, :] = corner.astype(send_ref.dtype)
    for pair in range(box // 2):
        columns = []
        for b in (2 * pair, 2 * pair + 1):
            psi = psi_ref[0, b]
            density = psi * psi * weight
            parts = [jnp.where(owner == n, density, 0.0) for n in range(count)]
            columns.append(jnp.concatenate(parts, axis=0))
        up, down = split(jnp.concatenate(columns, axis=1))
        out = dot(wave_terms, jnp.concatenate([up, up, down], axis=0))
        for o in range(plan.orb):
            rows = out[plan.slots * o : plan.slots * (o + 1)]
            tile = jnp.concatenate([rows[:, :grid], rows[:, grid:]], axis=0)
            send_ref[o, 0, 2 * plan.slots * pair : 2 * plan.slots * (pair + 1), :] = tile.astype(send_ref.dtype)


def spectrum_kernel(plan, where_ref, after_ref, spectrum_ref, *refs):
    half, slots, grid, rows = plan.half, plan.slots, plan.grid, plan.ky_block
    outs = refs[: 2 * half]
    block_ref, edge_ref, sems = refs[2 * half :]
    me = where_ref[0]
    group, index = me // half, lax.rem(me, half)
    copies = []

    def fetch(target, source, buffer, number):
        first = jnp.minimum(target * slots, max(plan.kx_block - slots, 0))
        first = pl.multiple_of(first, SUB)
        copy = pltpu.make_async_copy(source.at[:, pl.ds(first, slots), :], buffer, sems.at[number])
        copy.start()
        copies.append(copy)

    for step in range(half):
        fetch(group * half + lax.rem(index + step, half), spectrum_ref, block_ref.at[step], step)
    for step in range(half):
        fetch((1 - group) * half + step, spectrum_ref.at[pl.ds(0, 1)], edge_ref.at[pl.ds(step, 1)], half + step)
    odd = lax.rem(lax.broadcasted_iota(jnp.int32, (1, 1, grid), 2), 2) == 1

    def fold(values):
        last = values[:, :, grid : grid + 1]
        return values[:, :, :grid] + jnp.where(odd, last, -last)

    for step in range(half):
        copies[half + step].wait()
        outs[half + step][...] = fold(edge_ref[pl.ds(step, 1)])
    for step in list(range(1, half)) + [0]:
        copies[step].wait()
        outs[step][...] = fold(block_ref[step])


def solve_kernel(plan, where_ref, recv_ref, *refs):
    half, slots, grid, box, count = plan.half, plan.slots, plan.grid, plan.box, plan.per_group
    spectrum_refs = refs[:half]
    edge_refs = refs[half : 2 * half]
    zh_ref, zl_ref, yh_ref, yl_ref, vh_ref, vl_ref, wh_ref, wl_ref, send_ref = refs[2 * half : 2 * half + 9]
    field_ref, table_ref, corner_ref, sem = refs[2 * half + 9 :]
    index = where_ref[0]
    depth = plan.area
    all_groups = plan.orb * plan.groups
    owner = lane_owner((1, grid), box)
    for group in range(all_groups):
        tile = recv_ref[group, depth : depth + 2 * SUB, :].astype(F32).astype(jnp.int32)
        table_ref[2 * group : 2 * group + 2, :] = tile[:2]
    copy = pltpu.make_async_copy(table_ref, corner_ref, sem)
    copy.start()
    field_ref[...] = jnp.zeros_like(field_ref)
    copy.wait()

    def start(group, n):
        return pl.multiple_of(corner_ref[2 * group + 1, box * n] * slots, SUB)

    def place(group, carry):
        values = recv_ref[group, :depth, :].astype(F32)
        for n in range(count):
            shift = lax.rem(corner_ref[2 * group, box * n] - box * n + grid, grid)
            moved = pltpu.roll(jnp.where(owner == n, values, 0.0), shift, 1)
            field_ref[pl.ds(start(group, n), depth), :] += moved
        return carry

    lax.fori_loop(0, all_groups, place, 0)
    zh, zl, wh, wl = zh_ref[...], zl_ref[...], wh_ref[...], wl_ref[...]
    yh, yl, vh, vl = yh_ref[index], yl_ref[index], vh_ref[index], vl_ref[index]
    row = lax.broadcasted_iota(jnp.int32, (grid, 1), 0)
    edge_row = lax.rem(index, half) * plan.ky_block
    for s in range(slots):
        plane = field_ref[pl.ds(s, grid, stride=slots), :]
        modes = table_dot(yh, yl, dot_table(plane, zh, zl))
        spectrum = jnp.concatenate([ref[:, s, :] for ref in spectrum_refs], axis=0)
        edge = edge_refs[0][0, s : s + 1, :]
        for ref in edge_refs[1:]:
            edge = edge + ref[0, s : s + 1, :]
        other = jnp.where(row == edge_row, edge, spectrum)
        both = jnp.concatenate([spectrum, other], axis=0)
        modes = modes * jnp.concatenate([both, both], axis=1)
        field_ref[pl.ds(s, grid, stride=slots), :] = dot_table(table_dot(vh, vl, modes), wh, wl)

    def cut(group, carry):
        values = jnp.zeros((depth, grid), F32)
        for n in range(count):
            shift = lax.rem(box * n - corner_ref[2 * group, box * n] + grid, grid)
            rows = field_ref[pl.ds(start(group, n), depth), :]
            values = jnp.where(owner == n, pltpu.roll(rows, shift, 1), values)
        send_ref[group] = values.astype(send_ref.dtype)
        return carry

    lax.fori_loop(0, all_groups, cut, 0)


def terms_kernel(
    plan, recv_ref, psi_ref, wave_ref, dh_ref, dl_ref, ih_ref, il_ref, oh_ref, ol_ref, send_ref, stage_ref,
):
    box, grid, count, slots = plan.box, plan.grid, plan.per_group, plan.slots
    owner = lane_owner((1, grid), box)
    wave = jnp.concatenate(split(wave_ref[0].T), axis=1)
    for pair in range(box // 2):
        tiles = [recv_ref[o, 0, 2 * slots * pair : 2 * slots * (pair + 1), :].astype(F32) for o in range(plan.orb)]
        columns = [jnp.concatenate([t[slots * side : slots * (side + 1)] for t in tiles], axis=0) for side in range(2)]
        both = jnp.concatenate(columns, axis=1).astype(BF16)
        out = dot(wave, jnp.concatenate([both, both], axis=0))
        for side, b in enumerate((2 * pair, 2 * pair + 1)):
            mine = out[:, grid * side : grid * (side + 1)]
            potential = jnp.zeros((box, grid), F32)
            for n in range(count):
                potential = jnp.where(owner == n, mine[box * n : box * (n + 1)], potential)
            stage_ref[b] = potential * psi_ref[0, b]
    span = SUB * box
    ih, il, oh, ol = ih_ref[...], il_ref[...], oh_ref[...], ol_ref[...]
    for t in range(box // SUB):
        values = stage_ref[SUB * t : SUB * (t + 1)].reshape(span, grid)
        stage_ref[SUB * t : SUB * (t + 1)] = table_dot(ih, il, values).reshape(SUB, box, grid)
    for t in range(box // SUB):
        values = stage_ref[:, SUB * t : SUB * (t + 1), :].reshape(span, grid)
        stage_ref[:, SUB * t : SUB * (t + 1), :] = table_dot(oh, ol, values).reshape(box, SUB, grid)
    up, down = split(stage_ref[...].reshape(box * box, grid))
    dh, dl = dh_ref[...], dl_ref[...]
    last = ((1,), (1,))
    out = dot(dh, up, last) + dot(dl, up, last) + dot(dh, down, last)
    part = plan.box_part * count
    for p in range(plan.pln):
        send_ref[p, 0] = out[part * p : part * (p + 1)].astype(send_ref.dtype)


def sum_kernel(plan, recv_ref, out_ref):
    total = recv_ref[0, 0].astype(F32)
    for p in range(1, plan.pln):
        total = total + recv_ref[p, 0].astype(F32)
    section = plan.box * plan.box
    count = plan.per_group
    for j in range(plan.box_part):
        out_ref[0, :, section * j : section * (j + 1)] = total[count * j : count * (j + 1)].astype(out_ref.dtype)


def whole_spec(array):
    rank = len(array.shape)
    return pl.BlockSpec(array.shape, lambda *_: (0,) * rank)


def per_device(plan, orbitals, occupations, box_offsets, kernel_spectrum):
    orb, pln, half, slots = plan.orb, plan.pln, plan.half, plan.slots
    groups, count, box, grid = plan.groups, plan.per_group, plan.box, plan.grid
    plane_index = lax.axis_index("pln")
    where = plane_index.astype(jnp.int32)[None]
    smem = pl.BlockSpec(memory_space=pltpu.SMEM)
    params = pltpu.CompilerParams(vmem_limit_bytes=VMEM_LIMIT)
    coefs = orbitals.reshape(groups, count, orbitals.shape[1])
    area = plan.area
    tables = [*plan.depth, *plan.inner, *plan.outer]
    send, psi, wave = pl.pallas_call(
        functools.partial(density_kernel, plan),
        grid=(groups,),
        in_specs=[smem, smem, smem, pl.BlockSpec((1, count, orbitals.shape[1]), lambda g: (g, 0, 0))]
        + [whole_spec(t) for t in tables]
        + [whole_spec(plan.wave)],
        out_specs=[
            pl.BlockSpec((orb, 1, area + 2 * SUB, grid), lambda g: (0, g, 0, 0)),
            pl.BlockSpec((1, box, box, grid), lambda g: (g, 0, 0, 0)),
            pl.BlockSpec((1, plan.rows, grid), lambda g: (g, 0, 0)),
        ],
        out_shape=[
            jax.ShapeDtypeStruct((orb, groups, area + 2 * SUB, grid), BF16),
            jax.ShapeDtypeStruct((groups, box, box, grid), F32),
            jax.ShapeDtypeStruct((groups, plan.rows, grid), F32),
        ],
        scratch_shapes=[pltpu.VMEM((grid, box * box), F32)],
        compiler_params=params,
        name="density",
    )(where, box_offsets, occupations, coefs, *tables, plan.wave)
    received = lax.all_to_all(send, "orb", split_axis=0, concat_axis=0, tiled=True)
    received = received.reshape(orb * groups, area + 2 * SUB, grid)

    anywhere = pl.BlockSpec(memory_space=pl.ANY)
    by_ky = jnp.transpose(kernel_spectrum, (1, 2, 0))
    shapes = [jax.ShapeDtypeStruct((plan.ky_block, slots, grid), F32)] * half
    shapes += [jax.ShapeDtypeStruct((1, slots, grid), F32)] * half
    pieces = pl.pallas_call(
        functools.partial(spectrum_kernel, plan),
        grid=(1,),
        in_specs=[smem, anywhere, anywhere],
        out_specs=[whole_spec(shape) for shape in shapes],
        out_shape=shapes,
        scratch_shapes=[
            pltpu.VMEM((half, plan.ky_block, slots, plan.doubled), F32),
            pltpu.VMEM((half, slots, plan.doubled), F32),
            pltpu.SemaphoreType.DMA((2 * half,)),
        ],
        compiler_params=params,
        name="spectrum",
    )(where, wave, by_ky)
    pieces = list(pieces)
    for step in range(1, half):
        pairs = [(g * half + i, g * half + (i + step) % half) for g in range(2) for i in range(half)]
        pieces[step] = lax.ppermute(pieces[step], "pln", pairs)
    for step in range(half):
        pieces[half + step] = lax.ppermute(pieces[half + step], "pln", [(0, half + step), (half, step)])

    tables = [*plan.forward_z, *plan.forward_y, *plan.inverse_y, *plan.inverse_z]
    blocks = [received, *pieces, *tables]
    send = pl.pallas_call(
        functools.partial(solve_kernel, plan),
        grid=(1,),
        in_specs=[smem] + [whole_spec(t) for t in blocks],
        out_specs=pl.BlockSpec((orb * groups, area, grid), lambda g: (0, 0, 0)),
        out_shape=jax.ShapeDtypeStruct((orb * groups, area, grid), BF16),
        scratch_shapes=[
            pltpu.VMEM((grid * slots, grid), F32),
            pltpu.VMEM((2 * orb * groups, grid), jnp.int32),
            pltpu.SMEM((2 * orb * groups, grid), jnp.int32),
            pltpu.SemaphoreType.DMA,
        ],
        compiler_params=params,
        name="solve",
    )(where, *blocks)
    send = send.reshape(orb, groups, area, grid)
    received = lax.all_to_all(send, "orb", split_axis=0, concat_axis=0, tiled=True)
    tables = [*plan.depth, *plan.inner_back, *plan.outer_back]
    part = plan.box_part * count
    send = pl.pallas_call(
        functools.partial(terms_kernel, plan),
        grid=(groups,),
        in_specs=[
            pl.BlockSpec((orb, 1, area, grid), lambda g: (0, g, 0, 0)),
            pl.BlockSpec((1, box, box, grid), lambda g: (g, 0, 0, 0)),
            pl.BlockSpec((1, plan.rows, grid), lambda g: (g, 0, 0)),
        ]
        + [whole_spec(t) for t in tables],
        out_specs=pl.BlockSpec((pln, 1, part, box * box), lambda g: (0, g, 0, 0)),
        out_shape=jax.ShapeDtypeStruct((pln, groups, part, box * box), BF16),
        scratch_shapes=[pltpu.VMEM((box, box, grid), F32)],
        compiler_params=params,
        name="terms",
    )(received, psi, wave, *tables)
    received = lax.all_to_all(send, "pln", split_axis=0, concat_axis=0, tiled=True)
    cells = plan.box_part * box * box
    result = pl.pallas_call(
        functools.partial(sum_kernel, plan),
        grid=(groups,),
        in_specs=[pl.BlockSpec((pln, 1, part, box * box), lambda g: (0, g, 0, 0))],
        out_specs=pl.BlockSpec((1, count, cells), lambda g: (g, 0, 0)),
        out_shape=jax.ShapeDtypeStruct((groups, count, cells), BF16),
        compiler_params=params,
        name="sum",
    )(received)
    return result.reshape(groups * count, cells)


def solution(mesh):
    in_specs = (P("orb", None), P("orb"), P("orb", None), P(None, "pln", "orb"))
    out_specs = P("orb", "pln")

    def whole(orbitals, occupations, box_offsets, kernel_spectrum):
        plan = Plan(mesh, orbitals.shape, kernel_spectrum.shape)
        return jax.shard_map(
            functools.partial(per_device, plan), mesh=mesh, in_specs=in_specs, out_specs=out_specs, check_vma=False
        )(orbitals, occupations, box_offsets, kernel_spectrum)

    return whole
```

```python
import functools
import math

import jax
import jax.numpy as jnp
import numpy as np
from jax import lax
from jax.experimental import pallas as pl
from jax.experimental.pallas import tpu as pltpu
from jax.sharding import PartitionSpec as P

MAGIC_TAPS = (
    8.433424733352934e-07,
    -1.290557201342061e-05,
    8.76298447621056e-05,
    -0.00030158038132690465,
    0.001747237136729939,
    -0.009420470302010804,
    0.023738214637249424,
    0.0612625895831208,
    0.9940415697834004,
    -0.06048952891969835,
    -0.021030251609303816,
    0.013372634148547948,
    -0.0034412814449349387,
    0.0004944322768868992,
    -5.185986881173433e-05,
    2.7273449291197967e-06,
)
F32 = jnp.float32
BF16 = jnp.bfloat16
SUB = 8
VMEM_LIMIT = 60 * 1024 * 1024


def magic_filter(box):
    table = np.zeros((box, box))
    for row in range(box):
        for tap in range(-8, 8):
            if 0 <= row + tap < box:
                table[row, row + tap] = MAGIC_TAPS[tap + 8]
    return table.astype(np.float32).astype(np.float64)


def cas(product, doubled):
    angle = 2.0 * math.pi * (product % doubled) / doubled
    return np.cos(angle) + np.sin(angle)


def halves(table):
    high = np.asarray(table, np.float32).astype(jnp.bfloat16)
    low = (np.asarray(table, np.float64) - high.astype(np.float64)).astype(jnp.bfloat16)
    return high, low


def split(values):
    high = values.astype(BF16)
    low = (values - high.astype(F32)).astype(BF16)
    return high, low


def dot(left, right, dims=((1,), (0,))):
    return lax.dot_general(left, right, (dims, ((), ())), preferred_element_type=F32)


def terms_of(values, axis):
    high, low = split(values)
    return jnp.concatenate([high, high, low], axis=axis)


def stacked(table, axis):
    high, low = halves(table)
    return np.concatenate([high, low, high], axis=axis)


class Plan:
    def __init__(self, mesh, orbital_shape, kernel_shape):
        self.orb = mesh.shape["orb"]
        self.pln = mesh.shape["pln"]
        self.doubled = doubled = kernel_shape[0]
        self.grid = grid = doubled // 2
        self.box = box = round(orbital_shape[1] ** (1 / 3))
        self.per_group = grid // box
        self.groups = orbital_shape[0] // self.orb // self.per_group
        self.ky_block = kernel_shape[1] // self.pln
        self.kx_block = kernel_shape[2] // self.orb
        self.slots = SUB * -(-self.kx_block // (SUB * self.pln))
        self.half = self.pln // 2
        self.rows = self.orb * self.slots
        self.area = box * self.slots
        self.box_part = box // self.pln
        magic = magic_filter(box)
        eye = np.eye(SUB)
        depth = np.zeros((box, self.per_group, self.per_group, box))
        for n in range(self.per_group):
            depth[:, n, n, :] = magic.T
        depth = depth.reshape(grid, grid)
        self.depth = np.concatenate(halves(depth), axis=0)
        self.depth_back = stacked(depth, 1)
        self.inner = stacked(np.kron(eye, magic), 1)
        self.outer = stacked(np.kron(magic, eye), 1)
        self.inner_back = stacked(np.kron(eye, magic.T), 1)
        self.outer_back = stacked(np.kron(magic.T, eye), 1)
        places = np.arange(grid)
        wave = np.zeros((self.pln, self.orb, self.slots, grid))
        for p in range(self.pln):
            for s in range(self.slots):
                within = p * self.slots + s
                if within < self.kx_block:
                    k = self.kx_block * np.arange(self.orb) + within
                    wave[p, :, s, :] = cas(k[:, None] * places[None, :], doubled)
        self.wave = wave.reshape(self.pln, self.rows, grid).astype(np.float32)
        kz = np.concatenate([places, doubled - places])
        along_z = cas(places[:, None] * kz[None, :], doubled)
        along_z[:, grid] = 0.0
        self.forward_z = stacked(along_z, 0)
        self.inverse_z = stacked(along_z.T / doubled, 0)
        forward = np.zeros((self.pln, 2, grid, grid))
        weight = np.zeros((self.pln, 2, grid))
        for p in range(self.pln):
            group, index = divmod(p, self.half)
            base = grid * group
            for piece in range(self.half):
                block = (index - piece) % self.half
                for r in range(self.ky_block):
                    j = block * self.ky_block + r
                    row = piece * self.ky_block + r
                    angle = 2.0 * math.pi * ((base + j) * places % doubled) / doubled
                    forward[p, 0, row] = np.cos(angle)
                    forward[p, 1, row] = np.sin(angle)
                    weight[p, :, row] = 2.0
                    if j == 0:
                        edge = (base + grid) % doubled
                        forward[p, 1, row] = np.cos(2.0 * math.pi * (edge * places % doubled) / doubled)
                        weight[p, :, row] = 1.0
        inverse = forward * weight[..., None] / doubled**2
        self.forward_y = stacked(forward.reshape(self.pln, doubled, grid), 2)
        self.inverse_y = stacked(inverse.reshape(self.pln, doubled, grid).transpose(0, 2, 1), 2)
        self.quarter = box // 4


def lane_owner(shape, box):
    return lax.broadcasted_iota(jnp.int32, shape, len(shape) - 1) // box


def start_copies(sems, first, *pairs):
    copies = []
    for number, (source, target) in enumerate(pairs):
        copy = pltpu.make_async_copy(source, target, sems.at[first + number])
        copy.start()
        copies.append(copy)
    return copies


def wait_copies(copies):
    for copy in copies:
        copy.wait()


def density_kernel(
    plan, where_ref, corner_ref, weight_ref, coef_any, depth_any, inner_any, outer_any, wave_any,
    send_any, psi_any, wave_out_any,
    coef_ref, depth_ref, inner_ref, outer_ref, wave_ref, stage_ref, psi_ref, send_ref, sems,
):
    box, grid, count, slots = plan.box, plan.grid, plan.per_group, plan.slots
    section = box * box
    group = pl.program_id(0)
    fetched = start_copies(
        sems, 0, (coef_any.at[group], coef_ref), (depth_any, depth_ref), (inner_any, inner_ref),
        (outer_any, outer_ref), (wave_any.at[where_ref[0]], wave_ref),
    )
    wait_copies(fetched[:2])
    for p in range(box):
        stage_ref[count * p : count * (p + 1), :] = coef_ref[:, section * p : section * (p + 1)].astype(F32)
    coef = stage_ref[...].astype(BF16)
    first = dot(jnp.concatenate([coef, coef], axis=0), depth_ref[...], ((0,), (0,)))
    span = SUB * box
    wait_copies(fetched[2:])
    inner, outer = inner_ref[...], outer_ref[...]
    second = [dot(inner, terms_of(first[span * t : span * (t + 1)], 0)) for t in range(box // SUB)]
    second = jnp.concatenate(second, axis=0).reshape(box, box // SUB, SUB, grid)
    for t in range(box // SUB):
        third = dot(outer, terms_of(second[:, t].reshape(span, grid), 0))
        psi_ref[:, SUB * t : SUB * (t + 1), :] = third.reshape(box, SUB, grid)
    owner = lane_owner((1, grid), box)
    whole_wave = wave_ref[...]
    wave = jnp.zeros_like(whole_wave)
    weight = jnp.zeros((1, grid), F32)
    kind = lax.broadcasted_iota(jnp.int32, (2 * SUB, 1), 0)
    corner = jnp.zeros((2 * SUB, grid), F32)
    for n in range(count):
        number = group * count + n
        shift = lax.rem(box * n - corner_ref[number, 2] + grid, grid)
        wave = jnp.where(owner == n, pltpu.roll(whole_wave, shift, 1), wave)
        weight = jnp.where(owner == n, weight_ref[number], weight)
        place = jnp.where(kind == 0, corner_ref[number, 0], corner_ref[number, 1])
        corner = jnp.where(owner == n, place.astype(F32), corner)
    wave_ref[...] = wave
    for o in range(plan.orb):
        send_ref[o, plan.area :, :] = corner.astype(send_ref.dtype)
    high, low = split(wave)
    wave_terms = jnp.concatenate([high, low, high], axis=1)
    rows = pl.ds(plan.area, 2 * SUB)
    sent = start_copies(
        sems, 5, (psi_ref, psi_any.at[group]), (wave_ref, wave_out_any.at[group]),
        (send_ref.at[:, rows, :], send_any.at[:, group, rows, :]),
    )
    per_part = plan.quarter // 2
    for pair in range(box // 2):
        columns = []
        for b in (2 * pair, 2 * pair + 1):
            psi = psi_ref[b]
            density = psi * psi * weight
            columns.append(jnp.concatenate([jnp.where(owner == n, density, 0.0) for n in range(count)], axis=0))
        out = dot(wave_terms, terms_of(jnp.concatenate(columns, axis=1), 0))
        for o in range(plan.orb):
            mine = out[slots * o : slots * (o + 1)]
            tile = jnp.concatenate([mine[:, :grid], mine[:, grid:]], axis=0)
            send_ref[o, 2 * slots * pair : 2 * slots * (pair + 1), :] = tile.astype(send_ref.dtype)
        if pair % per_part == per_part - 1:
            part = pair // per_part
            rows = pl.ds(plan.quarter * slots * part, plan.quarter * slots)
            sent += start_copies(sems, 8 + part, (send_ref.at[:, rows, :], send_any.at[:, group, rows, :]))
    wait_copies(sent)


def spectrum_kernel(plan, where_ref, after_ref, spectrum_ref, *refs):
    half, slots, grid, rows = plan.half, plan.slots, plan.grid, plan.ky_block
    outs = refs[: 2 * half]
    block_ref, edge_ref, sems = refs[2 * half :]
    me = where_ref[0]
    group, index = me // half, lax.rem(me, half)
    copies = []

    def fetch(target, source, buffer, number):
        first = jnp.minimum(target * slots, max(plan.kx_block - slots, 0))
        first = pl.multiple_of(first, SUB)
        copy = pltpu.make_async_copy(source.at[:, pl.ds(first, slots), :], buffer, sems.at[number])
        copy.start()
        copies.append(copy)

    for step in range(half):
        fetch(group * half + lax.rem(index + step, half), spectrum_ref, block_ref.at[step], step)
    for step in range(half):
        fetch((1 - group) * half + step, spectrum_ref.at[pl.ds(0, 1)], edge_ref.at[pl.ds(step, 1)], half + step)
    odd = lax.rem(lax.broadcasted_iota(jnp.int32, (1, 1, grid), 2), 2) == 1

    def fold(values):
        last = values[:, :, grid : grid + 1]
        return values[:, :, :grid] + jnp.where(odd, last, -last)

    for step in range(half):
        copies[half + step].wait()
        outs[half + step][...] = fold(edge_ref[pl.ds(step, 1)])
    for step in list(range(1, half)) + [0]:
        copies[step].wait()
        outs[step][...] = fold(block_ref[step])


def solve_kernel(plan, where_ref, recv_any, *refs):
    half, slots, grid, box, count = plan.half, plan.slots, plan.grid, plan.box, plan.per_group
    piece_anys = refs[: 2 * half]
    forward_z_any, forward_y_any, inverse_y_any, inverse_z_any, send_any = refs[2 * half : 2 * half + 5]
    (
        recv_ref, spectrum_ref, edge_ref, forward_z_ref, forward_y_ref, inverse_y_ref, inverse_z_ref,
        field_ref, result_ref, send_ref, table_ref, corner_ref, corner_sem, recv_sems, sems, send_sems,
    ) = refs[2 * half + 5 :]
    index = where_ref[0]
    depth = plan.area
    all_groups = plan.orb * plan.groups
    owner = lane_owner((1, grid), box)
    rows = pl.ds(depth, 2 * SUB)
    first = start_copies(sems, 0, (recv_any.at[:, rows, :], recv_ref.at[:, rows, :]))

    def data_copy(group):
        rows = pl.ds(0, depth)
        return pltpu.make_async_copy(recv_any.at[group, rows, :], recv_ref.at[group, rows, :], recv_sems.at[group])

    def fetch(group, carry):
        data_copy(group).start()
        return carry

    lax.fori_loop(0, all_groups, fetch, 0)
    pairs = [(forward_z_any, forward_z_ref), (forward_y_any.at[index], forward_y_ref)]
    pairs += [(inverse_y_any.at[index], inverse_y_ref), (inverse_z_any, inverse_z_ref)]
    pairs += [(piece_anys[step], spectrum_ref.at[step]) for step in range(half)]
    pairs += [(piece_anys[half + step], edge_ref.at[pl.ds(step, 1)]) for step in range(half)]
    later = start_copies(sems, 1, *pairs)
    field_ref[...] = jnp.zeros_like(field_ref)
    wait_copies(first)
    for group in range(all_groups):
        tile = recv_ref[group, depth : depth + 2 * SUB, :].astype(F32).astype(jnp.int32)
        table_ref[2 * group : 2 * group + 2, :] = tile[:2]
    copy = pltpu.make_async_copy(table_ref, corner_ref, corner_sem)
    copy.start()
    copy.wait()

    def start(group, n):
        return pl.multiple_of(corner_ref[2 * group + 1, box * n] * slots, SUB)

    def place(group, carry):
        data_copy(group).wait()
        values = recv_ref[group, :depth, :].astype(F32)
        for n in range(count):
            shift = lax.rem(corner_ref[2 * group, box * n] - box * n + grid, grid)
            moved = pltpu.roll(jnp.where(owner == n, values, 0.0), shift, 1)
            field_ref[pl.ds(start(group, n), depth), :] += moved
        return carry

    lax.fori_loop(0, all_groups, place, 0)
    wait_copies(later)
    forward_z, forward_y = forward_z_ref[...], forward_y_ref[...]
    inverse_y, inverse_z = inverse_y_ref[...], inverse_z_ref[...]
    row = lax.broadcasted_iota(jnp.int32, (grid, 1), 0)
    edge_row = lax.rem(index, half) * plan.ky_block
    edges = edge_ref[0]
    for step in range(1, half):
        edges = edges + edge_ref[step]
    for s in range(slots):
        plane = field_ref[pl.ds(s, grid, stride=slots), :]
        modes = dot(forward_y, terms_of(dot(terms_of(plane, 1), forward_z), 0))
        spectrum = jnp.concatenate([spectrum_ref[step, :, s, :] for step in range(half)], axis=0)
        other = jnp.where(row == edge_row, edges[s : s + 1], spectrum)
        both = jnp.concatenate([spectrum, other], axis=0)
        modes = modes * jnp.concatenate([both, both], axis=1)
        plane = dot(terms_of(dot(inverse_y, terms_of(modes, 0)), 1), inverse_z)
        result_ref[pl.ds(s, grid, stride=slots), :] = plane

    def send_copy(group):
        return pltpu.make_async_copy(send_ref.at[group], send_any.at[group], send_sems.at[group])

    def cut(group, carry):
        values = jnp.zeros((depth, grid), F32)
        for n in range(count):
            shift = lax.rem(box * n - corner_ref[2 * group, box * n] + grid, grid)
            rows = result_ref[pl.ds(start(group, n), depth), :]
            values = jnp.where(owner == n, pltpu.roll(rows, shift, 1), values)
        send_ref[group] = values.astype(send_ref.dtype)
        send_copy(group).start()
        return carry

    lax.fori_loop(0, all_groups, cut, 0)

    def finish(group, carry):
        send_copy(group).wait()
        return carry

    lax.fori_loop(0, all_groups, finish, 0)


def terms_kernel(plan, where_ref, recv_any, psi_any, wave_any, depth_any, inner_any, outer_any, *refs):
    box, grid, count, slots, pln = plan.box, plan.grid, plan.per_group, plan.slots, plan.pln
    out_anys = refs[:pln]
    recv_ref, psi_ref, wave_ref, depth_ref, inner_ref, outer_ref, stage_ref, own_ref, send_ref, sems = refs[pln:]
    group = pl.program_id(0)
    fetched = start_copies(sems, 0, (wave_any.at[group], wave_ref))
    quarter = plan.quarter
    for part in range(4):
        rows = pl.ds(quarter * slots * part, quarter * slots)
        boxes = pl.ds(quarter * part, quarter)
        fetched += start_copies(
            sems, 1 + 2 * part, (recv_any.at[:, group, rows, :], recv_ref.at[:, rows, :]),
            (psi_any.at[group, boxes], psi_ref.at[boxes]),
        )
    tables = start_copies(sems, 9, (inner_any, inner_ref), (outer_any, outer_ref), (depth_any, depth_ref))
    owner = lane_owner((1, grid), box)
    wait_copies(fetched[:1])
    wave = jnp.concatenate(split(wave_ref[...].T), axis=1)
    for pair in range(box // 2):
        if pair % (quarter // 2) == 0:
            part = pair // (quarter // 2)
            wait_copies(fetched[1 + 2 * part : 3 + 2 * part])
        tiles = [recv_ref[o, 2 * slots * pair : 2 * slots * (pair + 1), :].astype(F32) for o in range(plan.orb)]
        columns = [jnp.concatenate([t[slots * side : slots * (side + 1)] for t in tiles], axis=0) for side in range(2)]
        both = jnp.concatenate(columns, axis=1).astype(BF16)
        out = dot(wave, jnp.concatenate([both, both], axis=0))
        for side, b in enumerate((2 * pair, 2 * pair + 1)):
            mine = out[:, grid * side : grid * (side + 1)]
            potential = jnp.zeros((box, grid), F32)
            for n in range(count):
                potential = jnp.where(owner == n, mine[box * n : box * (n + 1)], potential)
            stage_ref[b] = potential * psi_ref[b]
    span = SUB * box
    wait_copies(tables)
    inner, outer = inner_ref[...], outer_ref[...]
    second = []
    for t in range(box // SUB):
        values = stage_ref[SUB * t : SUB * (t + 1)].reshape(span, grid)
        second.append(dot(inner, terms_of(values, 0)))
    second = jnp.concatenate(second, axis=0).reshape(box, box // SUB, SUB, grid)
    for t in range(box // SUB):
        values = dot(outer, terms_of(second[:, t].reshape(span, grid), 0))
        stage_ref[:, SUB * t : SUB * (t + 1), :] = values.reshape(box, SUB, grid)
    values = terms_of(stage_ref[...].reshape(box * box, grid), 1)
    out = dot(depth_ref[...], values, ((1,), (1,)))
    part = plan.box_part * count
    for p in range(pln):
        own_ref[p] = out[part * p : part * (p + 1)]
        send_ref[p] = own_ref[p].astype(send_ref.dtype)
    me = where_ref[0]
    pairs = [(own_ref.at[me], out_anys[0].at[group])]
    pairs += [(send_ref.at[lax.rem(me + step, pln)], out_anys[step].at[group]) for step in range(1, pln)]
    wait_copies(start_copies(sems, 12, *pairs))


def sum_kernel(plan, *refs):
    out_ref = refs[plan.pln]
    total = refs[0][0]
    for ref in refs[1 : plan.pln]:
        total = total + ref[0].astype(F32)
    section = plan.box * plan.box
    count = plan.per_group
    for j in range(plan.box_part):
        out_ref[0, :, section * j : section * (j + 1)] = total[count * j : count * (j + 1)].astype(out_ref.dtype)


def whole_spec(array):
    rank = len(array.shape)
    return pl.BlockSpec(array.shape, lambda *_: (0,) * rank)


def per_device(plan, orbitals, occupations, box_offsets, kernel_spectrum):
    orb, pln, half, slots = plan.orb, plan.pln, plan.half, plan.slots
    groups, count, box, grid = plan.groups, plan.per_group, plan.box, plan.grid
    plane_index = lax.axis_index("pln")
    where = plane_index.astype(jnp.int32)[None]
    smem = pl.BlockSpec(memory_space=pltpu.SMEM)
    params = pltpu.CompilerParams(vmem_limit_bytes=VMEM_LIMIT)
    coefs = orbitals.reshape(groups, count, orbitals.shape[1])
    area = plan.area
    anywhere = pl.BlockSpec(memory_space=pl.ANY)
    dma = pltpu.SemaphoreType.DMA

    def buffer(array, dtype=None):
        return pltpu.VMEM(array.shape, dtype or array.dtype)

    tables = [plan.depth, plan.inner, plan.outer]
    send, psi, wave = pl.pallas_call(
        functools.partial(density_kernel, plan),
        grid=(groups,),
        in_specs=[smem, smem, smem] + [anywhere] * 5,
        out_specs=[anywhere] * 3,
        out_shape=[
            jax.ShapeDtypeStruct((orb, groups, area + 2 * SUB, grid), BF16),
            jax.ShapeDtypeStruct((groups, box, box, grid), F32),
            jax.ShapeDtypeStruct((groups, plan.rows, grid), F32),
        ],
        scratch_shapes=[
            pltpu.VMEM((count, orbitals.shape[1]), BF16),
            *[buffer(t) for t in tables],
            pltpu.VMEM((plan.rows, grid), F32),
            pltpu.VMEM((grid, box * box), F32),
            pltpu.VMEM((box, box, grid), F32),
            pltpu.VMEM((orb, area + 2 * SUB, grid), BF16),
            dma((12,)),
        ],
        compiler_params=params,
        name="density",
    )(where, box_offsets, occupations, coefs, *tables, plan.wave)
    received = lax.all_to_all(send, "orb", split_axis=0, concat_axis=0, tiled=True)
    received = received.reshape(orb * groups, area + 2 * SUB, grid)

    by_ky = jnp.transpose(kernel_spectrum, (1, 2, 0))
    shapes = [jax.ShapeDtypeStruct((plan.ky_block, slots, grid), F32)] * half
    shapes += [jax.ShapeDtypeStruct((1, slots, grid), F32)] * half
    pieces = pl.pallas_call(
        functools.partial(spectrum_kernel, plan),
        grid=(1,),
        in_specs=[smem, anywhere, anywhere],
        out_specs=[whole_spec(shape) for shape in shapes],
        out_shape=shapes,
        scratch_shapes=[
            pltpu.VMEM((half, plan.ky_block, slots, plan.doubled), F32),
            pltpu.VMEM((half, slots, plan.doubled), F32),
            pltpu.SemaphoreType.DMA((2 * half,)),
        ],
        compiler_params=params,
        name="spectrum",
    )(where, wave, by_ky)
    pieces = list(pieces)
    for step in range(1, half):
        pairs = [(g * half + i, g * half + (i + step) % half) for g in range(2) for i in range(half)]
        pieces[step] = lax.ppermute(pieces[step], "pln", pairs)
    for step in range(half):
        pieces[half + step] = lax.ppermute(pieces[half + step], "pln", [(0, half + step), (half, step)])

    tables = [plan.forward_z, plan.forward_y, plan.inverse_y, plan.inverse_z]
    blocks = [received, *pieces, *tables]
    send = pl.pallas_call(
        functools.partial(solve_kernel, plan),
        in_specs=[smem] + [anywhere] * len(blocks),
        out_specs=anywhere,
        out_shape=jax.ShapeDtypeStruct((orb * groups, area, grid), BF16),
        scratch_shapes=[
            buffer(received),
            pltpu.VMEM((half, plan.ky_block, slots, grid), F32),
            pltpu.VMEM((half, slots, grid), F32),
            buffer(plan.forward_z),
            buffer(plan.forward_y[0]),
            buffer(plan.inverse_y[0]),
            buffer(plan.inverse_z),
            pltpu.VMEM((grid * slots, grid), F32),
            pltpu.VMEM((grid * slots, grid), F32),
            pltpu.VMEM((orb * groups, area, grid), BF16),
            pltpu.VMEM((2 * orb * groups, grid), jnp.int32),
            pltpu.SMEM((2 * orb * groups, grid), jnp.int32),
            dma,
            dma((orb * groups,)),
            dma((5 + 2 * half,)),
            dma((orb * groups,)),
        ],
        compiler_params=params,
        name="solve",
    )(where, *blocks)
    send = send.reshape(orb, groups, area, grid)
    received = lax.all_to_all(send, "orb", split_axis=0, concat_axis=0, tiled=True)
    tables = [plan.depth_back, plan.inner_back, plan.outer_back]
    part = plan.box_part * count
    finished = pl.pallas_call(
        functools.partial(terms_kernel, plan),
        grid=(groups,),
        in_specs=[smem] + [anywhere] * 6,
        out_specs=[anywhere] * pln,
        out_shape=[jax.ShapeDtypeStruct((groups, part, box * box), BF16 if step else F32) for step in range(pln)],
        scratch_shapes=[
            pltpu.VMEM((orb, area, grid), BF16),
            pltpu.VMEM((box, box, grid), F32),
            pltpu.VMEM((plan.rows, grid), F32),
            *[buffer(t) for t in tables],
            pltpu.VMEM((box, box, grid), F32),
            pltpu.VMEM((pln, part, box * box), F32),
            pltpu.VMEM((pln, part, box * box), BF16),
            dma((12 + pln,)),
        ],
        compiler_params=params,
        name="terms",
    )(where, received, psi, wave, *tables)
    finished = list(finished)
    for step in range(1, pln):
        finished[step] = lax.ppermute(finished[step], "pln", [(p, (p + step) % pln) for p in range(pln)])
    cells = plan.box_part * box * box
    result = pl.pallas_call(
        functools.partial(sum_kernel, plan),
        grid=(groups,),
        in_specs=[pl.BlockSpec((1, part, box * box), lambda g: (g, 0, 0))] * pln,
        out_specs=pl.BlockSpec((1, count, cells), lambda g: (g, 0, 0)),
        out_shape=jax.ShapeDtypeStruct((groups, count, cells), BF16),
        compiler_params=params,
        name="sum",
    )(*finished)
    return result.reshape(groups * count, cells)


def solution(mesh):
    in_specs = (P("orb", None), P("orb"), P("orb", None), P(None, "pln", "orb"))
    out_specs = P("orb", "pln")

    def whole(orbitals, occupations, box_offsets, kernel_spectrum):
        plan = Plan(mesh, orbitals.shape, kernel_spectrum.shape)
        return jax.shard_map(
            functools.partial(per_device, plan), mesh=mesh, in_specs=in_specs, out_specs=out_specs, check_vma=False
        )(orbitals, occupations, box_offsets, kernel_spectrum)

    return whole
```

```python
import functools
import math

import jax
import jax.numpy as jnp
import numpy as np
from jax import lax
from jax.experimental import pallas as pl
from jax.experimental.pallas import tpu as pltpu
from jax.sharding import PartitionSpec as P

MAGIC_TAPS = (
    8.433424733352934e-07,
    -1.290557201342061e-05,
    8.76298447621056e-05,
    -0.00030158038132690465,
    0.001747237136729939,
    -0.009420470302010804,
    0.023738214637249424,
    0.0612625895831208,
    0.9940415697834004,
    -0.06048952891969835,
    -0.021030251609303816,
    0.013372634148547948,
    -0.0034412814449349387,
    0.0004944322768868992,
    -5.185986881173433e-05,
    2.7273449291197967e-06,
)
F32 = jnp.float32
BF16 = jnp.bfloat16
SUB = 8
LARGE = 60 * 1024 * 1024
SMALL = 32 * 1024 * 1024


def magic_filter(box):
    table = np.zeros((box, box))
    for row in range(box):
        for tap in range(-8, 8):
            if 0 <= row + tap < box:
                table[row, row + tap] = MAGIC_TAPS[tap + 8]
    return table.astype(np.float32).astype(np.float64)


def cas(product, doubled):
    angle = 2.0 * math.pi * (product % doubled) / doubled
    return np.cos(angle) + np.sin(angle)


def halves(table):
    high = np.asarray(table, np.float32).astype(jnp.bfloat16)
    low = (np.asarray(table, np.float64) - high.astype(np.float64)).astype(jnp.bfloat16)
    return high, low


def split(values):
    high = values.astype(BF16)
    low = (values - high.astype(F32)).astype(BF16)
    return high, low


def dot(left, right, dims=((1,), (0,))):
    return lax.dot_general(left, right, (dims, ((), ())), preferred_element_type=F32)


def terms_of(values, axis):
    high, low = split(values)
    return jnp.concatenate([high, high, low], axis=axis)


def stacked(table, axis):
    high, low = halves(table)
    return np.concatenate([high, low, high], axis=axis)


SINE = (1.0, -1.0 / 6, 1.0 / 120, -1.0 / 5040, 1.0 / 362880)
COSINE = (1.0, -1.0 / 2, 1.0 / 24, -1.0 / 720, 1.0 / 40320)


def turn(steps, doubled):
    quarter = doubled // 4
    place = (steps + quarter // 2) & (doubled - 1)
    quadrant = place // quarter
    angle = (place - quadrant * quarter - quarter // 2).astype(F32) * (2.0 * math.pi / doubled)
    square = angle * angle
    cosine, sine = COSINE[-1], SINE[-1]
    for even, odd in zip(COSINE[-2::-1], SINE[-2::-1]):
        cosine, sine = cosine * square + even, sine * square + odd
    return quadrant, cosine, sine * angle


def cosine_table(steps, doubled):
    quadrant, cosine, sine = turn(steps, doubled)
    value = jnp.where((quadrant & 1) == 0, cosine, -sine)
    return jnp.where(quadrant < 2, value, -value)


def cas_table(steps, doubled):
    quadrant, cosine, sine = turn(steps, doubled)
    value = jnp.where((quadrant & 1) == 0, cosine + sine, cosine - sine)
    return jnp.where(quadrant < 2, value, -value)


def iota(shape, axis):
    return lax.broadcasted_iota(jnp.int32, shape, axis)


def stack_terms(table, axis):
    high, low = split(table)
    return jnp.concatenate([high, low, high], axis=axis)


def tap_table(step):
    value = jnp.zeros(step.shape, F32)
    for tap in range(-8, 8):
        value = jnp.where(step == tap, np.float32(MAGIC_TAPS[tap + 8]), value)
    return value


def inner_back_table(box):
    span = SUB * box
    one = tap_table(iota((box, span), 0) - (iota((box, span), 1) & (box - 1)))
    whole = jnp.concatenate([one] * SUB, axis=0)
    return jnp.where(iota((span, span), 0) // box == iota((span, span), 1) // box, whole, 0.0)


def outer_back_table(box):
    span = SUB * box
    row, column = iota((span, span), 0), iota((span, span), 1)
    value = tap_table(row // SUB - column // SUB)
    return jnp.where((row & (SUB - 1)) == (column & (SUB - 1)), value, 0.0)


def depth_back_table(plan):
    grid, box, count = plan.grid, plan.box, plan.per_group
    row, column = iota((grid, grid), 0), iota((grid, grid), 1)
    value = tap_table(row // count - (column & (box - 1)))
    return jnp.where((row & (count - 1)) == column // box, value, 0.0)


def mode_table(plan, me, shape, axis):
    grid, doubled, half = plan.grid, plan.doubled, plan.half
    line = tuple(doubled if dim == axis else 1 for dim in range(2))
    group, index = me // half, lax.rem(me, half)
    mode = iota(line, axis)
    within = mode & (grid - 1)
    block = (index - within // plan.ky_block + half) & (half - 1)
    step = block * plan.ky_block + (within & (plan.ky_block - 1))
    edge = (mode >= grid) & (step == 0)
    frequency = jnp.where(edge, ((1 - group) * grid), group * grid + step)
    quarter = jnp.where((mode >= grid) & (step != 0), doubled // 4, 0)
    weight = jnp.where(step == 0, 1.0, 2.0)
    return cosine_table(frequency * iota(shape, 1 - axis) - quarter, doubled), weight


def depth_mode_table(plan, shape, axis):
    grid, doubled = plan.grid, plan.doubled
    place = iota(shape, axis)
    frequency = jnp.where(place < grid, place, grid - place)
    return jnp.where(place == grid, 0.0, cas_table(frequency * iota(shape, 1 - axis), doubled))


class Plan:
    def __init__(self, mesh, orbital_shape, kernel_shape):
        self.orb = mesh.shape["orb"]
        self.pln = mesh.shape["pln"]
        self.doubled = doubled = kernel_shape[0]
        self.grid = grid = doubled // 2
        self.box = box = round(orbital_shape[1] ** (1 / 3))
        self.per_group = grid // box
        self.groups = orbital_shape[0] // self.orb // self.per_group
        self.ky_block = kernel_shape[1] // self.pln
        self.kx_block = kernel_shape[2] // self.orb
        self.slots = SUB * -(-self.kx_block // (SUB * self.pln))
        self.half = self.pln // 2
        self.rows = self.orb * self.slots
        self.area = box * self.slots
        self.box_part = box // self.pln
        magic = magic_filter(box)
        eye = np.eye(SUB)
        depth = np.zeros((box, self.per_group, self.per_group, box))
        for n in range(self.per_group):
            depth[:, n, n, :] = magic.T
        depth = depth.reshape(grid, grid)
        self.depth = np.concatenate(halves(depth), axis=0)
        self.inner = stacked(np.kron(eye, magic), 1)
        self.outer = stacked(np.kron(magic, eye), 1)
        places = np.arange(grid)
        wave = np.zeros((self.pln, self.orb, self.slots, grid))
        for p in range(self.pln):
            for s in range(self.slots):
                within = p * self.slots + s
                if within < self.kx_block:
                    k = self.kx_block * np.arange(self.orb) + within
                    wave[p, :, s, :] = cas(k[:, None] * places[None, :], doubled)
        self.wave = wave.reshape(self.pln, self.rows, grid).astype(np.float32)
        self.quarter = box // 4


def lane_owner(shape, box):
    return lax.broadcasted_iota(jnp.int32, shape, len(shape) - 1) // box


def start_copies(sems, first, *pairs):
    copies = []
    for number, (source, target) in enumerate(pairs):
        copy = pltpu.make_async_copy(source, target, sems.at[first + number])
        copy.start()
        copies.append(copy)
    return copies


def wait_copies(copies):
    for copy in copies:
        copy.wait()


def density_kernel(
    plan, where_ref, corner_ref, weight_ref, coef_any, depth_any, inner_any, outer_any, wave_any, spectrum_any,
    send_any, psi_any, wave_out_any, *refs,
):
    piece_anys = refs[: 2 * plan.half]
    coef_ref, depth_ref, inner_ref, outer_ref, wave_ref, stage_ref, psi_ref, send_ref, *spectrum_refs, sems = refs[2 * plan.half :]
    box, grid, count, slots = plan.box, plan.grid, plan.per_group, plan.slots
    section = box * box
    group = pl.program_id(0)
    fetched = start_copies(
        sems, 0, (coef_any.at[group], coef_ref), (depth_any, depth_ref), (inner_any, inner_ref),
        (outer_any, outer_ref), (wave_any.at[where_ref[0]], wave_ref),
    )

    @pl.when(group == 0)
    def _():
        start_spectrum(plan, where_ref[0], spectrum_any, *spectrum_refs)

    wait_copies(fetched[:2])
    for p in range(box):
        stage_ref[count * p : count * (p + 1), :] = coef_ref[:, section * p : section * (p + 1)].astype(F32)
    coef = stage_ref[...].astype(BF16)
    first = dot(jnp.concatenate([coef, coef], axis=0), depth_ref[...], ((0,), (0,)))
    span = SUB * box
    wait_copies(fetched[2:])
    inner, outer = inner_ref[...], outer_ref[...]
    second = [dot(inner, terms_of(first[span * t : span * (t + 1)], 0)) for t in range(box // SUB)]
    second = jnp.concatenate(second, axis=0).reshape(box, box // SUB, SUB, grid)
    for t in range(box // SUB):
        third = dot(outer, terms_of(second[:, t].reshape(span, grid), 0))
        psi_ref[:, SUB * t : SUB * (t + 1), :] = third.reshape(box, SUB, grid)
    owner = lane_owner((1, grid), box)
    whole_wave = wave_ref[...]
    wave = jnp.zeros_like(whole_wave)
    weight = jnp.zeros((1, grid), F32)
    kind = lax.broadcasted_iota(jnp.int32, (2 * SUB, 1), 0)
    corner = jnp.zeros((2 * SUB, grid), F32)
    for n in range(count):
        number = group * count + n
        shift = lax.rem(box * n - corner_ref[number, 2] + grid, grid)
        wave = jnp.where(owner == n, pltpu.roll(whole_wave, shift, 1), wave)
        weight = jnp.where(owner == n, weight_ref[number], weight)
        place = jnp.where(kind == 0, corner_ref[number, 0], corner_ref[number, 1])
        corner = jnp.where(owner == n, place.astype(F32), corner)
    wave_ref[...] = wave
    for o in range(plan.orb):
        send_ref[o, plan.area :, :] = corner.astype(send_ref.dtype)
    high, low = split(wave)
    wave_terms = jnp.concatenate([high, low, high], axis=1)
    rows = pl.ds(plan.area, 2 * SUB)
    sent = start_copies(
        sems, 5, (psi_ref, psi_any.at[group]), (wave_ref, wave_out_any.at[group]),
        (send_ref.at[:, rows, :], send_any.at[:, group, rows, :]),
    )
    per_part = plan.quarter // 2
    for pair in range(box // 2):
        columns = []
        for b in (2 * pair, 2 * pair + 1):
            psi = psi_ref[b]
            density = psi * psi * weight
            columns.append(jnp.concatenate([jnp.where(owner == n, density, 0.0) for n in range(count)], axis=0))
        out = dot(wave_terms, terms_of(jnp.concatenate(columns, axis=1), 0))
        for o in range(plan.orb):
            mine = out[slots * o : slots * (o + 1)]
            tile = jnp.concatenate([mine[:, :grid], mine[:, grid:]], axis=0)
            send_ref[o, 2 * slots * pair : 2 * slots * (pair + 1), :] = tile.astype(send_ref.dtype)
        if pair % per_part == per_part - 1:
            part = pair // per_part
            rows = pl.ds(plan.quarter * slots * part, plan.quarter * slots)
            sent += start_copies(sems, 8 + part, (send_ref.at[:, rows, :], send_any.at[:, group, rows, :]))

    @pl.when(group == 0)
    def _():
        finish_spectrum(plan, where_ref[0], spectrum_any, piece_anys, *spectrum_refs)

    wait_copies(sent)


def spectrum_copies(plan, me, spectrum_any, block_ref, edge_ref, sems):
    half, slots = plan.half, plan.slots
    group, index = me // half, lax.rem(me, half)

    def fetch(target, source, buffer, number):
        first = jnp.minimum(target * slots, max(plan.kx_block - slots, 0))
        first = pl.multiple_of(first, SUB)
        return pltpu.make_async_copy(source.at[:, pl.ds(first, slots), :], buffer, sems.at[number])

    copies = []
    for step in range(half):
        copies.append(fetch(group * half + lax.rem(index + step, half), spectrum_any, block_ref.at[step], step))
    for step in range(half):
        target = (1 - group) * half + step
        copies.append(fetch(target, spectrum_any.at[pl.ds(0, 1)], edge_ref.at[pl.ds(step, 1)], half + step))
    return copies


def start_spectrum(plan, me, spectrum_any, block_ref, edge_ref, block_out_ref, edge_out_ref, sems, out_sems):
    for copy in spectrum_copies(plan, me, spectrum_any, block_ref, edge_ref, sems):
        copy.start()


def finish_spectrum(plan, me, spectrum_any, piece_anys, block_ref, edge_ref, block_out_ref, edge_out_ref, sems, out_sems):
    half, grid = plan.half, plan.grid
    wait_copies(spectrum_copies(plan, me, spectrum_any, block_ref, edge_ref, sems))
    odd = (iota((1, 1, grid), 2) & 1) == 1

    def fold(values):
        last = values[..., grid : grid + 1]
        return values[..., :grid] + jnp.where(odd, last, -last)

    edge_out_ref[...] = fold(edge_ref[...])
    pairs = []
    for step in range(half):
        block_out_ref[step] = fold(block_ref[step])
        pairs.append((block_out_ref.at[step], piece_anys[step]))
    pairs += [(edge_out_ref.at[pl.ds(step, 1)], piece_anys[half + step]) for step in range(half)]
    wait_copies(start_copies(out_sems, 0, *pairs))


def solve_kernel(plan, where_ref, recv_ref, *refs):
    half, slots, grid, box, count = plan.half, plan.slots, plan.grid, plan.box, plan.per_group
    doubled = plan.doubled
    piece_refs, edge_refs = refs[:half], refs[half : 2 * half]
    send_ref, field_ref, result_ref, table_ref, corner_ref, sem = refs[2 * half :]
    me = where_ref[0]
    depth = plan.area
    all_groups = plan.orb * plan.groups
    owner = lane_owner((1, grid), box)
    for group in range(all_groups):
        tile = recv_ref[group, depth : depth + 2 * SUB, :].astype(F32).astype(jnp.int32)
        table_ref[2 * group : 2 * group + 2, :] = tile[:2]
    copy = pltpu.make_async_copy(table_ref, corner_ref, sem)
    copy.start()
    field_ref[...] = jnp.zeros_like(field_ref)
    forward, _ = mode_table(plan, me, (doubled, grid), 0)
    forward_y = stack_terms(forward, 1)
    inverse, weight = mode_table(plan, me, (grid, doubled), 1)
    inverse_y = stack_terms(inverse * (weight * (1.0 / doubled**3)), 1)
    forward_z = stack_terms(depth_mode_table(plan, (grid, doubled), 1), 0)
    inverse_z = stack_terms(depth_mode_table(plan, (doubled, grid), 0), 0)
    copy.wait()

    def start(group, n):
        return pl.multiple_of(corner_ref[2 * group + 1, box * n] * slots, SUB)

    def place(group, carry):
        values = recv_ref[group, :depth, :].astype(F32)
        for n in range(count):
            shift = lax.rem(corner_ref[2 * group, box * n] - box * n + grid, grid)
            moved = pltpu.roll(jnp.where(owner == n, values, 0.0), shift, 1)
            field_ref[pl.ds(start(group, n), depth), :] += moved
        return carry

    lax.fori_loop(0, all_groups, place, 0)
    row = iota((grid, 1), 0)
    edge_row = lax.rem(me, half) * plan.ky_block
    edges = edge_refs[0][0]
    for ref in edge_refs[1:]:
        edges = edges + ref[0]
    for pair in range(slots // 2):
        both = (2 * pair, 2 * pair + 1)
        planes = jnp.concatenate([field_ref[pl.ds(s, grid, stride=slots), :] for s in both], axis=1)
        modes = dot(forward_y, terms_of(planes, 0))
        back = []
        for side, s in enumerate(both):
            spectrum = jnp.concatenate([ref[pl.ds(s, plan.ky_block, stride=slots), :] for ref in piece_refs], axis=0)
            other = jnp.where(row == edge_row, edges[s : s + 1], spectrum)
            spectrum = jnp.concatenate([spectrum, other], axis=0)
            mine = dot(terms_of(modes[:, grid * side : grid * (side + 1)], 1), forward_z)
            mine = mine * jnp.concatenate([spectrum, spectrum], axis=1)
            back.append(dot(terms_of(mine, 1), inverse_z))
        planes = dot(inverse_y, terms_of(jnp.concatenate(back, axis=1), 0))
        for side, s in enumerate(both):
            result_ref[pl.ds(s, grid, stride=slots), :] = planes[:, grid * side : grid * (side + 1)]

    def cut(group, carry):
        values = jnp.zeros((depth, grid), F32)
        for n in range(count):
            shift = lax.rem(box * n - corner_ref[2 * group, box * n] + grid, grid)
            rows = result_ref[pl.ds(start(group, n), depth), :]
            values = jnp.where(owner == n, pltpu.roll(rows, shift, 1), values)
        send_ref[group] = values.astype(send_ref.dtype)
        return carry

    lax.fori_loop(0, all_groups, cut, 0)


def terms_kernel(plan, where_ref, recv_ref, psi_any, wave_ref, *refs):
    box, grid, count, slots, pln = plan.box, plan.grid, plan.per_group, plan.slots, plan.pln
    out_refs = refs[:pln]
    psi_ref, stage_ref, own_ref, sem = refs[pln:]
    group = pl.program_id(0)
    copy = pltpu.make_async_copy(psi_any.at[group], psi_ref, sem)
    copy.start()
    owner = lane_owner((1, grid), box)
    wave = jnp.concatenate(split(wave_ref[0].T), axis=1)
    inner = stack_terms(inner_back_table(box), 1)
    outer = stack_terms(outer_back_table(box), 1)
    back = stack_terms(depth_back_table(plan), 1)
    copy.wait()
    for pair in range(box // 2):
        tiles = [recv_ref[o, 0, 2 * slots * pair : 2 * slots * (pair + 1), :].astype(F32) for o in range(plan.orb)]
        columns = [jnp.concatenate([t[slots * side : slots * (side + 1)] for t in tiles], axis=0) for side in range(2)]
        both = jnp.concatenate(columns, axis=1).astype(BF16)
        out = dot(wave, jnp.concatenate([both, both], axis=0))
        for side, b in enumerate((2 * pair, 2 * pair + 1)):
            mine = out[:, grid * side : grid * (side + 1)]
            potential = jnp.zeros((box, grid), F32)
            for n in range(count):
                potential = jnp.where(owner == n, mine[box * n : box * (n + 1)], potential)
            stage_ref[b] = potential * psi_ref[b]
    span = SUB * box
    second = []
    for t in range(box // SUB):
        values = stage_ref[SUB * t : SUB * (t + 1)].reshape(span, grid)
        second.append(dot(inner, terms_of(values, 0)))
    second = jnp.concatenate(second, axis=0).reshape(box, box // SUB, SUB, grid)
    for t in range(box // SUB):
        values = dot(outer, terms_of(second[:, t].reshape(span, grid), 0))
        stage_ref[:, SUB * t : SUB * (t + 1), :] = values.reshape(box, SUB, grid)
    values = terms_of(stage_ref[...].reshape(box * box, grid), 1)
    out = dot(back, values, ((1,), (1,)))
    part = plan.box_part * count
    for p in range(pln):
        own_ref[p] = out[part * p : part * (p + 1)]
    me = where_ref[0]
    out_refs[0][0] = own_ref[me]
    for step in range(1, pln):
        out_refs[step][0] = own_ref[lax.rem(me + step, pln)].astype(BF16)


def sum_kernel(plan, *refs):
    out_ref = refs[plan.pln]
    total = refs[0][0]
    for ref in refs[1 : plan.pln]:
        total = total + ref[0].astype(F32)
    section = plan.box * plan.box
    count = plan.per_group
    for j in range(plan.box_part):
        out_ref[0, :, section * j : section * (j + 1)] = total[count * j : count * (j + 1)].astype(out_ref.dtype)


def per_device(plan, orbitals, occupations, box_offsets, kernel_spectrum):
    orb, pln, half, slots = plan.orb, plan.pln, plan.half, plan.slots
    groups, count, box, grid = plan.groups, plan.per_group, plan.box, plan.grid
    plane_index = lax.axis_index("pln")
    where = plane_index.astype(jnp.int32)[None]
    smem = pl.BlockSpec(memory_space=pltpu.SMEM)
    anywhere = pl.BlockSpec(memory_space=pl.ANY)
    vmem = pl.BlockSpec(memory_space=pltpu.VMEM)
    dma = pltpu.SemaphoreType.DMA
    coefs = orbitals.reshape(groups, count, orbitals.shape[1])
    by_ky = jnp.transpose(kernel_spectrum, (1, 2, 0))
    area = plan.area
    padded = area + 2 * SUB
    tables = [plan.depth, plan.inner, plan.outer]
    piece = jax.ShapeDtypeStruct((plan.ky_block, slots, grid), F32)
    edge = jax.ShapeDtypeStruct((1, slots, grid), F32)
    send, psi, wave, *pieces = pl.pallas_call(
        functools.partial(density_kernel, plan),
        grid=(groups,),
        in_specs=[smem, smem, smem] + [anywhere] * 6,
        out_specs=[anywhere] * (3 + 2 * half),
        out_shape=[
            jax.ShapeDtypeStruct((orb, groups, padded, grid), BF16),
            jax.ShapeDtypeStruct((groups, box, box, grid), F32),
            jax.ShapeDtypeStruct((groups, plan.rows, grid), F32),
            *[piece] * half,
            *[edge] * half,
        ],
        scratch_shapes=[
            pltpu.VMEM((count, orbitals.shape[1]), BF16),
            *[pltpu.VMEM(t.shape, t.dtype) for t in tables],
            pltpu.VMEM((plan.rows, grid), F32),
            pltpu.VMEM((grid, box * box), F32),
            pltpu.VMEM((box, box, grid), F32),
            pltpu.VMEM((orb, padded, grid), BF16),
            pltpu.VMEM((half, plan.ky_block, slots, plan.doubled), F32),
            pltpu.VMEM((half, slots, plan.doubled), F32),
            pltpu.VMEM((half, plan.ky_block, slots, grid), F32),
            pltpu.VMEM((half, slots, grid), F32),
            dma((2 * half,)),
            dma((2 * half,)),
            dma((12,)),
        ],
        compiler_params=pltpu.CompilerParams(vmem_limit_bytes=LARGE),
        name="density",
    )(where, box_offsets, occupations, coefs, *tables, plan.wave, by_ky)
    received = lax.all_to_all(send, "orb", split_axis=0, concat_axis=0, tiled=True)
    received = received.reshape(orb * groups, padded, grid)
    for step in range(1, half):
        pairs = [(g * half + i, g * half + (i + step) % half) for g in range(2) for i in range(half)]
        pieces[step] = lax.ppermute(pieces[step], "pln", pairs)
    for step in range(half):
        pieces[half + step] = lax.ppermute(pieces[half + step], "pln", [(0, half + step), (half, step)])
    pieces[:half] = [p.reshape(plan.ky_block * slots, grid) for p in pieces[:half]]

    small = pltpu.CompilerParams(vmem_limit_bytes=SMALL)
    send = pl.pallas_call(
        functools.partial(solve_kernel, plan),
        in_specs=[smem] + [vmem] * (1 + 2 * half),
        out_specs=vmem,
        out_shape=jax.ShapeDtypeStruct((orb * groups, area, grid), BF16),
        scratch_shapes=[
            pltpu.VMEM((grid * slots, grid), F32),
            pltpu.VMEM((grid * slots, grid), F32),
            pltpu.VMEM((2 * orb * groups, grid), jnp.int32),
            pltpu.SMEM((2 * orb * groups, grid), jnp.int32),
            dma,
        ],
        compiler_params=small,
        name="solve",
    )(where, received, *pieces)
    send = send.reshape(orb, groups, area, grid)
    received = lax.all_to_all(send, "orb", split_axis=0, concat_axis=0, tiled=True)
    part = plan.box_part * count
    finished = pl.pallas_call(
        functools.partial(terms_kernel, plan),
        grid=(groups,),
        in_specs=[
            smem,
            pl.BlockSpec((orb, 1, area, grid), lambda g: (0, g, 0, 0)),
            anywhere,
            pl.BlockSpec((1, plan.rows, grid), lambda g: (g, 0, 0)),
        ],
        out_specs=[pl.BlockSpec((1, part, box * box), lambda g: (g, 0, 0))] * pln,
        out_shape=[jax.ShapeDtypeStruct((groups, part, box * box), BF16 if step else F32) for step in range(pln)],
        scratch_shapes=[
            pltpu.VMEM((box, box, grid), F32),
            pltpu.VMEM((box, box, grid), F32),
            pltpu.VMEM((pln, part, box * box), F32),
            dma,
        ],
        compiler_params=small,
        name="terms",
    )(where, received, psi, wave)
    finished = list(finished)
    for step in range(1, pln):
        finished[step] = lax.ppermute(finished[step], "pln", [(p, (p + step) % pln) for p in range(pln)])
    cells = plan.box_part * box * box
    result = pl.pallas_call(
        functools.partial(sum_kernel, plan),
        grid=(groups,),
        in_specs=[pl.BlockSpec((1, part, box * box), lambda g: (g, 0, 0))] * pln,
        out_specs=pl.BlockSpec((1, count, cells), lambda g: (g, 0, 0)),
        out_shape=jax.ShapeDtypeStruct((groups, count, cells), BF16),
        compiler_params=small,
        name="sum",
    )(*finished)
    return result.reshape(groups * count, cells)


def solution(mesh):
    in_specs = (P("orb", None), P("orb"), P("orb", None), P(None, "pln", "orb"))
    out_specs = P("orb", "pln")

    def whole(orbitals, occupations, box_offsets, kernel_spectrum):
        plan = Plan(mesh, orbitals.shape, kernel_spectrum.shape)
        return jax.shard_map(
            functools.partial(per_device, plan), mesh=mesh, in_specs=in_specs, out_specs=out_specs, check_vma=False
        )(orbitals, occupations, box_offsets, kernel_spectrum)

    return whole
```

```python
import functools
import math

import jax
import jax.numpy as jnp
import numpy as np
from jax import lax
from jax.experimental import pallas as pl
from jax.experimental.pallas import tpu as pltpu
from jax.sharding import PartitionSpec as P

MAGIC_TAPS = (
    8.433424733352934e-07,
    -1.290557201342061e-05,
    8.76298447621056e-05,
    -0.00030158038132690465,
    0.001747237136729939,
    -0.009420470302010804,
    0.023738214637249424,
    0.0612625895831208,
    0.9940415697834004,
    -0.06048952891969835,
    -0.021030251609303816,
    0.013372634148547948,
    -0.0034412814449349387,
    0.0004944322768868992,
    -5.185986881173433e-05,
    2.7273449291197967e-06,
)
F32 = jnp.float32
BF16 = jnp.bfloat16
SUB = 8
LARGE = 60 * 1024 * 1024
SMALL = 32 * 1024 * 1024


def magic_filter(box):
    table = np.zeros((box, box))
    for row in range(box):
        for tap in range(-8, 8):
            if 0 <= row + tap < box:
                table[row, row + tap] = MAGIC_TAPS[tap + 8]
    return table.astype(np.float32).astype(np.float64)


def cas(product, doubled):
    angle = 2.0 * math.pi * (product % doubled) / doubled
    return np.cos(angle) + np.sin(angle)


def halves(table):
    high = np.asarray(table, np.float32).astype(jnp.bfloat16)
    low = (np.asarray(table, np.float64) - high.astype(np.float64)).astype(jnp.bfloat16)
    return high, low


def split(values):
    high = values.astype(BF16)
    low = (values - high.astype(F32)).astype(BF16)
    return high, low


def dot(left, right, dims=((1,), (0,))):
    return lax.dot_general(left, right, (dims, ((), ())), preferred_element_type=F32)


def terms_of(values, axis):
    high, low = split(values)
    return jnp.concatenate([high, high, low], axis=axis)


def stacked(table, axis):
    high, low = halves(table)
    return np.concatenate([high, low, high], axis=axis)


SINE = (1.0, -1.0 / 6, 1.0 / 120, -1.0 / 5040, 1.0 / 362880)
COSINE = (1.0, -1.0 / 2, 1.0 / 24, -1.0 / 720, 1.0 / 40320)


def turn(steps, doubled):
    quarter = doubled // 4
    place = (steps + quarter // 2) & (doubled - 1)
    quadrant = place // quarter
    angle = (place - quadrant * quarter - quarter // 2).astype(F32) * (2.0 * math.pi / doubled)
    square = angle * angle
    cosine, sine = COSINE[-1], SINE[-1]
    for even, odd in zip(COSINE[-2::-1], SINE[-2::-1]):
        cosine, sine = cosine * square + even, sine * square + odd
    return quadrant, cosine, sine * angle


def cosine_table(steps, doubled):
    quadrant, cosine, sine = turn(steps, doubled)
    value = jnp.where((quadrant & 1) == 0, cosine, -sine)
    return jnp.where(quadrant < 2, value, -value)


def cas_table(steps, doubled):
    quadrant, cosine, sine = turn(steps, doubled)
    value = jnp.where((quadrant & 1) == 0, cosine + sine, cosine - sine)
    return jnp.where(quadrant < 2, value, -value)


def iota(shape, axis):
    return lax.broadcasted_iota(jnp.int32, shape, axis)


def stack_terms(table, axis):
    high, low = split(table)
    return jnp.concatenate([high, low, high], axis=axis)


def tap_table(step):
    value = jnp.zeros(step.shape, F32)
    for tap in range(-8, 8):
        value = jnp.where(step == tap, np.float32(MAGIC_TAPS[tap + 8]), value)
    return value


def inner_back_table(box):
    span = SUB * box
    one = tap_table(iota((box, span), 0) - (iota((box, span), 1) & (box - 1)))
    whole = jnp.concatenate([one] * SUB, axis=0)
    return jnp.where(iota((span, span), 0) // box == iota((span, span), 1) // box, whole, 0.0)


def outer_back_table(box):
    span = SUB * box
    row, column = iota((span, span), 0), iota((span, span), 1)
    value = tap_table(row // SUB - column // SUB)
    return jnp.where((row & (SUB - 1)) == (column & (SUB - 1)), value, 0.0)


def depth_back_table(plan):
    grid, box, count = plan.grid, plan.box, plan.per_group
    row, column = iota((grid, grid), 0), iota((grid, grid), 1)
    value = tap_table(row // count - (column & (box - 1)))
    return jnp.where((row & (count - 1)) == column // box, value, 0.0)


def mode_table(plan, me, shape, axis):
    grid, doubled, half = plan.grid, plan.doubled, plan.half
    line = tuple(doubled if dim == axis else 1 for dim in range(2))
    group, index = me // half, lax.rem(me, half)
    mode = iota(line, axis)
    within = mode & (grid - 1)
    block = (index - within // plan.ky_block + half) & (half - 1)
    step = block * plan.ky_block + (within & (plan.ky_block - 1))
    edge = (mode >= grid) & (step == 0)
    frequency = jnp.where(edge, ((1 - group) * grid), group * grid + step)
    quarter = jnp.where((mode >= grid) & (step != 0), doubled // 4, 0)
    weight = jnp.where(step == 0, 1.0, 2.0)
    return cosine_table(frequency * iota(shape, 1 - axis) - quarter, doubled), weight


def depth_mode_table(plan, shape, axis):
    grid, doubled = plan.grid, plan.doubled
    place = iota(shape, axis)
    frequency = jnp.where(place < grid, place, grid - place)
    return jnp.where(place == grid, 0.0, cas_table(frequency * iota(shape, 1 - axis), doubled))


class Plan:
    def __init__(self, mesh, orbital_shape, kernel_shape):
        self.orb = mesh.shape["orb"]
        self.pln = mesh.shape["pln"]
        self.doubled = doubled = kernel_shape[0]
        self.grid = grid = doubled // 2
        self.box = box = round(orbital_shape[1] ** (1 / 3))
        self.per_group = grid // box
        self.groups = orbital_shape[0] // self.orb // self.per_group
        self.ky_block = kernel_shape[1] // self.pln
        self.kx_block = kernel_shape[2] // self.orb
        self.slots = SUB * -(-self.kx_block // (SUB * self.pln))
        self.half = self.pln // 2
        self.rows = self.orb * self.slots
        self.area = box * self.slots
        self.box_part = box // self.pln
        magic = magic_filter(box)
        eye = np.eye(SUB)
        depth = np.zeros((box, self.per_group, self.per_group, box))
        for n in range(self.per_group):
            depth[:, n, n, :] = magic.T
        depth = depth.reshape(grid, grid)
        self.depth = np.concatenate(halves(depth), axis=0)
        self.inner = stacked(np.kron(eye, magic), 1)
        self.outer = stacked(np.kron(magic, eye), 1)
        places = np.arange(grid)
        wave = np.zeros((self.pln, self.orb, self.slots, grid))
        for p in range(self.pln):
            for s in range(self.slots):
                within = p * self.slots + s
                if within < self.kx_block:
                    k = self.kx_block * np.arange(self.orb) + within
                    wave[p, :, s, :] = cas(k[:, None] * places[None, :], doubled)
        self.wave = wave.reshape(self.pln, self.rows, grid).astype(np.float32)
        self.quarter = box // 4


def lane_owner(shape, box):
    return lax.broadcasted_iota(jnp.int32, shape, len(shape) - 1) // box


def start_copies(sems, first, *pairs):
    copies = []
    for number, (source, target) in enumerate(pairs):
        copy = pltpu.make_async_copy(source, target, sems.at[first + number])
        copy.start()
        copies.append(copy)
    return copies


def wait_copies(copies):
    for copy in copies:
        copy.wait()


def density_kernel(
    plan, where_ref, corner_ref, weight_ref, coef_any, depth_any, inner_any, outer_any, wave_any, spectrum_any,
    send_ref, psi_any, wave_out_any, *refs,
):
    piece_refs = refs[: 2 * plan.half]
    coef_ref, depth_ref, inner_ref, outer_ref, wave_ref, own_wave_ref, stage_ref, psi_ref = refs[2 * plan.half : -4]
    block_ref, edge_ref, spectrum_sems, sems = refs[-4:]
    box, grid, count, slots = plan.box, plan.grid, plan.per_group, plan.slots
    section = box * box
    span = SUB * box
    me = where_ref[0]
    coef_copy = pltpu.make_async_copy(coef_any, coef_ref, sems.at[0])
    coef_copy.start()
    fetched = start_copies(
        sems, 1, (depth_any, depth_ref), (inner_any, inner_ref), (outer_any, outer_ref), (wave_any.at[me], wave_ref)
    )
    spectrum = spectrum_copies(plan, me, spectrum_any, block_ref, edge_ref, spectrum_sems)
    for copy in spectrum:
        copy.start()
    owner = lane_owner((1, grid), box)
    coef_copy.wait()
    wait_copies(fetched)
    for group in range(plan.groups):
        for p in range(box):
            stage_ref[count * p : count * (p + 1), :] = coef_ref[group, :, section * p : section * (p + 1)].astype(F32)
        coef = stage_ref[...].astype(BF16)
        first = dot(jnp.concatenate([coef, coef], axis=0), depth_ref[...], ((0,), (0,)))
        inner, outer = inner_ref[...], outer_ref[...]
        second = [dot(inner, terms_of(first[span * t : span * (t + 1)], 0)) for t in range(box // SUB)]
        second = jnp.concatenate(second, axis=0).reshape(box, box // SUB, SUB, grid)
        for t in range(box // SUB):
            third = dot(outer, terms_of(second[:, t].reshape(span, grid), 0))
            psi_ref[:, SUB * t : SUB * (t + 1), :] = third.reshape(box, SUB, grid)
        sent = start_copies(sems, 5, (psi_ref, psi_any.at[group]))
        whole_wave = wave_ref[...]
        wave = jnp.zeros_like(whole_wave)
        weight = jnp.zeros((1, grid), F32)
        kind = iota((2 * SUB, 1), 0)
        corner = jnp.zeros((2 * SUB, grid), F32)
        for n in range(count):
            number = group * count + n
            shift = lax.rem(box * n - corner_ref[number, 2] + grid, grid)
            wave = jnp.where(owner == n, pltpu.roll(whole_wave, shift, 1), wave)
            weight = jnp.where(owner == n, weight_ref[number], weight)
            place = jnp.where(kind == 0, corner_ref[number, 0], corner_ref[number, 1])
            corner = jnp.where(owner == n, place.astype(F32), corner)
        own_wave_ref[...] = wave
        sent += start_copies(sems, 6, (own_wave_ref, wave_out_any.at[group]))
        for o in range(plan.orb):
            send_ref[o, group, plan.area :, :] = corner.astype(send_ref.dtype)
        high, low = split(wave)
        wave_terms = jnp.concatenate([high, low, high], axis=1)
        if group == 0:
            wait_copies(spectrum)
            fold_spectrum(plan, piece_refs, block_ref, edge_ref)
        for pair in range(box // 2):
            columns = []
            for b in (2 * pair, 2 * pair + 1):
                psi = psi_ref[b]
                density = psi * psi * weight
                columns.append(jnp.concatenate([jnp.where(owner == n, density, 0.0) for n in range(count)], axis=0))
            out = dot(wave_terms, terms_of(jnp.concatenate(columns, axis=1), 0))
            for o in range(plan.orb):
                mine = out[slots * o : slots * (o + 1)]
                tile = jnp.concatenate([mine[:, :grid], mine[:, grid:]], axis=0)
                send_ref[o, group, 2 * slots * pair : 2 * slots * (pair + 1), :] = tile.astype(send_ref.dtype)
        wait_copies(sent)


def spectrum_copies(plan, me, spectrum_any, block_ref, edge_ref, sems):
    half, slots = plan.half, plan.slots
    group, index = me // half, lax.rem(me, half)

    def fetch(target, source, buffer, number):
        first = jnp.minimum(target * slots, max(plan.kx_block - slots, 0))
        first = pl.multiple_of(first, SUB)
        return pltpu.make_async_copy(source.at[:, pl.ds(first, slots), :], buffer, sems.at[number])

    copies = []
    for step in range(half):
        copies.append(fetch(group * half + lax.rem(index + step, half), spectrum_any, block_ref.at[step], step))
    for step in range(half):
        target = (1 - group) * half + step
        copies.append(fetch(target, spectrum_any.at[pl.ds(0, 1)], edge_ref.at[pl.ds(step, 1)], half + step))
    return copies


def fold_spectrum(plan, piece_refs, block_ref, edge_ref):
    half, grid = plan.half, plan.grid
    odd = (iota((1, 1, grid), 2) & 1) == 1

    def fold(values):
        last = values[..., grid : grid + 1]
        return values[..., :grid] + jnp.where(odd, last, -last)

    for step in range(half):
        piece_refs[step][...] = fold(block_ref[step])
        piece_refs[half + step][...] = fold(edge_ref[pl.ds(step, 1)])


def tables_kernel(plan, where_ref, wave_any, piece_any, *refs):
    forward_y_ref, forward_z_ref, inverse_y_ref, inverse_z_ref, inner_ref, outer_ref, back_ref = refs[:7]
    wave_out_ref, piece_ref, wave_ref, sems = refs[7:]
    grid, doubled, me = plan.grid, plan.doubled, where_ref[0]
    copies = start_copies(sems, 0, (wave_any, wave_ref), (piece_any, piece_ref))
    forward, _ = mode_table(plan, me, (doubled, grid), 0)
    forward_y_ref[...] = jnp.concatenate(split(forward), axis=1)
    forward_z_ref[...] = jnp.concatenate(split(depth_mode_table(plan, (grid, doubled), 1)), axis=0)
    inverse, weight = mode_table(plan, me, (grid, doubled), 1)
    inverse_y_ref[...] = stack_terms(inverse * (weight * (1.0 / doubled**3)), 1)
    inverse_z_ref[...] = stack_terms(depth_mode_table(plan, (doubled, grid), 0), 0)
    inner_ref[...] = stack_terms(inner_back_table(plan.box), 1)
    outer_ref[...] = stack_terms(outer_back_table(plan.box), 1)
    back_ref[...] = stack_terms(depth_back_table(plan), 1)
    wait_copies(copies)
    for group in range(plan.groups):
        wave_out_ref[group] = jnp.concatenate(split(wave_ref[group].T), axis=1)


def solve_kernel(plan, where_ref, recv_ref, *refs):
    half, slots, grid, box, count = plan.half, plan.slots, plan.grid, plan.box, plan.per_group
    piece_refs, edge_refs = refs[:half], refs[half : 2 * half]
    forward_y_ref, forward_z_ref, inverse_y_ref, inverse_z_ref = refs[2 * half : 2 * half + 4]
    send_ref, field_ref, result_ref, table_ref, corner_ref, sem = refs[2 * half + 4 :]
    me = where_ref[0]
    depth = plan.area
    all_groups = plan.orb * plan.groups
    owner = lane_owner((1, grid), box)
    for group in range(all_groups):
        tile = recv_ref[group, depth : depth + 2 * SUB, :].astype(F32).astype(jnp.int32)
        table_ref[2 * group : 2 * group + 2, :] = tile[:2]
    copy = pltpu.make_async_copy(table_ref, corner_ref, sem)
    copy.start()
    field_ref[...] = jnp.zeros_like(field_ref)
    forward_y, forward_z = forward_y_ref[...], forward_z_ref[...]
    inverse_y, inverse_z = inverse_y_ref[...], inverse_z_ref[...]
    copy.wait()

    def start(group, n):
        return pl.multiple_of(corner_ref[2 * group + 1, box * n] * slots, SUB)

    def place(group, carry):
        values = recv_ref[group, :depth, :].astype(F32)
        for n in range(count):
            shift = lax.rem(corner_ref[2 * group, box * n] - box * n + grid, grid)
            moved = pltpu.roll(jnp.where(owner == n, values, 0.0), shift, 1)
            field_ref[pl.ds(start(group, n), depth), :] += moved
        return carry

    lax.fori_loop(0, all_groups, place, 0)
    row = iota((grid, 1), 0)
    edge_row = lax.rem(me, half) * plan.ky_block
    edges = edge_refs[0][0]
    for ref in edge_refs[1:]:
        edges = edges + ref[0]
    for pair in range(slots // 2):
        both = (2 * pair, 2 * pair + 1)
        planes = jnp.concatenate([field_ref[pl.ds(s, grid, stride=slots), :] for s in both], axis=1)
        planes = planes.astype(BF16)
        modes = dot(forward_y, jnp.concatenate([planes, planes], axis=0)).astype(BF16)
        back = []
        for side, s in enumerate(both):
            spectrum = jnp.concatenate([ref[pl.ds(s, plan.ky_block, stride=slots), :] for ref in piece_refs], axis=0)
            other = jnp.where(row == edge_row, edges[s : s + 1], spectrum)
            spectrum = jnp.concatenate([spectrum, other], axis=0)
            mine = modes[:, grid * side : grid * (side + 1)]
            mine = dot(jnp.concatenate([mine, mine], axis=1), forward_z)
            mine = mine * jnp.concatenate([spectrum, spectrum], axis=1)
            back.append(dot(terms_of(mine, 1), inverse_z))
        planes = dot(inverse_y, terms_of(jnp.concatenate(back, axis=1), 0))
        for side, s in enumerate(both):
            result_ref[pl.ds(s, grid, stride=slots), :] = planes[:, grid * side : grid * (side + 1)]

    def cut(group, carry):
        values = jnp.zeros((depth, grid), F32)
        for n in range(count):
            shift = lax.rem(box * n - corner_ref[2 * group, box * n] + grid, grid)
            rows = result_ref[pl.ds(start(group, n), depth), :]
            values = jnp.where(owner == n, pltpu.roll(rows, shift, 1), values)
        send_ref[group] = values.astype(send_ref.dtype)
        return carry

    lax.fori_loop(0, all_groups, cut, 0)


def terms_kernel(plan, where_ref, recv_ref, psi_any, wave_ref, inner_ref, outer_ref, back_ref, *refs):
    box, grid, count, slots, pln = plan.box, plan.grid, plan.per_group, plan.slots, plan.pln
    out_refs = refs[:pln]
    psi_ref, stage_ref, own_ref, sem = refs[pln:]
    group = pl.program_id(0)
    copy = pltpu.make_async_copy(psi_any.at[group], psi_ref, sem)
    copy.start()
    owner = lane_owner((1, grid), box)
    wave, inner, outer, back = wave_ref[0], inner_ref[...], outer_ref[...], back_ref[...]
    copy.wait()
    for pair in range(box // 2):
        tiles = [recv_ref[o, 0, 2 * slots * pair : 2 * slots * (pair + 1), :].astype(F32) for o in range(plan.orb)]
        columns = [jnp.concatenate([t[slots * side : slots * (side + 1)] for t in tiles], axis=0) for side in range(2)]
        both = jnp.concatenate(columns, axis=1).astype(BF16)
        out = dot(wave, jnp.concatenate([both, both], axis=0))
        for side, b in enumerate((2 * pair, 2 * pair + 1)):
            mine = out[:, grid * side : grid * (side + 1)]
            potential = jnp.zeros((box, grid), F32)
            for n in range(count):
                potential = jnp.where(owner == n, mine[box * n : box * (n + 1)], potential)
            stage_ref[b] = potential * psi_ref[b]
    span = SUB * box
    second = []
    for t in range(box // SUB):
        values = stage_ref[SUB * t : SUB * (t + 1)].reshape(span, grid)
        second.append(dot(inner, terms_of(values, 0)))
    second = jnp.concatenate(second, axis=0).reshape(box, box // SUB, SUB, grid)
    for t in range(box // SUB):
        values = dot(outer, terms_of(second[:, t].reshape(span, grid), 0))
        stage_ref[:, SUB * t : SUB * (t + 1), :] = values.reshape(box, SUB, grid)
    values = terms_of(stage_ref[...].reshape(box * box, grid), 1)
    out = dot(back, values, ((1,), (1,)))
    part = plan.box_part * count
    for p in range(pln):
        own_ref[p] = out[part * p : part * (p + 1)]
    me = where_ref[0]
    out_refs[0][0] = own_ref[me]
    for step in range(1, pln):
        out_refs[step][0] = own_ref[lax.rem(me + step, pln)].astype(BF16)


def sum_kernel(plan, *refs):
    out_ref = refs[plan.pln]
    total = refs[0][0]
    for ref in refs[1 : plan.pln]:
        total = total + ref[0].astype(F32)
    section = plan.box * plan.box
    count = plan.per_group
    for j in range(plan.box_part):
        out_ref[0, :, section * j : section * (j + 1)] = total[count * j : count * (j + 1)].astype(out_ref.dtype)


def per_device(plan, orbitals, occupations, box_offsets, kernel_spectrum):
    orb, pln, half, slots = plan.orb, plan.pln, plan.half, plan.slots
    groups, count, box, grid = plan.groups, plan.per_group, plan.box, plan.grid
    plane_index = lax.axis_index("pln")
    where = plane_index.astype(jnp.int32)[None]
    smem = pl.BlockSpec(memory_space=pltpu.SMEM)
    anywhere = pl.BlockSpec(memory_space=pl.ANY)
    vmem = pl.BlockSpec(memory_space=pltpu.VMEM)
    dma = pltpu.SemaphoreType.DMA
    coefs = orbitals.reshape(groups, count, orbitals.shape[1])
    by_ky = jnp.transpose(kernel_spectrum, (1, 2, 0))
    area = plan.area
    padded = area + 2 * SUB
    tables = [plan.depth, plan.inner, plan.outer]
    piece = jax.ShapeDtypeStruct((plan.ky_block, slots, grid), F32)
    edge = jax.ShapeDtypeStruct((1, slots, grid), F32)
    send, psi, wave, *pieces = pl.pallas_call(
        functools.partial(density_kernel, plan),
        in_specs=[smem, smem, smem] + [anywhere] * 6,
        out_specs=[vmem, anywhere, anywhere] + [vmem] * (2 * half),
        out_shape=[
            jax.ShapeDtypeStruct((orb, groups, padded, grid), BF16),
            jax.ShapeDtypeStruct((groups, box, box, grid), F32),
            jax.ShapeDtypeStruct((groups, plan.rows, grid), F32),
            *[piece] * half,
            *[edge] * half,
        ],
        scratch_shapes=[
            pltpu.VMEM(coefs.shape, BF16),
            *[pltpu.VMEM(t.shape, t.dtype) for t in tables],
            pltpu.VMEM((plan.rows, grid), F32),
            pltpu.VMEM((plan.rows, grid), F32),
            pltpu.VMEM((grid, box * box), F32),
            pltpu.VMEM((box, box, grid), F32),
            pltpu.VMEM((half, plan.ky_block, slots, plan.doubled), F32),
            pltpu.VMEM((half, slots, plan.doubled), F32),
            dma((2 * half,)),
            dma((7,)),
        ],
        compiler_params=pltpu.CompilerParams(vmem_limit_bytes=LARGE),
        name="density",
    )(where, box_offsets, occupations, coefs, *tables, plan.wave, by_ky)
    received = lax.all_to_all(send, "orb", split_axis=0, concat_axis=0, tiled=True)
    received = received.reshape(orb * groups, padded, grid)
    for step in range(1, half):
        pairs = [(g * half + i, g * half + (i + step) % half) for g in range(2) for i in range(half)]
        pieces[step] = lax.ppermute(pieces[step], "pln", pairs)
    for step in range(half):
        pieces[half + step] = lax.ppermute(pieces[half + step], "pln", [(0, half + step), (half, step)])
    pieces[:half] = [p.reshape(plan.ky_block * slots, grid) for p in pieces[:half]]

    small = pltpu.CompilerParams(vmem_limit_bytes=SMALL)
    span = SUB * box
    shapes = [(plan.doubled, 2 * grid), (2 * grid, plan.doubled), (grid, 3 * plan.doubled), (3 * plan.doubled, grid)]
    shapes += [(span, 3 * span), (span, 3 * span), (grid, 3 * grid), (groups, grid, 2 * plan.rows)]
    tables = pl.pallas_call(
        functools.partial(tables_kernel, plan),
        in_specs=[smem, anywhere, anywhere],
        out_specs=[vmem] * (len(shapes) + 1),
        out_shape=[*[jax.ShapeDtypeStruct(shape, BF16) for shape in shapes], jax.ShapeDtypeStruct(pieces[0].shape, F32)],
        scratch_shapes=[pltpu.VMEM(wave.shape, F32), dma((2,))],
        compiler_params=small,
        name="tables",
    )(where, wave, pieces[0])
    pieces[0] = tables[8]
    send = pl.pallas_call(
        functools.partial(solve_kernel, plan),
        in_specs=[smem] + [vmem] * (5 + 2 * half),
        out_specs=vmem,
        out_shape=jax.ShapeDtypeStruct((orb * groups, area, grid), BF16),
        scratch_shapes=[
            pltpu.VMEM((grid * slots, grid), F32),
            pltpu.VMEM((grid * slots, grid), F32),
            pltpu.VMEM((2 * orb * groups, grid), jnp.int32),
            pltpu.SMEM((2 * orb * groups, grid), jnp.int32),
            dma,
        ],
        compiler_params=small,
        name="solve",
    )(where, received, *pieces, *tables[:4])
    send = send.reshape(orb, groups, area, grid)
    received = lax.all_to_all(send, "orb", split_axis=0, concat_axis=0, tiled=True)
    part = plan.box_part * count
    finished = pl.pallas_call(
        functools.partial(terms_kernel, plan),
        grid=(groups,),
        in_specs=[
            smem,
            pl.BlockSpec((orb, 1, area, grid), lambda g: (0, g, 0, 0)),
            anywhere,
            pl.BlockSpec((1, grid, 2 * plan.rows), lambda g: (g, 0, 0)),
            vmem,
            vmem,
            vmem,
        ],
        out_specs=[pl.BlockSpec((1, part, box * box), lambda g: (g, 0, 0))] * pln,
        out_shape=[jax.ShapeDtypeStruct((groups, part, box * box), BF16 if step else F32) for step in range(pln)],
        scratch_shapes=[
            pltpu.VMEM((box, box, grid), F32),
            pltpu.VMEM((box, box, grid), F32),
            pltpu.VMEM((pln, part, box * box), F32),
            dma,
        ],
        compiler_params=small,
        name="terms",
    )(where, received, psi, tables[7], *tables[4:7])
    finished = list(finished)
    for step in range(1, pln):
        finished[step] = lax.ppermute(finished[step], "pln", [(p, (p + step) % pln) for p in range(pln)])
    cells = plan.box_part * box * box
    result = pl.pallas_call(
        functools.partial(sum_kernel, plan),
        grid=(groups,),
        in_specs=[pl.BlockSpec((1, part, box * box), lambda g: (g, 0, 0))] * pln,
        out_specs=pl.BlockSpec((1, count, cells), lambda g: (g, 0, 0)),
        out_shape=jax.ShapeDtypeStruct((groups, count, cells), BF16),
        compiler_params=small,
        name="sum",
    )(*finished)
    return result.reshape(groups * count, cells)


def solution(mesh):
    in_specs = (P("orb", None), P("orb"), P("orb", None), P(None, "pln", "orb"))
    out_specs = P("orb", "pln")

    def whole(orbitals, occupations, box_offsets, kernel_spectrum):
        plan = Plan(mesh, orbitals.shape, kernel_spectrum.shape)
        return jax.shard_map(
            functools.partial(per_device, plan), mesh=mesh, in_specs=in_specs, out_specs=out_specs, check_vma=False
        )(orbitals, occupations, box_offsets, kernel_spectrum)

    return whole
```

```python
import functools
import math

import jax
import jax.numpy as jnp
import numpy as np
from jax import lax
from jax.experimental import pallas as pl
from jax.experimental.pallas import tpu as pltpu
from jax.sharding import PartitionSpec as P

MAGIC_TAPS = (
    8.433424733352934e-07,
    -1.290557201342061e-05,
    8.76298447621056e-05,
    -0.00030158038132690465,
    0.001747237136729939,
    -0.009420470302010804,
    0.023738214637249424,
    0.0612625895831208,
    0.9940415697834004,
    -0.06048952891969835,
    -0.021030251609303816,
    0.013372634148547948,
    -0.0034412814449349387,
    0.0004944322768868992,
    -5.185986881173433e-05,
    2.7273449291197967e-06,
)
F32 = jnp.float32
BF16 = jnp.bfloat16
SUB = 8
LARGE = 60 * 1024 * 1024
SMALL = 32 * 1024 * 1024


def magic_filter(box):
    table = np.zeros((box, box))
    for row in range(box):
        for tap in range(-8, 8):
            if 0 <= row + tap < box:
                table[row, row + tap] = MAGIC_TAPS[tap + 8]
    return table.astype(np.float32).astype(np.float64)


def cas(product, doubled):
    angle = 2.0 * math.pi * (product % doubled) / doubled
    return np.cos(angle) + np.sin(angle)


def halves(table):
    high = np.asarray(table, np.float32).astype(jnp.bfloat16)
    low = (np.asarray(table, np.float64) - high.astype(np.float64)).astype(jnp.bfloat16)
    return high, low


def split(values):
    high = values.astype(BF16)
    low = (values - high.astype(F32)).astype(BF16)
    return high, low


def dot(left, right, dims=((1,), (0,))):
    return lax.dot_general(left, right, (dims, ((), ())), preferred_element_type=F32)


def terms_of(values, axis):
    high, low = split(values)
    return jnp.concatenate([high, high, low], axis=axis)


def stacked(table, axis):
    high, low = halves(table)
    return np.concatenate([high, low, high], axis=axis)


SINE = (1.0, -1.0 / 6, 1.0 / 120, -1.0 / 5040, 1.0 / 362880)
COSINE = (1.0, -1.0 / 2, 1.0 / 24, -1.0 / 720, 1.0 / 40320)


def turn(steps, doubled):
    quarter = doubled // 4
    place = (steps + quarter // 2) & (doubled - 1)
    quadrant = place // quarter
    angle = (place - quadrant * quarter - quarter // 2).astype(F32) * (2.0 * math.pi / doubled)
    square = angle * angle
    cosine, sine = COSINE[-1], SINE[-1]
    for even, odd in zip(COSINE[-2::-1], SINE[-2::-1]):
        cosine, sine = cosine * square + even, sine * square + odd
    return quadrant, cosine, sine * angle


def cosine_table(steps, doubled):
    quadrant, cosine, sine = turn(steps, doubled)
    value = jnp.where((quadrant & 1) == 0, cosine, -sine)
    return jnp.where(quadrant < 2, value, -value)


def cas_table(steps, doubled):
    quadrant, cosine, sine = turn(steps, doubled)
    value = jnp.where((quadrant & 1) == 0, cosine + sine, cosine - sine)
    return jnp.where(quadrant < 2, value, -value)


def iota(shape, axis):
    return lax.broadcasted_iota(jnp.int32, shape, axis)


def stack_terms(table, axis):
    high, low = split(table)
    return jnp.concatenate([high, low, high], axis=axis)


def tap_table(step):
    value = jnp.zeros(step.shape, F32)
    for tap in range(-8, 8):
        value = jnp.where(step == tap, np.float32(MAGIC_TAPS[tap + 8]), value)
    return value


def inner_back_table(box):
    span = SUB * box
    one = tap_table(iota((box, span), 0) - (iota((box, span), 1) & (box - 1)))
    whole = jnp.concatenate([one] * SUB, axis=0)
    return jnp.where(iota((span, span), 0) // box == iota((span, span), 1) // box, whole, 0.0)


def outer_back_table(box):
    span = SUB * box
    row, column = iota((span, span), 0), iota((span, span), 1)
    value = tap_table(row // SUB - column // SUB)
    return jnp.where((row & (SUB - 1)) == (column & (SUB - 1)), value, 0.0)


def depth_back_table(plan):
    grid, box, count = plan.grid, plan.box, plan.per_group
    row, column = iota((grid, grid), 0), iota((grid, grid), 1)
    value = tap_table(row // count - (column & (box - 1)))
    return jnp.where((row & (count - 1)) == column // box, value, 0.0)


def mode_table(plan, me, shape, axis):
    grid, doubled, half = plan.grid, plan.doubled, plan.half
    line = tuple(doubled if dim == axis else 1 for dim in range(2))
    group, index = me // half, lax.rem(me, half)
    mode = iota(line, axis)
    within = mode & (grid - 1)
    block = (index - within // plan.ky_block + half) & (half - 1)
    step = block * plan.ky_block + (within & (plan.ky_block - 1))
    edge = (mode >= grid) & (step == 0)
    frequency = jnp.where(edge, ((1 - group) * grid), group * grid + step)
    quarter = jnp.where((mode >= grid) & (step != 0), doubled // 4, 0)
    weight = jnp.where(step == 0, 1.0, 2.0)
    return cosine_table(frequency * iota(shape, 1 - axis) - quarter, doubled), weight


def depth_mode_table(plan, shape, axis):
    grid, doubled = plan.grid, plan.doubled
    place = iota(shape, axis)
    frequency = jnp.where(place < grid, place, grid - place)
    return jnp.where(place == grid, 0.0, cas_table(frequency * iota(shape, 1 - axis), doubled))


class Plan:
    def __init__(self, mesh, orbital_shape, kernel_shape):
        self.orb = mesh.shape["orb"]
        self.pln = mesh.shape["pln"]
        self.doubled = doubled = kernel_shape[0]
        self.grid = grid = doubled // 2
        self.box = box = round(orbital_shape[1] ** (1 / 3))
        self.per_group = grid // box
        self.groups = orbital_shape[0] // self.orb // self.per_group
        self.ky_block = kernel_shape[1] // self.pln
        self.kx_block = kernel_shape[2] // self.orb
        self.slots = SUB * -(-self.kx_block // (SUB * self.pln))
        self.half = self.pln // 2
        self.rows = self.orb * self.slots
        self.area = box * self.slots
        self.box_part = box // self.pln
        magic = magic_filter(box)
        eye = np.eye(SUB)
        depth = np.zeros((box, self.per_group, self.per_group, box))
        for n in range(self.per_group):
            depth[:, n, n, :] = magic.T
        depth = depth.reshape(grid, grid)
        self.depth = np.concatenate(halves(depth), axis=0)
        self.inner = stacked(np.kron(eye, magic), 1)
        self.outer = stacked(np.kron(magic, eye), 1)
        places = np.arange(grid)
        wave = np.zeros((self.pln, self.orb, self.slots, grid))
        for p in range(self.pln):
            for s in range(self.slots):
                within = p * self.slots + s
                if within < self.kx_block:
                    k = self.kx_block * np.arange(self.orb) + within
                    wave[p, :, s, :] = cas(k[:, None] * places[None, :], doubled)
        self.wave = wave.reshape(self.pln, self.rows, grid).astype(np.float32)
        self.quarter = box // 4


def lane_owner(shape, box):
    return lax.broadcasted_iota(jnp.int32, shape, len(shape) - 1) // box


def start_copies(sems, first, *pairs):
    copies = []
    for number, (source, target) in enumerate(pairs):
        copy = pltpu.make_async_copy(source, target, sems.at[first + number])
        copy.start()
        copies.append(copy)
    return copies


def wait_copies(copies):
    for copy in copies:
        copy.wait()


def density_kernel(
    plan, where_ref, corner_ref, weight_ref, coef_any, depth_any, inner_any, outer_any, wave_any, spectrum_any,
    send_any, psi_any, wave_out_any, *refs,
):
    half = plan.half
    piece_anys = refs[: 2 * half]
    coef_ref, depth_ref, inner_ref, outer_ref, wave_ref, own_wave_ref, stage_ref, psi_ref, send_ref = refs[2 * half : -7]
    block_ref, edge_ref, block_out_ref, edge_out_ref, spectrum_sems, out_sems, sems = refs[-7:]
    box, grid, count, slots = plan.box, plan.grid, plan.per_group, plan.slots
    section = box * box
    span = SUB * box
    me = lax.rem(where_ref[0], plan.pln)
    coef_copy = pltpu.make_async_copy(coef_any, coef_ref, sems.at[0])
    coef_copy.start()
    fetched = start_copies(
        sems, 1, (depth_any, depth_ref), (inner_any, inner_ref), (outer_any, outer_ref), (wave_any.at[me], wave_ref)
    )
    spectrum = spectrum_copies(plan, me, spectrum_any, block_ref, edge_ref, spectrum_sems)
    for copy in spectrum:
        copy.start()
    owner = lane_owner((1, grid), box)
    coef_copy.wait()
    wait_copies(fetched)
    for group in range(plan.groups):
        for p in range(box):
            stage_ref[count * p : count * (p + 1), :] = coef_ref[group, :, section * p : section * (p + 1)].astype(F32)
        coef = stage_ref[...].astype(BF16)
        first = dot(jnp.concatenate([coef, coef], axis=0), depth_ref[...], ((0,), (0,)))
        inner, outer = inner_ref[...], outer_ref[...]
        second = [dot(inner, terms_of(first[span * t : span * (t + 1)], 0)) for t in range(box // SUB)]
        second = jnp.concatenate(second, axis=0).reshape(box, box // SUB, SUB, grid)
        for t in range(box // SUB):
            third = dot(outer, terms_of(second[:, t].reshape(span, grid), 0))
            psi_ref[:, SUB * t : SUB * (t + 1), :] = third.reshape(box, SUB, grid)
        sent = start_copies(sems, 5, (psi_ref, psi_any.at[group]))
        whole_wave = wave_ref[...]
        wave = jnp.zeros_like(whole_wave)
        weight = jnp.zeros((1, grid), F32)
        kind = iota((2 * SUB, 1), 0)
        corner = jnp.zeros((2 * SUB, grid), F32)
        for n in range(count):
            number = group * count + n
            shift = lax.rem(box * n - corner_ref[number, 2] + grid, grid)
            wave = jnp.where(owner == n, pltpu.roll(whole_wave, shift, 1), wave)
            weight = jnp.where(owner == n, weight_ref[number], weight)
            place = jnp.where(kind == 0, corner_ref[number, 0], corner_ref[number, 1])
            corner = jnp.where(owner == n, place.astype(F32), corner)
        own_wave_ref[...] = wave
        sent += start_copies(sems, 6, (own_wave_ref, wave_out_any.at[group]))
        for o in range(plan.orb):
            send_ref[o, plan.area :, :] = corner.astype(send_ref.dtype)
        high, low = split(wave)
        wave_terms = jnp.concatenate([high, low, high], axis=1)
        if group == 0:
            wait_copies(spectrum)
            folded = fold_spectrum(plan, piece_anys, block_ref, edge_ref, block_out_ref, edge_out_ref, out_sems)
        rows = pl.ds(plan.area, 2 * SUB)
        sent += start_copies(sems, 7, (send_ref.at[:, rows, :], send_any.at[:, group, rows, :]))
        per_part = plan.quarter // 2
        for pair in range(box // 2):
            columns = []
            for b in (2 * pair, 2 * pair + 1):
                psi = psi_ref[b]
                density = psi * psi * weight
                columns.append(jnp.concatenate([jnp.where(owner == n, density, 0.0) for n in range(count)], axis=0))
            out = dot(wave_terms, terms_of(jnp.concatenate(columns, axis=1), 0))
            for o in range(plan.orb):
                mine = out[slots * o : slots * (o + 1)]
                tile = jnp.concatenate([mine[:, :grid], mine[:, grid:]], axis=0)
                send_ref[o, 2 * slots * pair : 2 * slots * (pair + 1), :] = tile.astype(send_ref.dtype)
            if pair % per_part == per_part - 1:
                part = pair // per_part
                rows = pl.ds(plan.quarter * slots * part, plan.quarter * slots)
                sent += start_copies(sems, 8 + part, (send_ref.at[:, rows, :], send_any.at[:, group, rows, :]))
        wait_copies(sent)
    wait_copies(folded)


def spectrum_copies(plan, me, spectrum_any, block_ref, edge_ref, sems):
    half, slots = plan.half, plan.slots
    group, index = me // half, lax.rem(me, half)

    def fetch(target, source, buffer, number):
        first = jnp.minimum(target * slots, max(plan.kx_block - slots, 0))
        first = pl.multiple_of(first, SUB)
        return pltpu.make_async_copy(source.at[:, pl.ds(first, slots), :], buffer, sems.at[number])

    copies = []
    for step in range(half):
        copies.append(fetch(group * half + lax.rem(index + step, half), spectrum_any, block_ref.at[step], step))
    for step in range(half):
        target = (1 - group) * half + step
        copies.append(fetch(target, spectrum_any.at[pl.ds(0, 1)], edge_ref.at[pl.ds(step, 1)], half + step))
    return copies


def fold_spectrum(plan, piece_anys, block_ref, edge_ref, block_out_ref, edge_out_ref, sems):
    half, grid = plan.half, plan.grid
    odd = (iota((1, 1, grid), 2) & 1) == 1

    def fold(values):
        last = values[..., grid : grid + 1]
        return values[..., :grid] + jnp.where(odd, last, -last)

    for step in range(half):
        block_out_ref[step] = fold(block_ref[step])
    edge_out_ref[...] = fold(edge_ref[...])
    pairs = [(block_out_ref.at[step], piece_anys[step]) for step in range(half)]
    pairs += [(edge_out_ref.at[pl.ds(step, 1)], piece_anys[half + step]) for step in range(half)]
    return start_copies(sems, 0, *pairs)


def tables_kernel(plan, where_ref, piece_any, *refs):
    forward_y_ref, forward_z_ref, inverse_y_ref, inverse_z_ref, inner_ref, outer_ref, back_ref = refs[:7]
    piece_ref, sems = refs[7:]
    grid, doubled, me = plan.grid, plan.doubled, lax.rem(where_ref[0], plan.pln)
    copies = start_copies(sems, 0, (piece_any, piece_ref))
    forward, _ = mode_table(plan, me, (doubled, grid), 0)
    forward_y_ref[...] = jnp.concatenate(split(forward), axis=1)
    forward_z_ref[...] = jnp.concatenate(split(depth_mode_table(plan, (grid, doubled), 1)), axis=0)
    inverse, weight = mode_table(plan, me, (grid, doubled), 1)
    inverse_y_ref[...] = stack_terms(inverse * (weight * (1.0 / doubled**3)), 1)
    inverse_z_ref[...] = stack_terms(depth_mode_table(plan, (doubled, grid), 0), 0)
    inner_ref[...] = stack_terms(inner_back_table(plan.box), 1)
    outer_ref[...] = stack_terms(outer_back_table(plan.box), 1)
    back_ref[...] = stack_terms(depth_back_table(plan), 1)
    wait_copies(copies)


def solve_kernel(plan, where_ref, recv_ref, *refs):
    half, slots, grid, box, count = plan.half, plan.slots, plan.grid, plan.box, plan.per_group
    piece_refs, edge_refs = refs[:half], refs[half : 2 * half]
    forward_y_ref, forward_z_ref, inverse_y_ref, inverse_z_ref = refs[2 * half : 2 * half + 4]
    send_refs = refs[2 * half + 4 : 2 * half + 4 + plan.orb]
    field_ref, result_ref, table_ref, corner_ref, sem = refs[2 * half + 4 + plan.orb :]
    me, own = lax.rem(where_ref[0], plan.pln), where_ref[0] // plan.pln
    depth = plan.area
    all_groups = plan.orb * plan.groups
    owner = lane_owner((1, grid), box)
    for group in range(all_groups):
        tile = recv_ref[group, depth : depth + 2 * SUB, :].astype(F32).astype(jnp.int32)
        table_ref[2 * group : 2 * group + 2, :] = tile[:2]
    copy = pltpu.make_async_copy(table_ref, corner_ref, sem)
    copy.start()
    field_ref[...] = jnp.zeros_like(field_ref)
    forward_y, forward_z = forward_y_ref[...], forward_z_ref[...]
    inverse_y, inverse_z = inverse_y_ref[...], inverse_z_ref[...]
    copy.wait()

    def start(group, n):
        return pl.multiple_of(corner_ref[2 * group + 1, box * n] * slots, SUB)

    def place(group, carry):
        values = recv_ref[group, :depth, :].astype(F32)
        for n in range(count):
            shift = lax.rem(corner_ref[2 * group, box * n] - box * n + grid, grid)
            moved = pltpu.roll(jnp.where(owner == n, values, 0.0), shift, 1)
            field_ref[pl.ds(start(group, n), depth), :] += moved
        return carry

    lax.fori_loop(0, all_groups, place, 0)
    row = iota((grid, 1), 0)
    edge_row = lax.rem(me, half) * plan.ky_block
    edges = edge_refs[0][0]
    for ref in edge_refs[1:]:
        edges = edges + ref[0]
    for pair in range(slots // 2):
        both = (2 * pair, 2 * pair + 1)
        planes = jnp.concatenate([field_ref[pl.ds(s, grid, stride=slots), :] for s in both], axis=1)
        planes = planes.astype(BF16)
        modes = dot(forward_y, jnp.concatenate([planes, planes], axis=0)).astype(BF16)
        back = []
        for side, s in enumerate(both):
            spectrum = jnp.concatenate([ref[pl.ds(s, plan.ky_block, stride=slots), :] for ref in piece_refs], axis=0)
            other = jnp.where(row == edge_row, edges[s : s + 1], spectrum)
            spectrum = jnp.concatenate([spectrum, other], axis=0)
            mine = modes[:, grid * side : grid * (side + 1)]
            mine = dot(jnp.concatenate([mine, mine], axis=1), forward_z)
            mine = mine * jnp.concatenate([spectrum, spectrum], axis=1)
            back.append(dot(terms_of(mine, 1), inverse_z))
        planes = dot(inverse_y, terms_of(jnp.concatenate(back, axis=1), 0))
        for side, s in enumerate(both):
            result_ref[pl.ds(s, grid, stride=slots), :] = planes[:, grid * side : grid * (side + 1)]

    def cut(d, group, carry):
        number = (own ^ d) * plan.groups + group
        values = jnp.zeros((depth, grid), F32)
        for n in range(count):
            shift = lax.rem(box * n - corner_ref[2 * number, box * n] + grid, grid)
            rows = result_ref[pl.ds(start(number, n), depth), :]
            values = jnp.where(owner == n, pltpu.roll(rows, shift, 1), values)
        send_refs[d][group] = values.astype(BF16)
        return carry

    for d in range(plan.orb):
        if plan.groups == 1:
            cut(d, 0, 0)
        else:
            lax.fori_loop(0, plan.groups, functools.partial(cut, d), 0)


def terms_kernel(plan, where_ref, *refs):
    box, grid, count, slots, pln = plan.box, plan.grid, plan.per_group, plan.slots, plan.pln
    recv_refs = refs[: plan.orb]
    psi_any, wave_ref, inner_ref, outer_ref, back_ref, *refs = refs[plan.orb :]
    out_refs = refs[:pln]
    psi_ref, stage_ref, own_ref, sem = refs[pln:]
    group = pl.program_id(0)
    copy = pltpu.make_async_copy(psi_any.at[group], psi_ref, sem)
    copy.start()
    owner = lane_owner((1, grid), box)
    own = where_ref[0] // pln
    rows = [wave_ref[0, pl.ds(pl.multiple_of((own ^ d) * slots, SUB), slots), :] for d in range(plan.orb)]
    wave = jnp.concatenate(split(jnp.concatenate(rows, axis=0).T), axis=1)
    inner, outer, back = inner_ref[...], outer_ref[...], back_ref[...]
    copy.wait()
    for pair in range(box // 2):
        tiles = [ref[0, 2 * slots * pair : 2 * slots * (pair + 1), :].astype(F32) for ref in recv_refs]
        columns = [jnp.concatenate([t[slots * side : slots * (side + 1)] for t in tiles], axis=0) for side in range(2)]
        both = jnp.concatenate(columns, axis=1).astype(BF16)
        out = dot(wave, jnp.concatenate([both, both], axis=0))
        for side, b in enumerate((2 * pair, 2 * pair + 1)):
            mine = out[:, grid * side : grid * (side + 1)]
            potential = jnp.zeros((box, grid), F32)
            for n in range(count):
                potential = jnp.where(owner == n, mine[box * n : box * (n + 1)], potential)
            stage_ref[b] = potential * psi_ref[b]
    span = SUB * box
    second = []
    for t in range(box // SUB):
        values = stage_ref[SUB * t : SUB * (t + 1)].reshape(span, grid)
        second.append(dot(inner, terms_of(values, 0)))
    second = jnp.concatenate(second, axis=0).reshape(box, box // SUB, SUB, grid)
    for t in range(box // SUB):
        values = dot(outer, terms_of(second[:, t].reshape(span, grid), 0))
        stage_ref[:, SUB * t : SUB * (t + 1), :] = values.reshape(box, SUB, grid)
    values = terms_of(stage_ref[...].reshape(box * box, grid), 1)
    out = dot(back, values, ((1,), (1,)))
    part = plan.box_part * count
    for p in range(pln):
        own_ref[p] = out[part * p : part * (p + 1)]
    me = lax.rem(where_ref[0], pln)
    out_refs[0][0] = own_ref[me]
    for step in range(1, pln):
        out_refs[step][0] = own_ref[lax.rem(me + step, pln)].astype(BF16)


def sum_kernel(plan, *refs):
    out_ref = refs[plan.pln]
    total = refs[0][0]
    for ref in refs[1 : plan.pln]:
        total = total + ref[0].astype(F32)
    section = plan.box * plan.box
    count = plan.per_group
    for j in range(plan.box_part):
        out_ref[0, :, section * j : section * (j + 1)] = total[count * j : count * (j + 1)].astype(out_ref.dtype)


def per_device(plan, orbitals, occupations, box_offsets, kernel_spectrum):
    orb, pln, half, slots = plan.orb, plan.pln, plan.half, plan.slots
    groups, count, box, grid = plan.groups, plan.per_group, plan.box, plan.grid
    plane_index = lax.axis_index("pln")
    where = (lax.axis_index("orb") * pln + plane_index).astype(jnp.int32)[None]
    smem = pl.BlockSpec(memory_space=pltpu.SMEM)
    anywhere = pl.BlockSpec(memory_space=pl.ANY)
    vmem = pl.BlockSpec(memory_space=pltpu.VMEM)
    dma = pltpu.SemaphoreType.DMA
    coefs = orbitals.reshape(groups, count, orbitals.shape[1])
    by_ky = jnp.transpose(kernel_spectrum, (1, 2, 0))
    area = plan.area
    padded = area + 2 * SUB
    tables = [plan.depth, plan.inner, plan.outer]
    piece = jax.ShapeDtypeStruct((plan.ky_block, slots, grid), F32)
    edge = jax.ShapeDtypeStruct((1, slots, grid), F32)
    send, psi, wave, *pieces = pl.pallas_call(
        functools.partial(density_kernel, plan),
        in_specs=[smem, smem, smem] + [anywhere] * 6,
        out_specs=[anywhere] * (3 + 2 * half),
        out_shape=[
            jax.ShapeDtypeStruct((orb, groups, padded, grid), BF16),
            jax.ShapeDtypeStruct((groups, box, box, grid), F32),
            jax.ShapeDtypeStruct((groups, plan.rows, grid), F32),
            *[piece] * half,
            *[edge] * half,
        ],
        scratch_shapes=[
            pltpu.VMEM(coefs.shape, BF16),
            *[pltpu.VMEM(t.shape, t.dtype) for t in tables],
            pltpu.VMEM((plan.rows, grid), F32),
            pltpu.VMEM((plan.rows, grid), F32),
            pltpu.VMEM((grid, box * box), F32),
            pltpu.VMEM((box, box, grid), F32),
            pltpu.VMEM((orb, padded, grid), BF16),
            pltpu.VMEM((half, plan.ky_block, slots, plan.doubled), F32),
            pltpu.VMEM((half, slots, plan.doubled), F32),
            pltpu.VMEM((half, plan.ky_block, slots, grid), F32),
            pltpu.VMEM((half, slots, grid), F32),
            dma((2 * half,)),
            dma((2 * half,)),
            dma((12,)),
        ],
        compiler_params=pltpu.CompilerParams(vmem_limit_bytes=LARGE),
        name="density",
    )(where, box_offsets, occupations, coefs, *tables, plan.wave, by_ky)
    received = lax.all_to_all(send, "orb", split_axis=0, concat_axis=0, tiled=True)
    received = received.reshape(orb * groups, padded, grid)
    for step in range(1, half):
        pairs = [(g * half + i, g * half + (i + step) % half) for g in range(2) for i in range(half)]
        pieces[step] = lax.ppermute(pieces[step], "pln", pairs)
    for step in range(half):
        pieces[half + step] = lax.ppermute(pieces[half + step], "pln", [(0, half + step), (half, step)])
    pieces[:half] = [p.reshape(plan.ky_block * slots, grid) for p in pieces[:half]]

    small = pltpu.CompilerParams(vmem_limit_bytes=SMALL)
    span = SUB * box
    shapes = [(plan.doubled, 2 * grid), (2 * grid, plan.doubled), (grid, 3 * plan.doubled), (3 * plan.doubled, grid)]
    shapes += [(span, 3 * span), (span, 3 * span), (grid, 3 * grid)]
    tables = pl.pallas_call(
        functools.partial(tables_kernel, plan),
        in_specs=[smem, anywhere],
        out_specs=[vmem] * (len(shapes) + 1),
        out_shape=[*[jax.ShapeDtypeStruct(shape, BF16) for shape in shapes], jax.ShapeDtypeStruct(pieces[0].shape, F32)],
        scratch_shapes=[dma((1,))],
        compiler_params=small,
        name="tables",
    )(where, pieces[0])
    pieces[0] = tables[7]
    send = pl.pallas_call(
        functools.partial(solve_kernel, plan),
        in_specs=[smem] + [vmem] * (5 + 2 * half),
        out_specs=[vmem] * orb,
        out_shape=[jax.ShapeDtypeStruct((groups, area, grid), BF16)] * orb,
        scratch_shapes=[
            pltpu.VMEM((grid * slots, grid), F32),
            pltpu.VMEM((grid * slots, grid), F32),
            pltpu.VMEM((2 * orb * groups, grid), jnp.int32),
            pltpu.SMEM((2 * orb * groups, grid), jnp.int32),
            dma,
        ],
        compiler_params=small,
        name="solve",
    )(where, received, *pieces, *tables[:4])
    received = [send[0]] + [None] * (orb - 1)
    for d in reversed(range(1, orb)):
        received[d] = lax.ppermute(send[d], "orb", [(o, o ^ d) for o in range(orb)])
    part = plan.box_part * count
    finished = pl.pallas_call(
        functools.partial(terms_kernel, plan),
        grid=(groups,),
        in_specs=[
            smem,
            *[pl.BlockSpec((1, area, grid), lambda g: (g, 0, 0))] * orb,
            anywhere,
            pl.BlockSpec((1, plan.rows, grid), lambda g: (g, 0, 0)),
            vmem,
            vmem,
            vmem,
        ],
        out_specs=[pl.BlockSpec((1, part, box * box), lambda g: (g, 0, 0))] * pln,
        out_shape=[jax.ShapeDtypeStruct((groups, part, box * box), BF16 if step else F32) for step in range(pln)],
        scratch_shapes=[
            pltpu.VMEM((box, box, grid), F32),
            pltpu.VMEM((box, box, grid), F32),
            pltpu.VMEM((pln, part, box * box), F32),
            dma,
        ],
        compiler_params=small,
        name="terms",
    )(where, *received, psi, wave, *tables[4:7])
    finished = list(finished)
    for step in range(1, pln):
        finished[step] = lax.ppermute(finished[step], "pln", [(p, (p + step) % pln) for p in range(pln)])
    cells = plan.box_part * box * box
    result = pl.pallas_call(
        functools.partial(sum_kernel, plan),
        grid=(groups,),
        in_specs=[pl.BlockSpec((1, part, box * box), lambda g: (g, 0, 0))] * pln,
        out_specs=pl.BlockSpec((1, count, cells), lambda g: (g, 0, 0)),
        out_shape=jax.ShapeDtypeStruct((groups, count, cells), BF16),
        compiler_params=small,
        name="sum",
    )(*finished)
    return result.reshape(groups * count, cells)


def solution(mesh):
    in_specs = (P("orb", None), P("orb"), P("orb", None), P(None, "pln", "orb"))
    out_specs = P("orb", "pln")

    def whole(orbitals, occupations, box_offsets, kernel_spectrum):
        plan = Plan(mesh, orbitals.shape, kernel_spectrum.shape)
        return jax.shard_map(
            functools.partial(per_device, plan), mesh=mesh, in_specs=in_specs, out_specs=out_specs, check_vma=False
        )(orbitals, occupations, box_offsets, kernel_spectrum)

    return whole
```

```python
import functools
import math

import jax
import jax.numpy as jnp
import numpy as np
from jax import lax
from jax.experimental import pallas as pl
from jax.experimental.pallas import tpu as pltpu
from jax.sharding import PartitionSpec as P

MAGIC_TAPS = (
    8.433424733352934e-07,
    -1.290557201342061e-05,
    8.76298447621056e-05,
    -0.00030158038132690465,
    0.001747237136729939,
    -0.009420470302010804,
    0.023738214637249424,
    0.0612625895831208,
    0.9940415697834004,
    -0.06048952891969835,
    -0.021030251609303816,
    0.013372634148547948,
    -0.0034412814449349387,
    0.0004944322768868992,
    -5.185986881173433e-05,
    2.7273449291197967e-06,
)
F32 = jnp.float32
BF16 = jnp.bfloat16
SUB = 8
LARGE = 60 * 1024 * 1024
SMALL = 32 * 1024 * 1024


def magic_filter(box):
    table = np.zeros((box, box))
    for row in range(box):
        for tap in range(-8, 8):
            if 0 <= row + tap < box:
                table[row, row + tap] = MAGIC_TAPS[tap + 8]
    return table.astype(np.float32).astype(np.float64)


def cas(product, doubled):
    angle = 2.0 * math.pi * (product % doubled) / doubled
    return np.cos(angle) + np.sin(angle)


def halves(table):
    high = np.asarray(table, np.float32).astype(jnp.bfloat16)
    low = (np.asarray(table, np.float64) - high.astype(np.float64)).astype(jnp.bfloat16)
    return high, low


def split(values):
    high = values.astype(BF16)
    low = (values - high.astype(F32)).astype(BF16)
    return high, low


def dot(left, right, dims=((1,), (0,))):
    return lax.dot_general(left, right, (dims, ((), ())), preferred_element_type=F32)


def terms_of(values, axis):
    high, low = split(values)
    return jnp.concatenate([high, high, low], axis=axis)


def stacked(table, axis):
    high, low = halves(table)
    return np.concatenate([high, low, high], axis=axis)


SINE = (1.0, -1.0 / 6, 1.0 / 120, -1.0 / 5040, 1.0 / 362880)
COSINE = (1.0, -1.0 / 2, 1.0 / 24, -1.0 / 720, 1.0 / 40320)


def turn(steps, doubled):
    quarter = doubled // 4
    place = (steps + quarter // 2) & (doubled - 1)
    quadrant = place // quarter
    angle = (place - quadrant * quarter - quarter // 2).astype(F32) * (2.0 * math.pi / doubled)
    square = angle * angle
    cosine, sine = COSINE[-1], SINE[-1]
    for even, odd in zip(COSINE[-2::-1], SINE[-2::-1]):
        cosine, sine = cosine * square + even, sine * square + odd
    return quadrant, cosine, sine * angle


def cosine_table(steps, doubled):
    quadrant, cosine, sine = turn(steps, doubled)
    value = jnp.where((quadrant & 1) == 0, cosine, -sine)
    return jnp.where(quadrant < 2, value, -value)


def cas_table(steps, doubled):
    quadrant, cosine, sine = turn(steps, doubled)
    value = jnp.where((quadrant & 1) == 0, cosine + sine, cosine - sine)
    return jnp.where(quadrant < 2, value, -value)


def iota(shape, axis):
    return lax.broadcasted_iota(jnp.int32, shape, axis)


def stack_terms(table, axis):
    high, low = split(table)
    return jnp.concatenate([high, low, high], axis=axis)


def tap_table(step):
    value = jnp.zeros(step.shape, F32)
    for tap in range(-8, 8):
        value = jnp.where(step == tap, np.float32(MAGIC_TAPS[tap + 8]), value)
    return value


def inner_back_table(box):
    span = SUB * box
    one = tap_table(iota((box, span), 0) - (iota((box, span), 1) & (box - 1)))
    whole = jnp.concatenate([one] * SUB, axis=0)
    return jnp.where(iota((span, span), 0) // box == iota((span, span), 1) // box, whole, 0.0)


def outer_back_table(box):
    span = SUB * box
    row, column = iota((span, span), 0), iota((span, span), 1)
    value = tap_table(row // SUB - column // SUB)
    return jnp.where((row & (SUB - 1)) == (column & (SUB - 1)), value, 0.0)


def depth_back_table(plan):
    grid, box, count = plan.grid, plan.box, plan.per_group
    row, column = iota((grid, grid), 0), iota((grid, grid), 1)
    value = tap_table(row // count - (column & (box - 1)))
    return jnp.where((row & (count - 1)) == column // box, value, 0.0)


def mode_table(plan, me, shape, axis):
    grid, doubled, half = plan.grid, plan.doubled, plan.half
    line = tuple(doubled if dim == axis else 1 for dim in range(2))
    group, index = me // half, lax.rem(me, half)
    mode = iota(line, axis)
    within = mode & (grid - 1)
    block = (index - within // plan.ky_block + half) & (half - 1)
    step = block * plan.ky_block + (within & (plan.ky_block - 1))
    edge = (mode >= grid) & (step == 0)
    frequency = jnp.where(edge, ((1 - group) * grid), group * grid + step)
    quarter = jnp.where((mode >= grid) & (step != 0), doubled // 4, 0)
    weight = jnp.where(step == 0, 1.0, 2.0)
    return cosine_table(frequency * iota(shape, 1 - axis) - quarter, doubled), weight


def depth_mode_table(plan, shape, axis):
    grid, doubled = plan.grid, plan.doubled
    place = iota(shape, axis)
    frequency = jnp.where(place < grid, place, grid - place)
    return jnp.where(place == grid, 0.0, cas_table(frequency * iota(shape, 1 - axis), doubled))


def side_by_side(table, parts):
    results = []
    for first, second in zip(parts[::2], parts[1::2]):
        width = first.shape[1]
        out = dot(table, terms_of(jnp.concatenate([first, second], axis=1), 0))
        results += [out[:, :width], out[:, width:]]
    return results


class Plan:
    def __init__(self, mesh, orbital_shape, kernel_shape):
        self.orb = mesh.shape["orb"]
        self.pln = mesh.shape["pln"]
        self.doubled = doubled = kernel_shape[0]
        self.grid = grid = doubled // 2
        self.box = box = round(orbital_shape[1] ** (1 / 3))
        self.per_group = grid // box
        self.groups = orbital_shape[0] // self.orb // self.per_group
        self.ky_block = kernel_shape[1] // self.pln
        self.kx_block = kernel_shape[2] // self.orb
        self.slots = SUB * -(-self.kx_block // (SUB * self.pln))
        self.half = self.pln // 2
        self.rows = self.orb * self.slots
        self.area = box * self.slots
        self.box_part = box // self.pln
        magic = magic_filter(box)
        eye = np.eye(SUB)
        depth = np.zeros((box, self.per_group, self.per_group, box))
        for n in range(self.per_group):
            depth[:, n, n, :] = magic.T
        depth = depth.reshape(grid, grid)
        self.depth = np.concatenate(halves(depth), axis=0)
        self.inner = stacked(np.kron(eye, magic), 1)
        self.outer = stacked(np.kron(magic, eye), 1)
        places = np.arange(grid)
        wave = np.zeros((self.pln, self.orb, self.slots, grid))
        for p in range(self.pln):
            for s in range(self.slots):
                within = p * self.slots + s
                if within < self.kx_block:
                    k = self.kx_block * np.arange(self.orb) + within
                    wave[p, :, s, :] = cas(k[:, None] * places[None, :], doubled)
        self.wave = wave.reshape(self.pln, self.rows, grid).astype(np.float32)
        self.quarter = box // 4


def lane_owner(shape, box):
    return lax.broadcasted_iota(jnp.int32, shape, len(shape) - 1) // box


def start_copies(sems, first, *pairs):
    copies = []
    for number, (source, target) in enumerate(pairs):
        copy = pltpu.make_async_copy(source, target, sems.at[first + number])
        copy.start()
        copies.append(copy)
    return copies


def wait_copies(copies):
    for copy in copies:
        copy.wait()


def density_kernel(
    plan, where_ref, corner_ref, weight_ref, coef_any, depth_any, inner_any, outer_any, wave_any, spectrum_any,
    send_any, psi_any, wave_out_any, *refs,
):
    half = plan.half
    piece_anys = refs[: 2 * half]
    coef_ref, depth_ref, inner_ref, outer_ref, wave_ref, own_wave_ref, stage_ref, psi_ref, send_ref = refs[2 * half : -7]
    block_ref, edge_ref, block_out_ref, edge_out_ref, spectrum_sems, out_sems, sems = refs[-7:]
    box, grid, count, slots = plan.box, plan.grid, plan.per_group, plan.slots
    section = box * box
    span = SUB * box
    me = lax.rem(where_ref[0], plan.pln)
    coef_copy = pltpu.make_async_copy(coef_any, coef_ref, sems.at[0])
    coef_copy.start()
    fetched = start_copies(
        sems, 1, (depth_any, depth_ref), (inner_any, inner_ref), (outer_any, outer_ref), (wave_any.at[me], wave_ref)
    )
    spectrum = spectrum_copies(plan, me, spectrum_any, block_ref, edge_ref, spectrum_sems)
    for copy in spectrum:
        copy.start()
    owner = lane_owner((1, grid), box)
    coef_copy.wait()
    wait_copies(fetched)
    for group in range(plan.groups):
        for p in range(box):
            stage_ref[count * p : count * (p + 1), :] = coef_ref[group, :, section * p : section * (p + 1)].astype(F32)
        coef = stage_ref[...].astype(BF16)
        first = dot(jnp.concatenate([coef, coef], axis=0), depth_ref[...], ((0,), (0,)))
        inner, outer = inner_ref[...], outer_ref[...]
        second = side_by_side(inner, [first[span * t : span * (t + 1)] for t in range(box // SUB)])
        second = jnp.concatenate(second, axis=0).reshape(box, box // SUB, SUB, grid)
        third = side_by_side(outer, [second[:, t].reshape(span, grid) for t in range(box // SUB)])
        for t in range(box // SUB):
            psi_ref[:, SUB * t : SUB * (t + 1), :] = third[t].reshape(box, SUB, grid)
        sent = start_copies(sems, 5, (psi_ref, psi_any.at[group]))
        whole_wave = wave_ref[...]
        wave = jnp.zeros_like(whole_wave)
        weight = jnp.zeros((1, grid), F32)
        kind = iota((2 * SUB, 1), 0)
        corner = jnp.zeros((2 * SUB, grid), F32)
        for n in range(count):
            number = group * count + n
            shift = lax.rem(box * n - corner_ref[number, 2] + grid, grid)
            wave = jnp.where(owner == n, pltpu.roll(whole_wave, shift, 1), wave)
            weight = jnp.where(owner == n, weight_ref[number], weight)
            place = jnp.where(kind == 0, corner_ref[number, 0], corner_ref[number, 1])
            corner = jnp.where(owner == n, place.astype(F32), corner)
        own_wave_ref[...] = wave
        sent += start_copies(sems, 6, (own_wave_ref, wave_out_any.at[group]))
        for o in range(plan.orb):
            send_ref[o, plan.area :, :] = corner.astype(send_ref.dtype)
        high, low = split(wave)
        wave_terms = jnp.concatenate([high, low, high], axis=1)
        if group == 0:
            wait_copies(spectrum)
            folded = fold_spectrum(plan, piece_anys, block_ref, edge_ref, block_out_ref, edge_out_ref, out_sems)
        rows = pl.ds(plan.area, 2 * SUB)
        sent += start_copies(sems, 7, (send_ref.at[:, rows, :], send_any.at[:, group, rows, :]))
        per_part = plan.quarter // 2
        for pair in range(box // 2):
            columns = []
            for b in (2 * pair, 2 * pair + 1):
                psi = psi_ref[b]
                density = psi * psi * weight
                columns.append(jnp.concatenate([jnp.where(owner == n, density, 0.0) for n in range(count)], axis=0))
            out = dot(wave_terms, terms_of(jnp.concatenate(columns, axis=1), 0))
            for o in range(plan.orb):
                mine = out[slots * o : slots * (o + 1)]
                tile = jnp.concatenate([mine[:, :grid], mine[:, grid:]], axis=0)
                send_ref[o, 2 * slots * pair : 2 * slots * (pair + 1), :] = tile.astype(send_ref.dtype)
            if pair % per_part == per_part - 1:
                part = pair // per_part
                rows = pl.ds(plan.quarter * slots * part, plan.quarter * slots)
                sent += start_copies(sems, 8 + part, (send_ref.at[:, rows, :], send_any.at[:, group, rows, :]))
        wait_copies(sent)
    wait_copies(folded)


def spectrum_copies(plan, me, spectrum_any, block_ref, edge_ref, sems):
    half, slots = plan.half, plan.slots
    group, index = me // half, lax.rem(me, half)

    def fetch(target, source, buffer, number):
        first = jnp.minimum(target * slots, max(plan.kx_block - slots, 0))
        first = pl.multiple_of(first, SUB)
        return pltpu.make_async_copy(source.at[:, pl.ds(first, slots), :], buffer, sems.at[number])

    copies = []
    for step in range(half):
        copies.append(fetch(group * half + lax.rem(index + step, half), spectrum_any, block_ref.at[step], step))
    for step in range(half):
        target = (1 - group) * half + step
        copies.append(fetch(target, spectrum_any.at[pl.ds(0, 1)], edge_ref.at[pl.ds(step, 1)], half + step))
    return copies


def fold_spectrum(plan, piece_anys, block_ref, edge_ref, block_out_ref, edge_out_ref, sems):
    half, grid = plan.half, plan.grid
    odd = (iota((1, 1, grid), 2) & 1) == 1

    def fold(values):
        last = values[..., grid : grid + 1]
        return values[..., :grid] + jnp.where(odd, last, -last)

    for step in range(half):
        block_out_ref[step] = fold(block_ref[step])
    edge_out_ref[...] = fold(edge_ref[...])
    pairs = [(block_out_ref.at[step], piece_anys[step]) for step in range(half)]
    pairs += [(edge_out_ref.at[pl.ds(step, 1)], piece_anys[half + step]) for step in range(half)]
    return start_copies(sems, 0, *pairs)


def tables_kernel(plan, where_ref, piece_any, *refs):
    forward_y_ref, forward_z_ref, inverse_y_ref, inverse_z_ref, inner_ref, outer_ref, back_ref = refs[:7]
    piece_ref, sems = refs[7:]
    grid, doubled, me = plan.grid, plan.doubled, lax.rem(where_ref[0], plan.pln)
    copies = start_copies(sems, 0, (piece_any, piece_ref))
    forward, _ = mode_table(plan, me, (doubled, grid), 0)
    forward_y_ref[...] = jnp.concatenate(split(forward), axis=1)
    forward_z_ref[...] = jnp.concatenate(split(depth_mode_table(plan, (grid, doubled), 1)), axis=0)
    inverse, weight = mode_table(plan, me, (grid, doubled), 1)
    inverse_y_ref[...] = stack_terms(inverse * (weight * (1.0 / doubled**3)), 1)
    inverse_z_ref[...] = stack_terms(depth_mode_table(plan, (doubled, grid), 0), 0)
    inner_ref[...] = stack_terms(inner_back_table(plan.box), 1)
    outer_ref[...] = stack_terms(outer_back_table(plan.box), 1)
    back_ref[...] = stack_terms(depth_back_table(plan), 1)
    wait_copies(copies)


def solve_kernel(plan, where_ref, recv_ref, *refs):
    half, slots, grid, box, count = plan.half, plan.slots, plan.grid, plan.box, plan.per_group
    piece_refs, edge_refs = refs[:half], refs[half : 2 * half]
    forward_y_ref, forward_z_ref, inverse_y_ref, inverse_z_ref = refs[2 * half : 2 * half + 4]
    chips = plan.orb // 2
    own_ref, swap_ref, *send_refs = refs[2 * half + 4 : 2 * half + 5 + chips]
    field_ref, result_ref, table_ref, corner_ref, sem = refs[2 * half + 5 + chips :]
    me, own = lax.rem(where_ref[0], plan.pln), where_ref[0] // plan.pln
    depth = plan.area
    all_groups = plan.orb * plan.groups
    owner = lane_owner((1, grid), box)
    for group in range(all_groups):
        tile = recv_ref[group, depth : depth + 2 * SUB, :].astype(F32).astype(jnp.int32)
        table_ref[2 * group : 2 * group + 2, :] = tile[:2]
    copy = pltpu.make_async_copy(table_ref, corner_ref, sem)
    copy.start()
    field_ref[...] = jnp.zeros_like(field_ref)
    forward_y, forward_z = forward_y_ref[...], forward_z_ref[...]
    inverse_y, inverse_z = inverse_y_ref[...], inverse_z_ref[...]
    copy.wait()

    def start(group, n):
        return pl.multiple_of(corner_ref[2 * group + 1, box * n] * slots, SUB)

    def place(group, carry):
        values = recv_ref[group, :depth, :].astype(F32)
        for n in range(count):
            shift = lax.rem(corner_ref[2 * group, box * n] - box * n + grid, grid)
            moved = pltpu.roll(jnp.where(owner == n, values, 0.0), shift, 1)
            field_ref[pl.ds(start(group, n), depth), :] += moved
        return carry

    lax.fori_loop(0, all_groups, place, 0)
    row = iota((grid, 1), 0)
    edge_row = lax.rem(me, half) * plan.ky_block
    edges = edge_refs[0][0]
    for ref in edge_refs[1:]:
        edges = edges + ref[0]
    for pair in range(slots // 2):
        both = (2 * pair, 2 * pair + 1)
        planes = jnp.concatenate([field_ref[pl.ds(s, grid, stride=slots), :] for s in both], axis=1)
        planes = planes.astype(BF16)
        modes = dot(forward_y, jnp.concatenate([planes, planes], axis=0)).astype(BF16)
        back = []
        for side, s in enumerate(both):
            spectrum = jnp.concatenate([ref[pl.ds(s, plan.ky_block, stride=slots), :] for ref in piece_refs], axis=0)
            other = jnp.where(row == edge_row, edges[s : s + 1], spectrum)
            spectrum = jnp.concatenate([spectrum, other], axis=0)
            mine = modes[:, grid * side : grid * (side + 1)]
            mine = dot(jnp.concatenate([mine, mine], axis=1), forward_z)
            mine = mine * jnp.concatenate([spectrum, spectrum], axis=1)
            back.append(dot(terms_of(mine, 1), inverse_z))
        planes = dot(inverse_y, terms_of(jnp.concatenate(back, axis=1), 0))
        for side, s in enumerate(both):
            result_ref[pl.ds(s, grid, stride=slots), :] = planes[:, grid * side : grid * (side + 1)]

    def cut(d, group, carry):
        number = (own ^ d) * plan.groups + group
        values = jnp.zeros((depth, grid), F32)
        for n in range(count):
            shift = lax.rem(box * n - corner_ref[2 * number, box * n] + grid, grid)
            rows = result_ref[pl.ds(start(number, n), depth), :]
            values = jnp.where(owner == n, pltpu.roll(rows, shift, 1), values)
        if d < 2:
            (own_ref, swap_ref)[d][group] = values.astype(BF16)
        else:
            send_refs[d // 2 - 1][d % 2, group] = values.astype(BF16)
        return carry

    for d in range(plan.orb):
        if plan.groups == 1:
            cut(d, 0, 0)
        else:
            lax.fori_loop(0, plan.groups, functools.partial(cut, d), 0)


def gather_kernel(swap_ref, *refs):
    out_ref = refs[-1]
    out_ref[0] = swap_ref[...]
    for number, ref in enumerate(refs[:-1]):
        out_ref[number + 1] = ref[1]


def terms_kernel(plan, where_ref, *refs):
    box, grid, count, slots, pln = plan.box, plan.grid, plan.per_group, plan.slots, plan.pln
    chips = plan.orb // 2
    own_ref, other_ref, *chip_refs = refs[: chips + 1]
    psi_any, wave_ref, inner_ref, outer_ref, back_ref, *refs = refs[chips + 1 :]

    def tile(d, rows):
        if d % 2:
            return other_ref[d // 2, 0, rows]
        return chip_refs[d // 2 - 1][0, 0, rows] if d else own_ref[0, rows]

    out_refs = refs[:pln]
    psi_ref, stage_ref, result_ref, sem = refs[pln:]
    group = pl.program_id(0)
    copy = pltpu.make_async_copy(psi_any.at[group], psi_ref, sem)
    copy.start()
    owner = lane_owner((1, grid), box)
    own = where_ref[0] // pln
    rows = [wave_ref[0, pl.ds(pl.multiple_of((own ^ d) * slots, SUB), slots), :] for d in range(plan.orb)]
    wave = jnp.concatenate(split(jnp.concatenate(rows, axis=0).T), axis=1)
    inner, outer, back = inner_ref[...], outer_ref[...], back_ref[...]
    copy.wait()
    for pair in range(box // 2):
        tiles = [tile(d, pl.ds(2 * slots * pair, 2 * slots)).astype(F32) for d in range(plan.orb)]
        columns = [jnp.concatenate([t[slots * side : slots * (side + 1)] for t in tiles], axis=0) for side in range(2)]
        both = jnp.concatenate(columns, axis=1).astype(BF16)
        out = dot(wave, jnp.concatenate([both, both], axis=0))
        for side, b in enumerate((2 * pair, 2 * pair + 1)):
            mine = out[:, grid * side : grid * (side + 1)]
            potential = jnp.zeros((box, grid), F32)
            for n in range(count):
                potential = jnp.where(owner == n, mine[box * n : box * (n + 1)], potential)
            stage_ref[b] = potential * psi_ref[b]
    span = SUB * box
    second = side_by_side(inner, [stage_ref[SUB * t : SUB * (t + 1)].reshape(span, grid) for t in range(box // SUB)])
    second = jnp.concatenate(second, axis=0).reshape(box, box // SUB, SUB, grid)
    third = side_by_side(outer, [second[:, t].reshape(span, grid) for t in range(box // SUB)])
    for t in range(box // SUB):
        stage_ref[:, SUB * t : SUB * (t + 1), :] = third[t].reshape(box, SUB, grid)
    values = terms_of(stage_ref[...].reshape(box * box, grid), 1)
    out = dot(back, values, ((1,), (1,)))
    part = plan.box_part * count
    for p in range(pln):
        result_ref[p] = out[part * p : part * (p + 1)]
    me = lax.rem(where_ref[0], pln)
    out_refs[0][0] = result_ref[me]
    for step in range(1, pln):
        out_refs[step][0] = result_ref[lax.rem(me + step, pln)].astype(BF16)


def sum_kernel(plan, *refs):
    out_ref = refs[plan.pln]
    total = refs[0][0]
    for ref in refs[1 : plan.pln]:
        total = total + ref[0].astype(F32)
    section = plan.box * plan.box
    count = plan.per_group
    for j in range(plan.box_part):
        out_ref[0, :, section * j : section * (j + 1)] = total[count * j : count * (j + 1)].astype(out_ref.dtype)


def per_device(plan, orbitals, occupations, box_offsets, kernel_spectrum):
    orb, pln, half, slots = plan.orb, plan.pln, plan.half, plan.slots
    groups, count, box, grid = plan.groups, plan.per_group, plan.box, plan.grid
    plane_index = lax.axis_index("pln")
    where = (lax.axis_index("orb") * pln + plane_index).astype(jnp.int32)[None]
    smem = pl.BlockSpec(memory_space=pltpu.SMEM)
    anywhere = pl.BlockSpec(memory_space=pl.ANY)
    vmem = pl.BlockSpec(memory_space=pltpu.VMEM)
    dma = pltpu.SemaphoreType.DMA
    coefs = orbitals.reshape(groups, count, orbitals.shape[1])
    by_ky = jnp.transpose(kernel_spectrum, (1, 2, 0))
    area = plan.area
    padded = area + 2 * SUB
    tables = [plan.depth, plan.inner, plan.outer]
    piece = jax.ShapeDtypeStruct((plan.ky_block, slots, grid), F32)
    edge = jax.ShapeDtypeStruct((1, slots, grid), F32)
    send, psi, wave, *pieces = pl.pallas_call(
        functools.partial(density_kernel, plan),
        in_specs=[smem, smem, smem] + [anywhere] * 6,
        out_specs=[anywhere] * (3 + 2 * half),
        out_shape=[
            jax.ShapeDtypeStruct((orb, groups, padded, grid), BF16),
            jax.ShapeDtypeStruct((groups, box, box, grid), F32),
            jax.ShapeDtypeStruct((groups, plan.rows, grid), F32),
            *[piece] * half,
            *[edge] * half,
        ],
        scratch_shapes=[
            pltpu.VMEM(coefs.shape, BF16),
            *[pltpu.VMEM(t.shape, t.dtype) for t in tables],
            pltpu.VMEM((plan.rows, grid), F32),
            pltpu.VMEM((plan.rows, grid), F32),
            pltpu.VMEM((grid, box * box), F32),
            pltpu.VMEM((box, box, grid), F32),
            pltpu.VMEM((orb, padded, grid), BF16),
            pltpu.VMEM((half, plan.ky_block, slots, plan.doubled), F32),
            pltpu.VMEM((half, slots, plan.doubled), F32),
            pltpu.VMEM((half, plan.ky_block, slots, grid), F32),
            pltpu.VMEM((half, slots, grid), F32),
            dma((2 * half,)),
            dma((2 * half,)),
            dma((12,)),
        ],
        compiler_params=pltpu.CompilerParams(vmem_limit_bytes=LARGE),
        name="density",
    )(where, box_offsets, occupations, coefs, *tables, plan.wave, by_ky)
    received = lax.all_to_all(send, "orb", split_axis=0, concat_axis=0, tiled=True)
    received = received.reshape(orb * groups, padded, grid)
    for step in range(1, half):
        pairs = [(g * half + i, g * half + (i + step) % half) for g in range(2) for i in range(half)]
        pieces[step] = lax.ppermute(pieces[step], "pln", pairs)
    for step in range(half):
        pieces[half + step] = lax.ppermute(pieces[half + step], "pln", [(0, half + step), (half, step)])
    pieces[:half] = [p.reshape(plan.ky_block * slots, grid) for p in pieces[:half]]

    small = pltpu.CompilerParams(vmem_limit_bytes=SMALL)
    span = SUB * box
    shapes = [(plan.doubled, 2 * grid), (2 * grid, plan.doubled), (grid, 3 * plan.doubled), (3 * plan.doubled, grid)]
    shapes += [(span, 3 * span), (span, 3 * span), (grid, 3 * grid)]
    tables = pl.pallas_call(
        functools.partial(tables_kernel, plan),
        in_specs=[smem, anywhere],
        out_specs=[vmem] * (len(shapes) + 1),
        out_shape=[*[jax.ShapeDtypeStruct(shape, BF16) for shape in shapes], jax.ShapeDtypeStruct(pieces[0].shape, F32)],
        scratch_shapes=[dma((1,))],
        compiler_params=small,
        name="tables",
    )(where, pieces[0])
    pieces[0] = tables[7]
    chips = orb // 2
    single = jax.ShapeDtypeStruct((groups, area, grid), BF16)
    send = pl.pallas_call(
        functools.partial(solve_kernel, plan),
        in_specs=[smem] + [vmem] * (5 + 2 * half),
        out_specs=[vmem] * (1 + chips),
        out_shape=[single] * 2 + [jax.ShapeDtypeStruct((2, groups, area, grid), BF16)] * (chips - 1),
        scratch_shapes=[
            pltpu.VMEM((grid * slots, grid), F32),
            pltpu.VMEM((grid * slots, grid), F32),
            pltpu.VMEM((2 * orb * groups, grid), jnp.int32),
            pltpu.SMEM((2 * orb * groups, grid), jnp.int32),
            dma,
        ],
        compiler_params=small,
        name="solve",
    )(where, received, *pieces, *tables[:4])
    own, swap, *send = send
    core_pairs = [(o, o ^ 1) for o in range(orb)]
    arrived = [None] * (chips - 1)
    for e in reversed(range(1, chips)):
        arrived[e - 1] = lax.ppermute(send[e - 1], "orb", [(o, o ^ (2 * e)) for o in range(orb)])
    gathered = pl.pallas_call(
        gather_kernel,
        in_specs=[vmem] * chips,
        out_specs=vmem,
        out_shape=jax.ShapeDtypeStruct((chips, groups, area, grid), BF16),
        compiler_params=small,
        name="gather",
    )(swap, *arrived)
    other = lax.ppermute(gathered, "orb", core_pairs)
    part = plan.box_part * count
    finished = pl.pallas_call(
        functools.partial(terms_kernel, plan),
        grid=(groups,),
        in_specs=[
            smem,
            pl.BlockSpec((1, area, grid), lambda g: (g, 0, 0)),
            pl.BlockSpec((chips, 1, area, grid), lambda g: (0, g, 0, 0)),
            *[pl.BlockSpec((1, 1, area, grid), lambda g: (0, g, 0, 0))] * (chips - 1),
            anywhere,
            pl.BlockSpec((1, plan.rows, grid), lambda g: (g, 0, 0)),
            vmem,
            vmem,
            vmem,
        ],
        out_specs=[pl.BlockSpec((1, part, box * box), lambda g: (g, 0, 0))] * pln,
        out_shape=[jax.ShapeDtypeStruct((groups, part, box * box), BF16 if step else F32) for step in range(pln)],
        scratch_shapes=[
            pltpu.VMEM((box, box, grid), F32),
            pltpu.VMEM((box, box, grid), F32),
            pltpu.VMEM((pln, part, box * box), F32),
            dma,
        ],
        compiler_params=small,
        name="terms",
    )(where, own, other, *arrived, psi, wave, *tables[4:7])
    finished = list(finished)
    for step in range(1, pln):
        finished[step] = lax.ppermute(finished[step], "pln", [(p, (p + step) % pln) for p in range(pln)])
    cells = plan.box_part * box * box
    result = pl.pallas_call(
        functools.partial(sum_kernel, plan),
        grid=(groups,),
        in_specs=[pl.BlockSpec((1, part, box * box), lambda g: (g, 0, 0))] * pln,
        out_specs=pl.BlockSpec((1, count, cells), lambda g: (g, 0, 0)),
        out_shape=jax.ShapeDtypeStruct((groups, count, cells), BF16),
        compiler_params=small,
        name="sum",
    )(*finished)
    return result.reshape(groups * count, cells)


def solution(mesh):
    in_specs = (P("orb", None), P("orb"), P("orb", None), P(None, "pln", "orb"))
    out_specs = P("orb", "pln")

    def whole(orbitals, occupations, box_offsets, kernel_spectrum):
        plan = Plan(mesh, orbitals.shape, kernel_spectrum.shape)
        return jax.shard_map(
            functools.partial(per_device, plan), mesh=mesh, in_specs=in_specs, out_specs=out_specs, check_vma=False
        )(orbitals, occupations, box_offsets, kernel_spectrum)

    return whole
```

```python
import functools
import math

import jax
import jax.numpy as jnp
import numpy as np
from jax import lax
from jax.experimental import pallas as pl
from jax.experimental.pallas import tpu as pltpu
from jax.sharding import PartitionSpec as P

MAGIC_TAPS = (
    8.433424733352934e-07,
    -1.290557201342061e-05,
    8.76298447621056e-05,
    -0.00030158038132690465,
    0.001747237136729939,
    -0.009420470302010804,
    0.023738214637249424,
    0.0612625895831208,
    0.9940415697834004,
    -0.06048952891969835,
    -0.021030251609303816,
    0.013372634148547948,
    -0.0034412814449349387,
    0.0004944322768868992,
    -5.185986881173433e-05,
    2.7273449291197967e-06,
)
F32 = jnp.float32
BF16 = jnp.bfloat16
SUB = 8
LARGE = 60 * 1024 * 1024
SMALL = 32 * 1024 * 1024


def magic_filter(box):
    table = np.zeros((box, box))
    for row in range(box):
        for tap in range(-8, 8):
            if 0 <= row + tap < box:
                table[row, row + tap] = MAGIC_TAPS[tap + 8]
    return table.astype(np.float32).astype(np.float64)


def cas(product, doubled):
    angle = 2.0 * math.pi * (product % doubled) / doubled
    return np.cos(angle) + np.sin(angle)


def halves(table):
    high = np.asarray(table, np.float32).astype(jnp.bfloat16)
    low = (np.asarray(table, np.float64) - high.astype(np.float64)).astype(jnp.bfloat16)
    return high, low


def split(values):
    high = values.astype(BF16)
    low = (values - high.astype(F32)).astype(BF16)
    return high, low


def dot(left, right, dims=((1,), (0,))):
    return lax.dot_general(left, right, (dims, ((), ())), preferred_element_type=F32)


def terms_of(values, axis):
    high, low = split(values)
    return jnp.concatenate([high, high, low], axis=axis)


def stacked(table, axis):
    high, low = halves(table)
    return np.concatenate([high, low, high], axis=axis)


SINE = (1.0, -1.0 / 6, 1.0 / 120, -1.0 / 5040, 1.0 / 362880)
COSINE = (1.0, -1.0 / 2, 1.0 / 24, -1.0 / 720, 1.0 / 40320)


def turn(steps, doubled):
    quarter = doubled // 4
    place = (steps + quarter // 2) & (doubled - 1)
    quadrant = place // quarter
    angle = (place - quadrant * quarter - quarter // 2).astype(F32) * (2.0 * math.pi / doubled)
    square = angle * angle
    cosine, sine = COSINE[-1], SINE[-1]
    for even, odd in zip(COSINE[-2::-1], SINE[-2::-1]):
        cosine, sine = cosine * square + even, sine * square + odd
    return quadrant, cosine, sine * angle


def cosine_table(steps, doubled):
    quadrant, cosine, sine = turn(steps, doubled)
    value = jnp.where((quadrant & 1) == 0, cosine, -sine)
    return jnp.where(quadrant < 2, value, -value)


def cas_table(steps, doubled):
    quadrant, cosine, sine = turn(steps, doubled)
    value = jnp.where((quadrant & 1) == 0, cosine + sine, cosine - sine)
    return jnp.where(quadrant < 2, value, -value)


def iota(shape, axis):
    return lax.broadcasted_iota(jnp.int32, shape, axis)


def stack_terms(table, axis):
    high, low = split(table)
    return jnp.concatenate([high, low, high], axis=axis)


def tap_table(step):
    value = jnp.zeros(step.shape, F32)
    for tap in range(-8, 8):
        value = jnp.where(step == tap, np.float32(MAGIC_TAPS[tap + 8]), value)
    return value


def inner_back_table(box):
    span = SUB * box
    one = tap_table(iota((box, span), 0) - (iota((box, span), 1) & (box - 1)))
    whole = jnp.concatenate([one] * SUB, axis=0)
    return jnp.where(iota((span, span), 0) // box == iota((span, span), 1) // box, whole, 0.0)


def outer_back_table(box):
    span = SUB * box
    row, column = iota((span, span), 0), iota((span, span), 1)
    value = tap_table(row // SUB - column // SUB)
    return jnp.where((row & (SUB - 1)) == (column & (SUB - 1)), value, 0.0)


def depth_back_table(plan):
    grid, box, count = plan.grid, plan.box, plan.per_group
    row, column = iota((grid, grid), 0), iota((grid, grid), 1)
    value = tap_table(row // count - (column & (box - 1)))
    return jnp.where((row & (count - 1)) == column // box, value, 0.0)


def mode_table(plan, me, shape, axis):
    grid, doubled, half = plan.grid, plan.doubled, plan.half
    line = tuple(doubled if dim == axis else 1 for dim in range(2))
    group, index = me // half, lax.rem(me, half)
    mode = iota(line, axis)
    within = mode & (grid - 1)
    block = (index - within // plan.ky_block + half) & (half - 1)
    step = block * plan.ky_block + (within & (plan.ky_block - 1))
    edge = (mode >= grid) & (step == 0)
    frequency = jnp.where(edge, ((1 - group) * grid), group * grid + step)
    quarter = jnp.where((mode >= grid) & (step != 0), doubled // 4, 0)
    weight = jnp.where(step == 0, 1.0, 2.0)
    return cosine_table(frequency * iota(shape, 1 - axis) - quarter, doubled), weight


def depth_mode_table(plan, shape, axis):
    grid, doubled = plan.grid, plan.doubled
    place = iota(shape, axis)
    frequency = jnp.where(place < grid, place, grid - place)
    return jnp.where(place == grid, 0.0, cas_table(frequency * iota(shape, 1 - axis), doubled))


def side_by_side(table, parts):
    results = []
    for first, second in zip(parts[::2], parts[1::2]):
        width = first.shape[1]
        out = dot(table, terms_of(jnp.concatenate([first, second], axis=1), 0))
        results += [out[:, :width], out[:, width:]]
    return results


class Plan:
    def __init__(self, mesh, orbital_shape, kernel_shape):
        self.orb = mesh.shape["orb"]
        self.pln = mesh.shape["pln"]
        self.doubled = doubled = kernel_shape[0]
        self.grid = grid = doubled // 2
        self.box = box = round(orbital_shape[1] ** (1 / 3))
        self.per_group = grid // box
        self.groups = orbital_shape[0] // self.orb // self.per_group
        self.ky_block = kernel_shape[1] // self.pln
        self.kx_block = kernel_shape[2] // self.orb
        self.slots = SUB * -(-self.kx_block // (SUB * self.pln))
        self.half = self.pln // 2
        self.rows = self.orb * self.slots
        self.area = box * self.slots
        self.box_part = box // self.pln
        magic = magic_filter(box)
        eye = np.eye(SUB)
        depth = np.zeros((box, self.per_group, self.per_group, box))
        for n in range(self.per_group):
            depth[:, n, n, :] = magic.T
        depth = depth.reshape(grid, grid)
        self.depth = np.concatenate(halves(depth), axis=0)
        self.inner = stacked(np.kron(eye, magic), 1)
        self.outer = stacked(np.kron(magic, eye), 1)
        places = np.arange(grid)
        wave = np.zeros((self.pln, self.orb, self.slots, grid))
        for p in range(self.pln):
            for s in range(self.slots):
                within = p * self.slots + s
                if within < self.kx_block:
                    k = self.kx_block * np.arange(self.orb) + within
                    wave[p, :, s, :] = cas(k[:, None] * places[None, :], doubled)
        self.wave = wave.reshape(self.pln, self.rows, grid).astype(np.float32)
        self.quarter = box // 4


def lane_owner(shape, box):
    return lax.broadcasted_iota(jnp.int32, shape, len(shape) - 1) // box


def start_copies(sems, first, *pairs):
    copies = []
    for number, (source, target) in enumerate(pairs):
        copy = pltpu.make_async_copy(source, target, sems.at[first + number])
        copy.start()
        copies.append(copy)
    return copies


def wait_copies(copies):
    for copy in copies:
        copy.wait()


def density_kernel(
    plan, where_ref, corner_ref, weight_ref, coef_any, depth_any, inner_any, outer_any, wave_any, spectrum_any,
    send_any, psi_any, wave_out_any, *refs,
):
    half = plan.half
    piece_anys = refs[: 2 * half]
    coef_ref, depth_ref, inner_ref, outer_ref, wave_ref, own_wave_ref, stage_ref, psi_ref, send_ref = refs[2 * half : -7]
    block_ref, edge_ref, block_out_ref, edge_out_ref, spectrum_sems, out_sems, sems = refs[-7:]
    box, grid, count, slots = plan.box, plan.grid, plan.per_group, plan.slots
    section = box * box
    span = SUB * box
    me = lax.rem(where_ref[0], plan.pln)
    coef_copy = pltpu.make_async_copy(coef_any, coef_ref, sems.at[0])
    coef_copy.start()
    fetched = start_copies(
        sems, 1, (depth_any, depth_ref), (inner_any, inner_ref), (outer_any, outer_ref), (wave_any.at[me], wave_ref)
    )
    spectrum = spectrum_copies(plan, me, spectrum_any, block_ref, edge_ref, spectrum_sems)
    for copy in spectrum:
        copy.start()
    owner = lane_owner((1, grid), box)
    owner_pair = jnp.concatenate([owner, owner], axis=1)
    coef_copy.wait()
    wait_copies(fetched[:1])
    for group in range(plan.groups):
        for p in range(box):
            stage_ref[count * p : count * (p + 1), :] = coef_ref[group, :, section * p : section * (p + 1)].astype(F32)
        coef = stage_ref[...].astype(BF16)
        first = dot(jnp.concatenate([coef, coef], axis=0), depth_ref[...], ((0,), (0,)))
        if group == 0:
            wait_copies(fetched[1:])
        inner, outer = inner_ref[...], outer_ref[...]
        second = side_by_side(inner, [first[span * t : span * (t + 1)] for t in range(box // SUB)])
        second = jnp.concatenate(second, axis=0).reshape(box, box // SUB, SUB, grid)
        third = side_by_side(outer, [second[:, t].reshape(span, grid) for t in range(box // SUB)])
        for t in range(box // SUB):
            psi_ref[:, SUB * t : SUB * (t + 1), :] = third[t].reshape(box, SUB, grid)
        sent = start_copies(sems, 5, (psi_ref, psi_any.at[group]))
        whole_wave = wave_ref[...]
        wave = jnp.zeros_like(whole_wave)
        weight = jnp.zeros((1, grid), F32)
        wave_terms = []
        kind = iota((2 * SUB, 1), 0)
        corner = jnp.zeros((2 * SUB, grid), F32)
        for n in range(count):
            number = group * count + n
            every = jnp.zeros_like(whole_wave)
            for block in range(count):
                shift = lax.rem(box * block - corner_ref[number, 2] + grid, grid)
                every = jnp.where(owner == block, pltpu.roll(whole_wave, shift, 1), every)
            high, low = split(every)
            wave_terms.append(jnp.where((owner & 1) == 0, high.astype(F32), low.astype(F32)).astype(BF16))
            wave = jnp.where(owner == n, every, wave)
            weight = jnp.where(owner == n, weight_ref[number], weight)
            place = jnp.where(kind == 0, corner_ref[number, 0], corner_ref[number, 1])
            corner = jnp.where(owner == n, place.astype(F32), corner)
        own_wave_ref[...] = wave
        sent += start_copies(sems, 6, (own_wave_ref, wave_out_any.at[group]))
        for o in range(plan.orb):
            send_ref[o, plan.area :, :] = corner.astype(send_ref.dtype)
        wave_terms = jnp.concatenate(wave_terms, axis=0)
        if group == 0:
            wait_copies(spectrum)
            folded = fold_spectrum(plan, piece_anys, block_ref, edge_ref, block_out_ref, edge_out_ref, out_sems)
        rows = pl.ds(plan.area, 2 * SUB)
        sent += start_copies(sems, 7, (send_ref.at[:, rows, :], send_any.at[:, group, rows, :]))
        per_part = plan.quarter // 2
        for pair in range(box // 2):
            columns = [psi_ref[b] * psi_ref[b] * weight for b in (2 * pair, 2 * pair + 1)]
            up, down = split(jnp.concatenate(columns, axis=1))
            out = dot(wave_terms, jnp.concatenate([up, up, down, down], axis=0))
            mine = out[: plan.rows]
            for n in range(1, count):
                mine = jnp.where(owner_pair == n, out[plan.rows * n : plan.rows * (n + 1)], mine)
            for o in range(plan.orb):
                part = mine[slots * o : slots * (o + 1)]
                tile = jnp.concatenate([part[:, :grid], part[:, grid:]], axis=0)
                send_ref[o, 2 * slots * pair : 2 * slots * (pair + 1), :] = tile.astype(send_ref.dtype)
            if pair % per_part == per_part - 1:
                part = pair // per_part
                rows = pl.ds(plan.quarter * slots * part, plan.quarter * slots)
                sent += start_copies(sems, 8 + part, (send_ref.at[:, rows, :], send_any.at[:, group, rows, :]))
        wait_copies(sent)
    wait_copies(folded)


def spectrum_copies(plan, me, spectrum_any, block_ref, edge_ref, sems):
    half, slots = plan.half, plan.slots
    group, index = me // half, lax.rem(me, half)

    def fetch(target, source, buffer, number):
        first = jnp.minimum(target * slots, max(plan.kx_block - slots, 0))
        first = pl.multiple_of(first, SUB)
        return pltpu.make_async_copy(source.at[:, pl.ds(first, slots), :], buffer, sems.at[number])

    copies = []
    for step in range(half):
        copies.append(fetch(group * half + lax.rem(index + step, half), spectrum_any, block_ref.at[step], step))
    for step in range(half):
        target = (1 - group) * half + step
        copies.append(fetch(target, spectrum_any.at[pl.ds(0, 1)], edge_ref.at[pl.ds(step, 1)], half + step))
    return copies


def fold_spectrum(plan, piece_anys, block_ref, edge_ref, block_out_ref, edge_out_ref, sems):
    half, grid = plan.half, plan.grid
    odd = (iota((1, 1, grid), 2) & 1) == 1

    def fold(values):
        last = values[..., grid : grid + 1]
        return values[..., :grid] + jnp.where(odd, last, -last)

    for step in range(half):
        block_out_ref[step] = fold(block_ref[step])
    edge_out_ref[...] = fold(edge_ref[...])
    pairs = [(block_out_ref.at[step], piece_anys[step]) for step in range(half)]
    pairs += [(edge_out_ref.at[pl.ds(step, 1)], piece_anys[half + step]) for step in range(half)]
    return start_copies(sems, 0, *pairs)


def tables_kernel(plan, where_ref, piece_any, *refs):
    forward_y_ref, forward_z_ref, inverse_y_ref, inverse_z_ref, inner_ref, outer_ref, back_ref = refs[:7]
    piece_ref, sems = refs[7:]
    grid, doubled, me = plan.grid, plan.doubled, lax.rem(where_ref[0], plan.pln)
    copies = start_copies(sems, 0, (piece_any, piece_ref))
    forward, _ = mode_table(plan, me, (doubled, grid), 0)
    forward_y_ref[...] = jnp.concatenate(split(forward), axis=1)
    forward_z_ref[...] = jnp.concatenate(split(depth_mode_table(plan, (grid, doubled), 1)), axis=0)
    inverse, weight = mode_table(plan, me, (grid, doubled), 1)
    inverse_y_ref[...] = stack_terms(inverse * (weight * (1.0 / doubled**3)), 1)
    inverse_z_ref[...] = stack_terms(depth_mode_table(plan, (doubled, grid), 0), 0)
    inner_ref[...] = stack_terms(inner_back_table(plan.box), 1)
    outer_ref[...] = stack_terms(outer_back_table(plan.box), 1)
    back_ref[...] = stack_terms(depth_back_table(plan), 1)
    wait_copies(copies)


def solve_kernel(plan, where_ref, recv_ref, *refs):
    half, slots, grid, box, count = plan.half, plan.slots, plan.grid, plan.box, plan.per_group
    piece_refs, edge_refs = refs[:half], refs[half : 2 * half]
    forward_y_ref, forward_z_ref, inverse_y_ref, inverse_z_ref = refs[2 * half : 2 * half + 4]
    chips = plan.orb // 2
    own_ref, swap_ref, *send_refs = refs[2 * half + 4 : 2 * half + 5 + chips]
    field_ref, result_ref, table_ref, corner_ref, sem = refs[2 * half + 5 + chips :]
    me, own = lax.rem(where_ref[0], plan.pln), where_ref[0] // plan.pln
    depth = plan.area
    all_groups = plan.orb * plan.groups
    owner = lane_owner((1, grid), box)
    for group in range(all_groups):
        tile = recv_ref[group, depth : depth + 2 * SUB, :].astype(F32).astype(jnp.int32)
        table_ref[2 * group : 2 * group + 2, :] = tile[:2]
    copy = pltpu.make_async_copy(table_ref, corner_ref, sem)
    copy.start()
    field_ref[...] = jnp.zeros_like(field_ref)
    forward_y, forward_z = forward_y_ref[...], forward_z_ref[...]
    inverse_y, inverse_z = inverse_y_ref[...], inverse_z_ref[...]
    copy.wait()

    def start(group, n):
        return pl.multiple_of(corner_ref[2 * group + 1, box * n] * slots, SUB)

    def place(group, carry):
        values = recv_ref[group, :depth, :]
        for n in range(count):
            shift = lax.rem(corner_ref[2 * group, box * n] - box * n + grid, grid)
            moved = pltpu.roll(jnp.where(owner == n, values, jnp.zeros_like(values)), shift, 1)
            field_ref[pl.ds(start(group, n), depth), :] += moved.astype(F32)
        return carry

    lax.fori_loop(0, all_groups, place, 0)
    row = iota((grid, 1), 0)
    edge_row = lax.rem(me, half) * plan.ky_block
    edges = edge_refs[0][0]
    for ref in edge_refs[1:]:
        edges = edges + ref[0]
    for pair in range(slots // 2):
        both = (2 * pair, 2 * pair + 1)
        planes = jnp.concatenate([field_ref[pl.ds(s, grid, stride=slots), :] for s in both], axis=1)
        planes = planes.astype(BF16)
        modes = dot(forward_y, jnp.concatenate([planes, planes], axis=0)).astype(BF16)
        back = []
        for side, s in enumerate(both):
            spectrum = jnp.concatenate([ref[pl.ds(s, plan.ky_block, stride=slots), :] for ref in piece_refs], axis=0)
            other = jnp.where(row == edge_row, edges[s : s + 1], spectrum)
            spectrum = jnp.concatenate([spectrum, other], axis=0)
            mine = modes[:, grid * side : grid * (side + 1)]
            mine = dot(jnp.concatenate([mine, mine], axis=1), forward_z)
            mine = mine * jnp.concatenate([spectrum, spectrum], axis=1)
            back.append(dot(terms_of(mine, 1), inverse_z))
        planes = dot(inverse_y, terms_of(jnp.concatenate(back, axis=1), 0))
        for side, s in enumerate(both):
            result_ref[pl.ds(s, grid, stride=slots), :] = planes[:, grid * side : grid * (side + 1)]

    def cut(d, group, carry):
        number = (own ^ d) * plan.groups + group
        values = jnp.zeros((depth, grid), BF16)
        for n in range(count):
            shift = lax.rem(box * n - corner_ref[2 * number, box * n] + grid, grid)
            rows = result_ref[pl.ds(start(number, n), depth), :].astype(BF16)
            values = jnp.where(owner == n, pltpu.roll(rows, shift, 1), values)
        if d < 2:
            (own_ref, swap_ref)[d][group] = values
        else:
            send_refs[d // 2 - 1][d % 2, group] = values
        return carry

    for d in range(plan.orb):
        if plan.groups == 1:
            cut(d, 0, 0)
        else:
            lax.fori_loop(0, plan.groups, functools.partial(cut, d), 0)


def gather_kernel(swap_ref, *refs):
    out_ref = refs[-1]
    out_ref[0] = swap_ref[...]
    for number, ref in enumerate(refs[:-1]):
        out_ref[number + 1] = ref[1]


def terms_kernel(plan, where_ref, *refs):
    box, grid, count, slots, pln = plan.box, plan.grid, plan.per_group, plan.slots, plan.pln
    chips = plan.orb // 2
    own_ref, other_ref, *chip_refs = refs[: chips + 1]
    psi_any, wave_ref, inner_ref, outer_ref, back_ref, *refs = refs[chips + 1 :]

    def tile(d, rows):
        if d % 2:
            return other_ref[d // 2, 0, rows]
        return chip_refs[d // 2 - 1][0, 0, rows] if d else own_ref[0, rows]

    out_refs = refs[:pln]
    psi_ref, stage_ref, result_ref, sem = refs[pln:]
    group = pl.program_id(0)
    copy = pltpu.make_async_copy(psi_any.at[group], psi_ref, sem)
    copy.start()
    owner = lane_owner((1, grid), box)
    own = where_ref[0] // pln
    rows = [wave_ref[0, pl.ds(pl.multiple_of((own ^ d) * slots, SUB), slots), :] for d in range(plan.orb)]
    wave = jnp.concatenate(split(jnp.concatenate(rows, axis=0).T), axis=1)
    inner, outer, back = inner_ref[...], outer_ref[...], back_ref[...]
    copy.wait()
    for pair in range(box // 2):
        tiles = [tile(d, pl.ds(2 * slots * pair, 2 * slots)).astype(F32) for d in range(plan.orb)]
        columns = [jnp.concatenate([t[slots * side : slots * (side + 1)] for t in tiles], axis=0) for side in range(2)]
        both = jnp.concatenate(columns, axis=1).astype(BF16)
        out = dot(wave, jnp.concatenate([both, both], axis=0))
        for side, b in enumerate((2 * pair, 2 * pair + 1)):
            mine = out[:, grid * side : grid * (side + 1)]
            potential = jnp.zeros((box, grid), F32)
            for n in range(count):
                potential = jnp.where(owner == n, mine[box * n : box * (n + 1)], potential)
            stage_ref[b] = potential * psi_ref[b]
    span = SUB * box
    second = side_by_side(inner, [stage_ref[SUB * t : SUB * (t + 1)].reshape(span, grid) for t in range(box // SUB)])
    second = jnp.concatenate(second, axis=0).reshape(box, box // SUB, SUB, grid)
    third = side_by_side(outer, [second[:, t].reshape(span, grid) for t in range(box // SUB)])
    for t in range(box // SUB):
        stage_ref[:, SUB * t : SUB * (t + 1), :] = third[t].reshape(box, SUB, grid)
    values = terms_of(stage_ref[...].reshape(box * box, grid), 1)
    out = dot(back, values, ((1,), (1,)))
    part = plan.box_part * count
    for p in range(pln):
        result_ref[p] = out[part * p : part * (p + 1)]
    me = lax.rem(where_ref[0], pln)
    out_refs[0][0] = result_ref[me]
    for step in range(1, pln):
        out_refs[step][0] = result_ref[lax.rem(me + step, pln)].astype(BF16)


def sum_kernel(plan, *refs):
    out_ref = refs[plan.pln]
    total = refs[0][0]
    for ref in refs[1 : plan.pln]:
        total = total + ref[0].astype(F32)
    section = plan.box * plan.box
    count = plan.per_group
    for j in range(plan.box_part):
        out_ref[0, :, section * j : section * (j + 1)] = total[count * j : count * (j + 1)].astype(out_ref.dtype)


def per_device(plan, orbitals, occupations, box_offsets, kernel_spectrum):
    orb, pln, half, slots = plan.orb, plan.pln, plan.half, plan.slots
    groups, count, box, grid = plan.groups, plan.per_group, plan.box, plan.grid
    plane_index = lax.axis_index("pln")
    where = (lax.axis_index("orb") * pln + plane_index).astype(jnp.int32)[None]
    smem = pl.BlockSpec(memory_space=pltpu.SMEM)
    anywhere = pl.BlockSpec(memory_space=pl.ANY)
    vmem = pl.BlockSpec(memory_space=pltpu.VMEM)
    dma = pltpu.SemaphoreType.DMA
    coefs = orbitals.reshape(groups, count, orbitals.shape[1])
    by_ky = jnp.transpose(kernel_spectrum, (1, 2, 0))
    area = plan.area
    padded = area + 2 * SUB
    tables = [plan.depth, plan.inner, plan.outer]
    piece = jax.ShapeDtypeStruct((plan.ky_block, slots, grid), F32)
    edge = jax.ShapeDtypeStruct((1, slots, grid), F32)
    send, psi, wave, *pieces = pl.pallas_call(
        functools.partial(density_kernel, plan),
        in_specs=[smem, smem, smem] + [anywhere] * 6,
        out_specs=[anywhere] * (3 + 2 * half),
        out_shape=[
            jax.ShapeDtypeStruct((orb, groups, padded, grid), BF16),
            jax.ShapeDtypeStruct((groups, box, box, grid), F32),
            jax.ShapeDtypeStruct((groups, plan.rows, grid), F32),
            *[piece] * half,
            *[edge] * half,
        ],
        scratch_shapes=[
            pltpu.VMEM(coefs.shape, BF16),
            *[pltpu.VMEM(t.shape, t.dtype) for t in tables],
            pltpu.VMEM((plan.rows, grid), F32),
            pltpu.VMEM((plan.rows, grid), F32),
            pltpu.VMEM((grid, box * box), F32),
            pltpu.VMEM((box, box, grid), F32),
            pltpu.VMEM((orb, padded, grid), BF16),
            pltpu.VMEM((half, plan.ky_block, slots, plan.doubled), F32),
            pltpu.VMEM((half, slots, plan.doubled), F32),
            pltpu.VMEM((half, plan.ky_block, slots, grid), F32),
            pltpu.VMEM((half, slots, grid), F32),
            dma((2 * half,)),
            dma((2 * half,)),
            dma((12,)),
        ],
        compiler_params=pltpu.CompilerParams(vmem_limit_bytes=LARGE),
        name="density",
    )(where, box_offsets, occupations, coefs, *tables, plan.wave, by_ky)
    received = lax.all_to_all(send, "orb", split_axis=0, concat_axis=0, tiled=True)
    received = received.reshape(orb * groups, padded, grid)
    for step in range(1, half):
        pairs = [(g * half + i, g * half + (i + step) % half) for g in range(2) for i in range(half)]
        pieces[step] = lax.ppermute(pieces[step], "pln", pairs)
    for step in range(half):
        pieces[half + step] = lax.ppermute(pieces[half + step], "pln", [(0, half + step), (half, step)])
    pieces[:half] = [p.reshape(plan.ky_block * slots, grid) for p in pieces[:half]]

    small = pltpu.CompilerParams(vmem_limit_bytes=SMALL)
    span = SUB * box
    shapes = [(plan.doubled, 2 * grid), (2 * grid, plan.doubled), (grid, 3 * plan.doubled), (3 * plan.doubled, grid)]
    shapes += [(span, 3 * span), (span, 3 * span), (grid, 3 * grid)]
    tables = pl.pallas_call(
        functools.partial(tables_kernel, plan),
        in_specs=[smem, anywhere],
        out_specs=[vmem] * (len(shapes) + 1),
        out_shape=[*[jax.ShapeDtypeStruct(shape, BF16) for shape in shapes], jax.ShapeDtypeStruct(pieces[0].shape, F32)],
        scratch_shapes=[dma((1,))],
        compiler_params=small,
        name="tables",
    )(where, pieces[0])
    pieces[0] = tables[7]
    chips = orb // 2
    single = jax.ShapeDtypeStruct((groups, area, grid), BF16)
    send = pl.pallas_call(
        functools.partial(solve_kernel, plan),
        in_specs=[smem] + [vmem] * (5 + 2 * half),
        out_specs=[vmem] * (1 + chips),
        out_shape=[single] * 2 + [jax.ShapeDtypeStruct((2, groups, area, grid), BF16)] * (chips - 1),
        scratch_shapes=[
            pltpu.VMEM((grid * slots, grid), F32),
            pltpu.VMEM((grid * slots, grid), F32),
            pltpu.VMEM((2 * orb * groups, grid), jnp.int32),
            pltpu.SMEM((2 * orb * groups, grid), jnp.int32),
            dma,
        ],
        compiler_params=small,
        name="solve",
    )(where, received, *pieces, *tables[:4])
    own, swap, *send = send
    core_pairs = [(o, o ^ 1) for o in range(orb)]
    arrived = [None] * (chips - 1)
    for e in reversed(range(1, chips)):
        arrived[e - 1] = lax.ppermute(send[e - 1], "orb", [(o, o ^ (2 * e)) for o in range(orb)])
    gathered = pl.pallas_call(
        gather_kernel,
        in_specs=[vmem] * chips,
        out_specs=vmem,
        out_shape=jax.ShapeDtypeStruct((chips, groups, area, grid), BF16),
        compiler_params=small,
        name="gather",
    )(swap, *arrived)
    other = lax.ppermute(gathered, "orb", core_pairs)
    part = plan.box_part * count
    finished = pl.pallas_call(
        functools.partial(terms_kernel, plan),
        grid=(groups,),
        in_specs=[
            smem,
            pl.BlockSpec((1, area, grid), lambda g: (g, 0, 0)),
            pl.BlockSpec((chips, 1, area, grid), lambda g: (0, g, 0, 0)),
            *[pl.BlockSpec((1, 1, area, grid), lambda g: (0, g, 0, 0))] * (chips - 1),
            anywhere,
            pl.BlockSpec((1, plan.rows, grid), lambda g: (g, 0, 0)),
            vmem,
            vmem,
            vmem,
        ],
        out_specs=[pl.BlockSpec((1, part, box * box), lambda g: (g, 0, 0))] * pln,
        out_shape=[jax.ShapeDtypeStruct((groups, part, box * box), BF16 if step else F32) for step in range(pln)],
        scratch_shapes=[
            pltpu.VMEM((box, box, grid), F32),
            pltpu.VMEM((box, box, grid), F32),
            pltpu.VMEM((pln, part, box * box), F32),
            dma,
        ],
        compiler_params=small,
        name="terms",
    )(where, own, other, *arrived, psi, wave, *tables[4:7])
    finished = list(finished)
    for step in range(1, pln):
        finished[step] = lax.ppermute(finished[step], "pln", [(p, (p + step) % pln) for p in range(pln)])
    cells = plan.box_part * box * box
    result = pl.pallas_call(
        functools.partial(sum_kernel, plan),
        grid=(groups,),
        in_specs=[pl.BlockSpec((1, part, box * box), lambda g: (g, 0, 0))] * pln,
        out_specs=pl.BlockSpec((1, count, cells), lambda g: (g, 0, 0)),
        out_shape=jax.ShapeDtypeStruct((groups, count, cells), BF16),
        compiler_params=small,
        name="sum",
    )(*finished)
    return result.reshape(groups * count, cells)


def solution(mesh):
    in_specs = (P("orb", None), P("orb"), P("orb", None), P(None, "pln", "orb"))
    out_specs = P("orb", "pln")

    def whole(orbitals, occupations, box_offsets, kernel_spectrum):
        plan = Plan(mesh, orbitals.shape, kernel_spectrum.shape)
        return jax.shard_map(
            functools.partial(per_device, plan), mesh=mesh, in_specs=in_specs, out_specs=out_specs, check_vma=False
        )(orbitals, occupations, box_offsets, kernel_spectrum)

    return whole
```

```python
import functools
import math

import jax
import jax.numpy as jnp
import numpy as np
from jax import lax
from jax.experimental import pallas as pl
from jax.experimental.pallas import tpu as pltpu
from jax.sharding import PartitionSpec as P

MAGIC_TAPS = (
    8.433424733352934e-07,
    -1.290557201342061e-05,
    8.76298447621056e-05,
    -0.00030158038132690465,
    0.001747237136729939,
    -0.009420470302010804,
    0.023738214637249424,
    0.0612625895831208,
    0.9940415697834004,
    -0.06048952891969835,
    -0.021030251609303816,
    0.013372634148547948,
    -0.0034412814449349387,
    0.0004944322768868992,
    -5.185986881173433e-05,
    2.7273449291197967e-06,
)
F32 = jnp.float32
BF16 = jnp.bfloat16
SUB = 8
LARGE = 60 * 1024 * 1024
SMALL = 32 * 1024 * 1024


def magic_filter(box):
    table = np.zeros((box, box))
    for row in range(box):
        for tap in range(-8, 8):
            if 0 <= row + tap < box:
                table[row, row + tap] = MAGIC_TAPS[tap + 8]
    return table.astype(np.float32).astype(np.float64)


def cas(product, doubled):
    angle = 2.0 * math.pi * (product % doubled) / doubled
    return np.cos(angle) + np.sin(angle)


def halves(table):
    high = np.asarray(table, np.float32).astype(jnp.bfloat16)
    low = (np.asarray(table, np.float64) - high.astype(np.float64)).astype(jnp.bfloat16)
    return high, low


def split(values):
    high = values.astype(BF16)
    low = (values - high.astype(F32)).astype(BF16)
    return high, low


def dot(left, right, dims=((1,), (0,))):
    return lax.dot_general(left, right, (dims, ((), ())), preferred_element_type=F32)


def terms_of(values, axis):
    high, low = split(values)
    return jnp.concatenate([high, high, low], axis=axis)


def stacked(table, axis):
    high, low = halves(table)
    return np.concatenate([high, low, high], axis=axis)


SINE = (1.0, -1.0 / 6, 1.0 / 120, -1.0 / 5040, 1.0 / 362880)
COSINE = (1.0, -1.0 / 2, 1.0 / 24, -1.0 / 720, 1.0 / 40320)


def turn(steps, doubled):
    quarter = doubled // 4
    place = (steps + quarter // 2) & (doubled - 1)
    quadrant = place // quarter
    angle = (place - quadrant * quarter - quarter // 2).astype(F32) * (2.0 * math.pi / doubled)
    square = angle * angle
    cosine, sine = COSINE[-1], SINE[-1]
    for even, odd in zip(COSINE[-2::-1], SINE[-2::-1]):
        cosine, sine = cosine * square + even, sine * square + odd
    return quadrant, cosine, sine * angle


def cosine_table(steps, doubled):
    quadrant, cosine, sine = turn(steps, doubled)
    value = jnp.where((quadrant & 1) == 0, cosine, -sine)
    return jnp.where(quadrant < 2, value, -value)


def cas_table(steps, doubled):
    quadrant, cosine, sine = turn(steps, doubled)
    value = jnp.where((quadrant & 1) == 0, cosine + sine, cosine - sine)
    return jnp.where(quadrant < 2, value, -value)


def iota(shape, axis):
    return lax.broadcasted_iota(jnp.int32, shape, axis)


def stack_terms(table, axis):
    high, low = split(table)
    return jnp.concatenate([high, low, high], axis=axis)


def tap_table(step):
    value = jnp.zeros(step.shape, F32)
    for tap in range(-8, 8):
        value = jnp.where(step == tap, np.float32(MAGIC_TAPS[tap + 8]), value)
    return value


def inner_back_table(box):
    span = SUB * box
    one = tap_table(iota((box, span), 0) - (iota((box, span), 1) & (box - 1)))
    whole = jnp.concatenate([one] * SUB, axis=0)
    return jnp.where(iota((span, span), 0) // box == iota((span, span), 1) // box, whole, 0.0)


def outer_back_table(box):
    span = SUB * box
    row, column = iota((span, span), 0), iota((span, span), 1)
    value = tap_table(row // SUB - column // SUB)
    return jnp.where((row & (SUB - 1)) == (column & (SUB - 1)), value, 0.0)


def depth_back_table(plan):
    grid, box, count = plan.grid, plan.box, plan.per_group
    row, column = iota((grid, grid), 0), iota((grid, grid), 1)
    value = tap_table(row // count - (column & (box - 1)))
    return jnp.where((row & (count - 1)) == column // box, value, 0.0)


def mode_table(plan, me, shape, axis):
    grid, doubled, half = plan.grid, plan.doubled, plan.half
    line = tuple(doubled if dim == axis else 1 for dim in range(2))
    group, index = me // half, lax.rem(me, half)
    mode = iota(line, axis)
    within = mode & (grid - 1)
    block = (index - within // plan.ky_block + half) & (half - 1)
    step = block * plan.ky_block + (within & (plan.ky_block - 1))
    edge = (mode >= grid) & (step == 0)
    frequency = jnp.where(edge, ((1 - group) * grid), group * grid + step)
    quarter = jnp.where((mode >= grid) & (step != 0), doubled // 4, 0)
    weight = jnp.where(step == 0, 1.0, 2.0)
    return cosine_table(frequency * iota(shape, 1 - axis) - quarter, doubled), weight


def depth_mode_table(plan, shape, axis):
    grid, doubled = plan.grid, plan.doubled
    place = iota(shape, axis)
    frequency = jnp.where(place < grid, place, grid - place)
    return jnp.where(place == grid, 0.0, cas_table(frequency * iota(shape, 1 - axis), doubled))


def side_by_side(table, parts):
    results = []
    for first, second in zip(parts[::2], parts[1::2]):
        width = first.shape[1]
        out = dot(table, terms_of(jnp.concatenate([first, second], axis=1), 0))
        results += [out[:, :width], out[:, width:]]
    return results


class Plan:
    def __init__(self, mesh, orbital_shape, kernel_shape):
        self.orb = mesh.shape["orb"]
        self.pln = mesh.shape["pln"]
        self.doubled = doubled = kernel_shape[0]
        self.grid = grid = doubled // 2
        self.box = box = round(orbital_shape[1] ** (1 / 3))
        self.per_group = grid // box
        self.groups = orbital_shape[0] // self.orb // self.per_group
        self.ky_block = kernel_shape[1] // self.pln
        self.kx_block = kernel_shape[2] // self.orb
        self.slots = SUB * -(-self.kx_block // (SUB * self.pln))
        self.half = self.pln // 2
        self.rows = self.orb * self.slots
        self.area = box * self.slots
        self.box_part = box // self.pln
        magic = magic_filter(box)
        eye = np.eye(SUB)
        depth = np.zeros((box, self.per_group, self.per_group, box))
        for n in range(self.per_group):
            depth[:, n, n, :] = magic.T
        depth = depth.reshape(grid, grid)
        self.depth = np.concatenate(halves(depth), axis=0)
        self.inner = stacked(np.kron(eye, magic), 1)
        self.outer = stacked(np.kron(magic, eye), 1)
        places = np.arange(grid)
        wave = np.zeros((self.pln, self.orb, self.slots, grid))
        for p in range(self.pln):
            for s in range(self.slots):
                within = p * self.slots + s
                if within < self.kx_block:
                    k = self.kx_block * np.arange(self.orb) + within
                    wave[p, :, s, :] = cas(k[:, None] * places[None, :], doubled)
        self.wave = wave.reshape(self.pln, self.rows, grid).astype(np.float32)
        self.quarter = box // 4


def lane_owner(shape, box):
    return lax.broadcasted_iota(jnp.int32, shape, len(shape) - 1) // box


def start_copies(sems, first, *pairs):
    copies = []
    for number, (source, target) in enumerate(pairs):
        copy = pltpu.make_async_copy(source, target, sems.at[first + number])
        copy.start()
        copies.append(copy)
    return copies


def wait_copies(copies):
    for copy in copies:
        copy.wait()


def density_kernel(
    plan, where_ref, corner_ref, weight_ref, coef_any, depth_any, inner_any, outer_any, wave_any, spectrum_any,
    send_any, psi_any, wave_out_any, *refs,
):
    half = plan.half
    piece_anys = refs[: 2 * half]
    coef_ref, depth_ref, inner_ref, outer_ref, wave_ref, own_wave_ref, stage_ref, psi_ref, send_ref = refs[2 * half : -7]
    block_ref, edge_ref, block_out_ref, edge_out_ref, spectrum_sems, out_sems, sems = refs[-7:]
    box, grid, count, slots = plan.box, plan.grid, plan.per_group, plan.slots
    section = box * box
    span = SUB * box
    me = lax.rem(where_ref[0], plan.pln)
    coef_copy = pltpu.make_async_copy(coef_any, coef_ref, sems.at[0])
    coef_copy.start()
    fetched = start_copies(
        sems, 1, (depth_any, depth_ref), (inner_any, inner_ref), (outer_any, outer_ref), (wave_any.at[me], wave_ref)
    )
    spectrum = spectrum_copies(plan, me, spectrum_any, block_ref, edge_ref, spectrum_sems)
    for copy in spectrum:
        copy.start()
    owner = lane_owner((1, grid), box)
    owner_pair = jnp.concatenate([owner, owner], axis=1)
    coef_copy.wait()
    wait_copies(fetched[:1])
    for group in range(plan.groups):
        for p in range(box):
            stage_ref[count * p : count * (p + 1), :] = coef_ref[group, :, section * p : section * (p + 1)].astype(F32)
        coef = stage_ref[...].astype(BF16)
        first = dot(jnp.concatenate([coef, coef], axis=0), depth_ref[...], ((0,), (0,)))
        if group == 0:
            wait_copies(fetched[1:])
        inner, outer = inner_ref[...], outer_ref[...]
        second = side_by_side(inner, [first[span * t : span * (t + 1)] for t in range(box // SUB)])
        second = jnp.concatenate(second, axis=0).reshape(box, box // SUB, SUB, grid)
        third = side_by_side(outer, [second[:, t].reshape(span, grid) for t in range(box // SUB)])
        for t in range(box // SUB):
            psi_ref[:, SUB * t : SUB * (t + 1), :] = third[t].reshape(box, SUB, grid)
        sent = start_copies(sems, 5, (psi_ref, psi_any.at[group]))
        whole_wave = wave_ref[...]
        wave = jnp.zeros_like(whole_wave)
        weight = jnp.zeros((1, grid), F32)
        wave_terms = []
        kind = iota((2 * SUB, 1), 0)
        corner = jnp.zeros((2 * SUB, grid), F32)
        for n in range(count):
            number = group * count + n
            every = jnp.zeros_like(whole_wave)
            for block in range(count):
                shift = lax.rem(box * block - corner_ref[number, 2] + grid, grid)
                every = jnp.where(owner == block, pltpu.roll(whole_wave, shift, 1), every)
            high, low = split(every)
            wave_terms.append(jnp.where((owner & 1) == 0, high.astype(F32), low.astype(F32)).astype(BF16))
            wave = jnp.where(owner == n, every, wave)
            weight = jnp.where(owner == n, weight_ref[number], weight)
            place = jnp.where(kind == 0, corner_ref[number, 0], corner_ref[number, 1])
            corner = jnp.where(owner == n, place.astype(F32), corner)
        own_wave_ref[...] = wave
        sent += start_copies(sems, 6, (own_wave_ref, wave_out_any.at[group]))
        for o in range(plan.orb):
            send_ref[o, plan.area :, :] = corner.astype(send_ref.dtype)
        wave_terms = jnp.concatenate(wave_terms, axis=0)
        if group == 0:
            wait_copies(spectrum)
            folded = fold_spectrum(plan, piece_anys, block_ref, edge_ref, block_out_ref, edge_out_ref, out_sems)
        rows = pl.ds(plan.area, 2 * SUB)
        sent += start_copies(sems, 7, (send_ref.at[:, rows, :], send_any.at[:, group, rows, :]))
        per_part = plan.quarter // 2
        for pair in range(box // 2):
            columns = [psi_ref[b] * psi_ref[b] * weight for b in (2 * pair, 2 * pair + 1)]
            up, down = split(jnp.concatenate(columns, axis=1))
            out = dot(wave_terms, jnp.concatenate([up, up, down, down], axis=0))
            mine = out[: plan.rows]
            for n in range(1, count):
                mine = jnp.where(owner_pair == n, out[plan.rows * n : plan.rows * (n + 1)], mine)
            for o in range(plan.orb):
                part = mine[slots * o : slots * (o + 1)]
                tile = jnp.concatenate([part[:, :grid], part[:, grid:]], axis=0)
                send_ref[o, 2 * slots * pair : 2 * slots * (pair + 1), :] = tile.astype(send_ref.dtype)
            if pair % per_part == per_part - 1:
                part = pair // per_part
                rows = pl.ds(plan.quarter * slots * part, plan.quarter * slots)
                sent += start_copies(sems, 8 + part, (send_ref.at[:, rows, :], send_any.at[:, group, rows, :]))
        wait_copies(sent)
    wait_copies(folded)


def spectrum_copies(plan, me, spectrum_any, block_ref, edge_ref, sems):
    half, slots = plan.half, plan.slots
    group, index = me // half, lax.rem(me, half)

    def fetch(target, source, buffer, number):
        first = jnp.minimum(target * slots, max(plan.kx_block - slots, 0))
        first = pl.multiple_of(first, SUB)
        return pltpu.make_async_copy(source.at[:, pl.ds(first, slots), :], buffer, sems.at[number])

    copies = []
    for step in range(half):
        copies.append(fetch(group * half + lax.rem(index + step, half), spectrum_any, block_ref.at[step], step))
    for step in range(half):
        target = (1 - group) * half + step
        copies.append(fetch(target, spectrum_any.at[pl.ds(0, 1)], edge_ref.at[pl.ds(step, 1)], half + step))
    return copies


def fold_spectrum(plan, piece_anys, block_ref, edge_ref, block_out_ref, edge_out_ref, sems):
    half, grid = plan.half, plan.grid
    odd = (iota((1, 1, grid), 2) & 1) == 1

    def fold(values):
        last = values[..., grid : grid + 1]
        return values[..., :grid] + jnp.where(odd, last, -last)

    for step in range(half):
        block_out_ref[step] = fold(block_ref[step])
    edge_out_ref[...] = fold(edge_ref[...])
    pairs = [(block_out_ref.at[step], piece_anys[step]) for step in range(half)]
    pairs += [(edge_out_ref.at[pl.ds(step, 1)], piece_anys[half + step]) for step in range(half)]
    return start_copies(sems, 0, *pairs)


def tables_kernel(plan, where_ref, piece_any, *refs):
    forward_y_ref, forward_z_ref, inverse_y_ref, inverse_z_ref, inner_ref, outer_ref, back_ref = refs[:7]
    piece_ref, sems = refs[7:]
    grid, doubled, me = plan.grid, plan.doubled, lax.rem(where_ref[0], plan.pln)
    copies = start_copies(sems, 0, (piece_any, piece_ref))
    forward, _ = mode_table(plan, me, (doubled, grid), 0)
    forward_y_ref[...] = jnp.concatenate(split(forward), axis=1)
    forward_z_ref[...] = jnp.concatenate(split(depth_mode_table(plan, (grid, doubled), 1)), axis=0)
    inverse, weight = mode_table(plan, me, (grid, doubled), 1)
    inverse_y_ref[...] = stack_terms(inverse * (weight * (1.0 / doubled**3)), 1)
    inverse_z_ref[...] = stack_terms(depth_mode_table(plan, (doubled, grid), 0), 0)
    inner_ref[...] = stack_terms(inner_back_table(plan.box), 1)
    outer_ref[...] = stack_terms(outer_back_table(plan.box), 1)
    back_ref[...] = stack_terms(depth_back_table(plan), 1)
    wait_copies(copies)


def solve_kernel(plan, where_ref, recv_ref, *refs):
    half, slots, grid, box, count = plan.half, plan.slots, plan.grid, plan.box, plan.per_group
    piece_refs, edge_refs = refs[:half], refs[half : 2 * half]
    forward_y_ref, forward_z_ref, inverse_y_ref, inverse_z_ref = refs[2 * half : 2 * half + 4]
    chips = plan.orb // 2
    own_ref, swap_ref, *send_refs = refs[2 * half + 4 : 2 * half + 5 + chips]
    field_ref, result_ref, table_ref, corner_ref, sem = refs[2 * half + 5 + chips :]
    me, own = lax.rem(where_ref[0], plan.pln), where_ref[0] // plan.pln
    depth = plan.area
    all_groups = plan.orb * plan.groups
    owner = lane_owner((1, grid), box)
    for group in range(all_groups):
        tile = recv_ref[group, depth : depth + 2 * SUB, :].astype(F32).astype(jnp.int32)
        table_ref[2 * group : 2 * group + 2, :] = tile[:2]
    copy = pltpu.make_async_copy(table_ref, corner_ref, sem)
    copy.start()
    field_ref[...] = jnp.zeros_like(field_ref)
    forward_y, forward_z = forward_y_ref[...], forward_z_ref[...]
    inverse_y, inverse_z = inverse_y_ref[...], inverse_z_ref[...]
    copy.wait()

    def start(group, n):
        return pl.multiple_of(corner_ref[2 * group + 1, box * n] * slots, SUB)

    def place(group, carry):
        values = recv_ref[group, :depth, :]
        for n in range(count):
            shift = lax.rem(corner_ref[2 * group, box * n] - box * n + grid, grid)
            moved = pltpu.roll(jnp.where(owner == n, values, jnp.zeros_like(values)), shift, 1)
            field_ref[pl.ds(start(group, n), depth), :] += moved.astype(F32)
        return carry

    if plan.groups == 1:
        for group in range(all_groups):
            place(group, 0)
    else:
        lax.fori_loop(0, all_groups, place, 0)
    row = iota((grid, 1), 0)
    edge_row = lax.rem(me, half) * plan.ky_block
    edges = edge_refs[0][0]
    for ref in edge_refs[1:]:
        edges = edges + ref[0]
    batch = slots // 2
    for first in range(0, slots, batch):
        rows, spectra = [], []
        for s in range(first, first + batch, 2):
            planes = [field_ref[pl.ds(t, grid, stride=slots), :] for t in (s, s + 1)]
            planes = jnp.concatenate(planes, axis=1).astype(BF16)
            modes = dot(forward_y, jnp.concatenate([planes, planes], axis=0)).astype(BF16)
            rows += [modes[:, :grid], modes[:, grid:]]
        for s in range(first, first + batch):
            spectrum = jnp.concatenate([ref[pl.ds(s, plan.ky_block, stride=slots), :] for ref in piece_refs], axis=0)
            spectra += [spectrum, jnp.where(row == edge_row, edges[s : s + 1], spectrum)]
        rows, spectra = jnp.concatenate(rows, axis=0), jnp.concatenate(spectra, axis=0)
        modes = dot(jnp.concatenate([rows, rows], axis=1), forward_z) * jnp.concatenate([spectra, spectra], axis=1)
        back = dot(terms_of(modes, 1), inverse_z)
        for t in range(0, batch, 2):
            size = 2 * grid
            both = [back[size * u : size * (u + 1)] for u in (t, t + 1)]
            planes = dot(inverse_y, terms_of(jnp.concatenate(both, axis=1), 0))
            for side in range(2):
                result_ref[pl.ds(first + t + side, grid, stride=slots), :] = planes[:, grid * side : grid * (side + 1)]

    def cut(d, group, carry):
        number = (own ^ d) * plan.groups + group
        values = jnp.zeros((depth, grid), BF16)
        for n in range(count):
            shift = lax.rem(box * n - corner_ref[2 * number, box * n] + grid, grid)
            rows = result_ref[pl.ds(start(number, n), depth), :].astype(BF16)
            values = jnp.where(owner == n, pltpu.roll(rows, shift, 1), values)
        if d < 2:
            (own_ref, swap_ref)[d][group] = values
        else:
            send_refs[d // 2 - 1][d % 2, group] = values
        return carry

    for d in range(plan.orb):
        if plan.groups == 1:
            cut(d, 0, 0)
        else:
            lax.fori_loop(0, plan.groups, functools.partial(cut, d), 0)


def gather_kernel(swap_ref, *refs):
    out_ref = refs[-1]
    out_ref[0] = swap_ref[...]
    for number, ref in enumerate(refs[:-1]):
        out_ref[number + 1] = ref[1]


def terms_kernel(plan, where_ref, *refs):
    box, grid, count, slots, pln = plan.box, plan.grid, plan.per_group, plan.slots, plan.pln
    chips = plan.orb // 2
    own_ref, other_ref, *chip_refs = refs[: chips + 1]
    psi_any, wave_ref, inner_ref, outer_ref, back_ref, *refs = refs[chips + 1 :]

    def tile(d, rows):
        if d % 2:
            return other_ref[d // 2, 0, rows]
        return chip_refs[d // 2 - 1][0, 0, rows] if d else own_ref[0, rows]

    out_refs = refs[:pln]
    psi_ref, stage_ref, result_ref, sem = refs[pln:]
    group = pl.program_id(0)
    copy = pltpu.make_async_copy(psi_any.at[group], psi_ref, sem)
    copy.start()
    owner = lane_owner((1, grid), box)
    own = where_ref[0] // pln
    rows = [wave_ref[0, pl.ds(pl.multiple_of((own ^ d) * slots, SUB), slots), :] for d in range(plan.orb)]
    wave = jnp.concatenate(split(jnp.concatenate(rows, axis=0).T), axis=1)
    inner, outer, back = inner_ref[...], outer_ref[...], back_ref[...]
    copy.wait()
    for pair in range(box // 2):
        tiles = [tile(d, pl.ds(2 * slots * pair, 2 * slots)).astype(F32) for d in range(plan.orb)]
        columns = [jnp.concatenate([t[slots * side : slots * (side + 1)] for t in tiles], axis=0) for side in range(2)]
        both = jnp.concatenate(columns, axis=1).astype(BF16)
        out = dot(wave, jnp.concatenate([both, both], axis=0))
        for side, b in enumerate((2 * pair, 2 * pair + 1)):
            mine = out[:, grid * side : grid * (side + 1)]
            potential = jnp.zeros((box, grid), F32)
            for n in range(count):
                potential = jnp.where(owner == n, mine[box * n : box * (n + 1)], potential)
            stage_ref[b] = potential * psi_ref[b]
    span = SUB * box
    second = side_by_side(inner, [stage_ref[SUB * t : SUB * (t + 1)].reshape(span, grid) for t in range(box // SUB)])
    second = jnp.concatenate(second, axis=0).reshape(box, box // SUB, SUB, grid)
    third = side_by_side(outer, [second[:, t].reshape(span, grid) for t in range(box // SUB)])
    for t in range(box // SUB):
        stage_ref[:, SUB * t : SUB * (t + 1), :] = third[t].reshape(box, SUB, grid)
    values = terms_of(stage_ref[...].reshape(box * box, grid), 1)
    out = dot(back, values, ((1,), (1,)))
    part = plan.box_part * count
    for p in range(pln):
        result_ref[p] = out[part * p : part * (p + 1)]
    me = lax.rem(where_ref[0], pln)
    out_refs[0][0] = result_ref[me]
    for step in range(1, pln):
        out_refs[step][0] = result_ref[lax.rem(me + step, pln)].astype(BF16)


def sum_kernel(plan, *refs):
    out_ref = refs[plan.pln]
    total = refs[0][0]
    for ref in refs[1 : plan.pln]:
        total = total + ref[0].astype(F32)
    section = plan.box * plan.box
    count = plan.per_group
    for j in range(plan.box_part):
        out_ref[0, :, section * j : section * (j + 1)] = total[count * j : count * (j + 1)].astype(out_ref.dtype)


def per_device(plan, orbitals, occupations, box_offsets, kernel_spectrum):
    orb, pln, half, slots = plan.orb, plan.pln, plan.half, plan.slots
    groups, count, box, grid = plan.groups, plan.per_group, plan.box, plan.grid
    plane_index = lax.axis_index("pln")
    where = (lax.axis_index("orb") * pln + plane_index).astype(jnp.int32)[None]
    smem = pl.BlockSpec(memory_space=pltpu.SMEM)
    anywhere = pl.BlockSpec(memory_space=pl.ANY)
    vmem = pl.BlockSpec(memory_space=pltpu.VMEM)
    dma = pltpu.SemaphoreType.DMA
    coefs = orbitals.reshape(groups, count, orbitals.shape[1])
    by_ky = jnp.transpose(kernel_spectrum, (1, 2, 0))
    area = plan.area
    padded = area + 2 * SUB
    tables = [plan.depth, plan.inner, plan.outer]
    piece = jax.ShapeDtypeStruct((plan.ky_block, slots, grid), F32)
    edge = jax.ShapeDtypeStruct((1, slots, grid), F32)
    send, psi, wave, *pieces = pl.pallas_call(
        functools.partial(density_kernel, plan),
        in_specs=[smem, smem, smem] + [anywhere] * 6,
        out_specs=[anywhere] * (3 + 2 * half),
        out_shape=[
            jax.ShapeDtypeStruct((orb, groups, padded, grid), BF16),
            jax.ShapeDtypeStruct((groups, box, box, grid), F32),
            jax.ShapeDtypeStruct((groups, plan.rows, grid), F32),
            *[piece] * half,
            *[edge] * half,
        ],
        scratch_shapes=[
            pltpu.VMEM(coefs.shape, BF16),
            *[pltpu.VMEM(t.shape, t.dtype) for t in tables],
            pltpu.VMEM((plan.rows, grid), F32),
            pltpu.VMEM((plan.rows, grid), F32),
            pltpu.VMEM((grid, box * box), F32),
            pltpu.VMEM((box, box, grid), F32),
            pltpu.VMEM((orb, padded, grid), BF16),
            pltpu.VMEM((half, plan.ky_block, slots, plan.doubled), F32),
            pltpu.VMEM((half, slots, plan.doubled), F32),
            pltpu.VMEM((half, plan.ky_block, slots, grid), F32),
            pltpu.VMEM((half, slots, grid), F32),
            dma((2 * half,)),
            dma((2 * half,)),
            dma((12,)),
        ],
        compiler_params=pltpu.CompilerParams(vmem_limit_bytes=LARGE),
        name="density",
    )(where, box_offsets, occupations, coefs, *tables, plan.wave, by_ky)
    received = lax.all_to_all(send, "orb", split_axis=0, concat_axis=0, tiled=True)
    received = received.reshape(orb * groups, padded, grid)
    for step in range(1, half):
        pairs = [(g * half + i, g * half + (i + step) % half) for g in range(2) for i in range(half)]
        pieces[step] = lax.ppermute(pieces[step], "pln", pairs)
    for step in range(half):
        pieces[half + step] = lax.ppermute(pieces[half + step], "pln", [(0, half + step), (half, step)])
    pieces[:half] = [p.reshape(plan.ky_block * slots, grid) for p in pieces[:half]]

    small = pltpu.CompilerParams(vmem_limit_bytes=SMALL)
    span = SUB * box
    shapes = [(plan.doubled, 2 * grid), (2 * grid, plan.doubled), (grid, 3 * plan.doubled), (3 * plan.doubled, grid)]
    shapes += [(span, 3 * span), (span, 3 * span), (grid, 3 * grid)]
    tables = pl.pallas_call(
        functools.partial(tables_kernel, plan),
        in_specs=[smem, anywhere],
        out_specs=[vmem] * (len(shapes) + 1),
        out_shape=[*[jax.ShapeDtypeStruct(shape, BF16) for shape in shapes], jax.ShapeDtypeStruct(pieces[0].shape, F32)],
        scratch_shapes=[dma((1,))],
        compiler_params=small,
        name="tables",
    )(where, pieces[0])
    pieces[0] = tables[7]
    chips = orb // 2
    single = jax.ShapeDtypeStruct((groups, area, grid), BF16)
    send = pl.pallas_call(
        functools.partial(solve_kernel, plan),
        in_specs=[smem] + [vmem] * (5 + 2 * half),
        out_specs=[vmem] * (1 + chips),
        out_shape=[single] * 2 + [jax.ShapeDtypeStruct((2, groups, area, grid), BF16)] * (chips - 1),
        scratch_shapes=[
            pltpu.VMEM((grid * slots, grid), F32),
            pltpu.VMEM((grid * slots, grid), F32),
            pltpu.VMEM((2 * orb * groups, grid), jnp.int32),
            pltpu.SMEM((2 * orb * groups, grid), jnp.int32),
            dma,
        ],
        compiler_params=small,
        name="solve",
    )(where, received, *pieces, *tables[:4])
    own, swap, *send = send
    core_pairs = [(o, o ^ 1) for o in range(orb)]
    arrived = [None] * (chips - 1)
    for e in reversed(range(1, chips)):
        arrived[e - 1] = lax.ppermute(send[e - 1], "orb", [(o, o ^ (2 * e)) for o in range(orb)])
    gathered = pl.pallas_call(
        gather_kernel,
        in_specs=[vmem] * chips,
        out_specs=vmem,
        out_shape=jax.ShapeDtypeStruct((chips, groups, area, grid), BF16),
        compiler_params=small,
        name="gather",
    )(swap, *arrived)
    other = lax.ppermute(gathered, "orb", core_pairs)
    part = plan.box_part * count
    finished = pl.pallas_call(
        functools.partial(terms_kernel, plan),
        grid=(groups,),
        in_specs=[
            smem,
            pl.BlockSpec((1, area, grid), lambda g: (g, 0, 0)),
            pl.BlockSpec((chips, 1, area, grid), lambda g: (0, g, 0, 0)),
            *[pl.BlockSpec((1, 1, area, grid), lambda g: (0, g, 0, 0))] * (chips - 1),
            anywhere,
            pl.BlockSpec((1, plan.rows, grid), lambda g: (g, 0, 0)),
            vmem,
            vmem,
            vmem,
        ],
        out_specs=[pl.BlockSpec((1, part, box * box), lambda g: (g, 0, 0))] * pln,
        out_shape=[jax.ShapeDtypeStruct((groups, part, box * box), BF16 if step else F32) for step in range(pln)],
        scratch_shapes=[
            pltpu.VMEM((box, box, grid), F32),
            pltpu.VMEM((box, box, grid), F32),
            pltpu.VMEM((pln, part, box * box), F32),
            dma,
        ],
        compiler_params=small,
        name="terms",
    )(where, own, other, *arrived, psi, wave, *tables[4:7])
    finished = list(finished)
    for step in range(1, pln):
        finished[step] = lax.ppermute(finished[step], "pln", [(p, (p + step) % pln) for p in range(pln)])
    cells = plan.box_part * box * box
    result = pl.pallas_call(
        functools.partial(sum_kernel, plan),
        grid=(groups,),
        in_specs=[pl.BlockSpec((1, part, box * box), lambda g: (g, 0, 0))] * pln,
        out_specs=pl.BlockSpec((1, count, cells), lambda g: (g, 0, 0)),
        out_shape=jax.ShapeDtypeStruct((groups, count, cells), BF16),
        compiler_params=small,
        name="sum",
    )(*finished)
    return result.reshape(groups * count, cells)


def solution(mesh):
    in_specs = (P("orb", None), P("orb"), P("orb", None), P(None, "pln", "orb"))
    out_specs = P("orb", "pln")

    def whole(orbitals, occupations, box_offsets, kernel_spectrum):
        plan = Plan(mesh, orbitals.shape, kernel_spectrum.shape)
        return jax.shard_map(
            functools.partial(per_device, plan), mesh=mesh, in_specs=in_specs, out_specs=out_specs, check_vma=False
        )(orbitals, occupations, box_offsets, kernel_spectrum)

    return whole
```

```python
import functools
import math

import jax
import jax.numpy as jnp
import numpy as np
from jax import lax
from jax.experimental import pallas as pl
from jax.experimental.pallas import tpu as pltpu
from jax.sharding import PartitionSpec as P

MAGIC_TAPS = (
    8.433424733352934e-07,
    -1.290557201342061e-05,
    8.76298447621056e-05,
    -0.00030158038132690465,
    0.001747237136729939,
    -0.009420470302010804,
    0.023738214637249424,
    0.0612625895831208,
    0.9940415697834004,
    -0.06048952891969835,
    -0.021030251609303816,
    0.013372634148547948,
    -0.0034412814449349387,
    0.0004944322768868992,
    -5.185986881173433e-05,
    2.7273449291197967e-06,
)
F32 = jnp.float32
BF16 = jnp.bfloat16
SUB = 8
LARGE = 60 * 1024 * 1024
SMALL = 32 * 1024 * 1024


def magic_filter(box):
    table = np.zeros((box, box))
    for row in range(box):
        for tap in range(-8, 8):
            if 0 <= row + tap < box:
                table[row, row + tap] = MAGIC_TAPS[tap + 8]
    return table.astype(np.float32).astype(np.float64)


def cas(product, doubled):
    angle = 2.0 * math.pi * (product % doubled) / doubled
    return np.cos(angle) + np.sin(angle)


def halves(table):
    high = np.asarray(table, np.float32).astype(jnp.bfloat16)
    low = (np.asarray(table, np.float64) - high.astype(np.float64)).astype(jnp.bfloat16)
    return high, low


def split(values):
    high = values.astype(BF16)
    low = (values - high.astype(F32)).astype(BF16)
    return high, low


def dot(left, right, dims=((1,), (0,))):
    return lax.dot_general(left, right, (dims, ((), ())), preferred_element_type=F32)


def terms_of(values, axis):
    high, low = split(values)
    return jnp.concatenate([high, high, low], axis=axis)


def stacked(table, axis):
    high, low = halves(table)
    return np.concatenate([high, low, high], axis=axis)


SINE = (1.0, -1.0 / 6, 1.0 / 120, -1.0 / 5040, 1.0 / 362880)
COSINE = (1.0, -1.0 / 2, 1.0 / 24, -1.0 / 720, 1.0 / 40320)


def turn(steps, doubled):
    quarter = doubled // 4
    place = (steps + quarter // 2) & (doubled - 1)
    quadrant = place // quarter
    angle = (place - quadrant * quarter - quarter // 2).astype(F32) * (2.0 * math.pi / doubled)
    square = angle * angle
    cosine, sine = COSINE[-1], SINE[-1]
    for even, odd in zip(COSINE[-2::-1], SINE[-2::-1]):
        cosine, sine = cosine * square + even, sine * square + odd
    return quadrant, cosine, sine * angle


def cosine_table(steps, doubled):
    quadrant, cosine, sine = turn(steps, doubled)
    value = jnp.where((quadrant & 1) == 0, cosine, -sine)
    return jnp.where(quadrant < 2, value, -value)


def cas_table(steps, doubled):
    quadrant, cosine, sine = turn(steps, doubled)
    value = jnp.where((quadrant & 1) == 0, cosine + sine, cosine - sine)
    return jnp.where(quadrant < 2, value, -value)


def iota(shape, axis):
    return lax.broadcasted_iota(jnp.int32, shape, axis)


def stack_terms(table, axis):
    high, low = split(table)
    return jnp.concatenate([high, low, high], axis=axis)


def tap_table(step):
    value = jnp.zeros(step.shape, F32)
    for tap in range(-8, 8):
        value = jnp.where(step == tap, np.float32(MAGIC_TAPS[tap + 8]), value)
    return value


def inner_back_table(box):
    span = SUB * box
    one = tap_table(iota((box, span), 0) - (iota((box, span), 1) & (box - 1)))
    whole = jnp.concatenate([one] * SUB, axis=0)
    return jnp.where(iota((span, span), 0) // box == iota((span, span), 1) // box, whole, 0.0)


def outer_back_table(box):
    span = SUB * box
    row, column = iota((span, span), 0), iota((span, span), 1)
    value = tap_table(row // SUB - column // SUB)
    return jnp.where((row & (SUB - 1)) == (column & (SUB - 1)), value, 0.0)


def depth_back_table(plan):
    grid, box, count = plan.grid, plan.box, plan.per_group
    row, column = iota((grid, grid), 0), iota((grid, grid), 1)
    value = tap_table(row // count - (column & (box - 1)))
    return jnp.where((row & (count - 1)) == column // box, value, 0.0)


def mode_table(plan, me, shape, axis):
    grid, doubled, half = plan.grid, plan.doubled, plan.half
    line = tuple(doubled if dim == axis else 1 for dim in range(2))
    group, index = me // half, lax.rem(me, half)
    mode = iota(line, axis)
    within = mode & (grid - 1)
    block = (index - within // plan.ky_block + half) & (half - 1)
    step = block * plan.ky_block + (within & (plan.ky_block - 1))
    edge = (mode >= grid) & (step == 0)
    frequency = jnp.where(edge, ((1 - group) * grid), group * grid + step)
    quarter = jnp.where((mode >= grid) & (step != 0), doubled // 4, 0)
    weight = jnp.where(step == 0, 1.0, 2.0)
    return cosine_table(frequency * iota(shape, 1 - axis) - quarter, doubled), weight


def depth_mode_table(plan, shape, axis):
    grid, doubled = plan.grid, plan.doubled
    place = iota(shape, axis)
    frequency = jnp.where(place < grid, place, grid - place)
    return jnp.where(place == grid, 0.0, cas_table(frequency * iota(shape, 1 - axis), doubled))


def side_by_side(table, parts):
    results = []
    for first, second in zip(parts[::2], parts[1::2]):
        width = first.shape[1]
        out = dot(table, terms_of(jnp.concatenate([first, second], axis=1), 0))
        results += [out[:, :width], out[:, width:]]
    return results


class Plan:
    def __init__(self, mesh, orbital_shape, kernel_shape):
        self.orb = mesh.shape["orb"]
        self.pln = mesh.shape["pln"]
        self.doubled = doubled = kernel_shape[0]
        self.grid = grid = doubled // 2
        self.box = box = round(orbital_shape[1] ** (1 / 3))
        self.per_group = grid // box
        self.groups = orbital_shape[0] // self.orb // self.per_group
        self.ky_block = kernel_shape[1] // self.pln
        self.kx_block = kernel_shape[2] // self.orb
        self.slots = SUB * -(-self.kx_block // (SUB * self.pln))
        self.half = self.pln // 2
        self.rows = self.orb * self.slots
        self.area = box * self.slots
        self.box_part = box // self.pln
        magic = magic_filter(box)
        eye = np.eye(SUB)
        depth = np.zeros((box, self.per_group, self.per_group, box))
        for n in range(self.per_group):
            depth[:, n, n, :] = magic.T
        depth = depth.reshape(grid, grid)
        self.depth = np.concatenate(halves(depth), axis=0)
        self.inner = stacked(np.kron(eye, magic), 1)
        self.outer = stacked(np.kron(magic, eye), 1)
        places = np.arange(grid)
        wave = np.zeros((self.pln, self.orb, self.slots, grid))
        for p in range(self.pln):
            for s in range(self.slots):
                within = p * self.slots + s
                if within < self.kx_block:
                    k = self.kx_block * np.arange(self.orb) + within
                    wave[p, :, s, :] = cas(k[:, None] * places[None, :], doubled)
        self.wave = wave.reshape(self.pln, self.rows, grid).astype(np.float32)
        self.quarter = box // 4


def lane_owner(shape, box):
    return lax.broadcasted_iota(jnp.int32, shape, len(shape) - 1) // box


def start_copies(sems, first, *pairs):
    copies = []
    for number, (source, target) in enumerate(pairs):
        copy = pltpu.make_async_copy(source, target, sems.at[first + number])
        copy.start()
        copies.append(copy)
    return copies


def wait_copies(copies):
    for copy in copies:
        copy.wait()


def density_kernel(
    plan, where_ref, corner_ref, weight_ref, coef_any, depth_any, inner_any, outer_any, wave_any, spectrum_any,
    send_any, psi_any, wave_out_any, *refs,
):
    half = plan.half
    piece_anys = refs[: 2 * half]
    coef_ref, depth_ref, inner_ref, outer_ref, wave_ref, own_wave_ref, stage_ref, psi_ref, send_ref = refs[2 * half : -7]
    block_ref, edge_ref, block_out_ref, edge_out_ref, spectrum_sems, out_sems, sems = refs[-7:]
    box, grid, count, slots = plan.box, plan.grid, plan.per_group, plan.slots
    section = box * box
    span = SUB * box
    me = lax.rem(where_ref[0], plan.pln)
    coef_copy = pltpu.make_async_copy(coef_any, coef_ref, sems.at[0])
    coef_copy.start()
    fetched = start_copies(
        sems, 1, (depth_any, depth_ref), (inner_any, inner_ref), (outer_any, outer_ref), (wave_any.at[me], wave_ref)
    )
    spectrum = spectrum_copies(plan, me, spectrum_any, block_ref, edge_ref, spectrum_sems)
    for copy in spectrum:
        copy.start()
    owner = lane_owner((1, grid), box)
    owner_pair = jnp.concatenate([owner, owner], axis=1)
    coef_copy.wait()
    wait_copies(fetched[:1])
    for group in range(plan.groups):
        for p in range(box):
            stage_ref[count * p : count * (p + 1), :] = coef_ref[group, :, section * p : section * (p + 1)].astype(F32)
        coef = stage_ref[...].astype(BF16)
        first = dot(jnp.concatenate([coef, coef], axis=0), depth_ref[...], ((0,), (0,)))
        if group == 0:
            wait_copies(fetched[1:])
        inner, outer = inner_ref[...], outer_ref[...]
        second = side_by_side(inner, [first[span * t : span * (t + 1)] for t in range(box // SUB)])
        second = jnp.concatenate(second, axis=0).reshape(box, box // SUB, SUB, grid)
        third = side_by_side(outer, [second[:, t].reshape(span, grid) for t in range(box // SUB)])
        for t in range(box // SUB):
            psi_ref[:, SUB * t : SUB * (t + 1), :] = third[t].reshape(box, SUB, grid)
        sent = start_copies(sems, 5, (psi_ref, psi_any.at[group]))
        whole_wave = wave_ref[...]
        wave = jnp.zeros_like(whole_wave)
        weight = jnp.zeros((1, grid), F32)
        wave_terms = []
        kind = iota((2 * SUB, 1), 0)
        corner = jnp.zeros((2 * SUB, grid), F32)
        for n in range(count):
            number = group * count + n
            every = jnp.zeros_like(whole_wave)
            for block in range(count):
                shift = lax.rem(box * block - corner_ref[number, 2] + grid, grid)
                every = jnp.where(owner == block, pltpu.roll(whole_wave, shift, 1), every)
            high, low = split(every)
            wave_terms.append(jnp.where((owner & 1) == 0, high.astype(F32), low.astype(F32)).astype(BF16))
            wave = jnp.where(owner == n, every, wave)
            weight = jnp.where(owner == n, weight_ref[number], weight)
            place = jnp.where(kind == 0, corner_ref[number, 0], corner_ref[number, 1])
            corner = jnp.where(owner == n, place.astype(F32), corner)
        own_wave_ref[...] = wave
        sent += start_copies(sems, 6, (own_wave_ref, wave_out_any.at[group]))
        for o in range(plan.orb):
            send_ref[o, plan.area :, :] = corner.astype(send_ref.dtype)
        wave_terms = jnp.concatenate(wave_terms, axis=0)
        if group == 0:
            wait_copies(spectrum)
            folded = fold_spectrum(plan, piece_anys, block_ref, edge_ref, block_out_ref, edge_out_ref, out_sems)
        rows = pl.ds(plan.area, 2 * SUB)
        sent += start_copies(sems, 7, (send_ref.at[:, rows, :], send_any.at[:, group, rows, :]))
        per_part = plan.quarter // 2
        for pair in range(box // 2):
            columns = [psi_ref[b] * psi_ref[b] * weight for b in (2 * pair, 2 * pair + 1)]
            up, down = split(jnp.concatenate(columns, axis=1))
            out = dot(wave_terms, jnp.concatenate([up, up, down, down], axis=0))
            mine = out[: plan.rows]
            for n in range(1, count):
                mine = jnp.where(owner_pair == n, out[plan.rows * n : plan.rows * (n + 1)], mine)
            for o in range(plan.orb):
                part = mine[slots * o : slots * (o + 1)]
                tile = jnp.concatenate([part[:, :grid], part[:, grid:]], axis=0)
                send_ref[o, 2 * slots * pair : 2 * slots * (pair + 1), :] = tile.astype(send_ref.dtype)
            if pair % per_part == per_part - 1:
                part = pair // per_part
                rows = pl.ds(plan.quarter * slots * part, plan.quarter * slots)
                sent += start_copies(sems, 8 + part, (send_ref.at[:, rows, :], send_any.at[:, group, rows, :]))
        wait_copies(sent)
    wait_copies(folded)


def spectrum_copies(plan, me, spectrum_any, block_ref, edge_ref, sems):
    half, slots = plan.half, plan.slots
    group, index = me // half, lax.rem(me, half)

    def fetch(target, source, buffer, number):
        first = jnp.minimum(target * slots, max(plan.kx_block - slots, 0))
        first = pl.multiple_of(first, SUB)
        return pltpu.make_async_copy(source.at[:, pl.ds(first, slots), :], buffer, sems.at[number])

    copies = []
    for step in range(half):
        copies.append(fetch(group * half + lax.rem(index + step, half), spectrum_any, block_ref.at[step], step))
    for step in range(half):
        target = (1 - group) * half + step
        copies.append(fetch(target, spectrum_any.at[pl.ds(0, 1)], edge_ref.at[pl.ds(step, 1)], half + step))
    return copies


def fold_spectrum(plan, piece_anys, block_ref, edge_ref, block_out_ref, edge_out_ref, sems):
    half, grid = plan.half, plan.grid
    odd = (iota((1, 1, grid), 2) & 1) == 1

    def fold(values):
        last = values[..., grid : grid + 1]
        return values[..., :grid] + jnp.where(odd, last, -last)

    for step in range(half):
        block_out_ref[step] = fold(block_ref[step])
    edge_out_ref[...] = fold(edge_ref[...])
    pairs = [(block_out_ref.at[step], piece_anys[step]) for step in range(half)]
    pairs += [(edge_out_ref.at[pl.ds(step, 1)], piece_anys[half + step]) for step in range(half)]
    return start_copies(sems, 0, *pairs)


def tables_kernel(plan, where_ref, piece_any, *refs):
    forward_y_ref, forward_z_ref, inverse_y_ref, inverse_z_ref, inner_ref, outer_ref, back_ref = refs[:7]
    piece_ref, sems = refs[7:]
    grid, doubled, me = plan.grid, plan.doubled, lax.rem(where_ref[0], plan.pln)
    copies = start_copies(sems, 0, (piece_any, piece_ref))
    forward, _ = mode_table(plan, me, (doubled, grid), 0)
    forward_y_ref[...] = jnp.concatenate(split(forward), axis=1)
    forward_z_ref[...] = jnp.concatenate(split(depth_mode_table(plan, (grid, doubled), 1)), axis=0)
    inverse, weight = mode_table(plan, me, (grid, doubled), 1)
    inverse_y_ref[...] = stack_terms(inverse * (weight * (1.0 / doubled**3)), 1)
    inverse_z_ref[...] = stack_terms(depth_mode_table(plan, (doubled, grid), 0), 0)
    inner_ref[...] = stack_terms(inner_back_table(plan.box), 1)
    outer_ref[...] = stack_terms(outer_back_table(plan.box), 1)
    back_ref[...] = stack_terms(depth_back_table(plan), 1)
    wait_copies(copies)


def solve_kernel(plan, where_ref, recv_ref, *refs):
    half, slots, grid, box, count = plan.half, plan.slots, plan.grid, plan.box, plan.per_group
    piece_refs, edge_refs = refs[:half], refs[half : 2 * half]
    forward_y_ref, forward_z_ref, inverse_y_ref, inverse_z_ref = refs[2 * half : 2 * half + 4]
    chips = plan.orb // 2
    own_ref, swap_ref, *send_refs = refs[2 * half + 4 : 2 * half + 5 + chips]
    field_ref, result_ref, table_ref, corner_ref, sem = refs[2 * half + 5 + chips :]
    me, own = lax.rem(where_ref[0], plan.pln), where_ref[0] // plan.pln
    depth = plan.area
    all_groups = plan.orb * plan.groups
    owner = lane_owner((1, grid), box)
    for group in range(all_groups):
        tile = recv_ref[group, depth : depth + 2 * SUB, :].astype(F32).astype(jnp.int32)
        table_ref[2 * group : 2 * group + 2, :] = tile[:2]
    copy = pltpu.make_async_copy(table_ref, corner_ref, sem)
    copy.start()
    field_ref[...] = jnp.zeros_like(field_ref)
    forward_y, forward_z = forward_y_ref[...], forward_z_ref[...]
    inverse_y, inverse_z = inverse_y_ref[...], inverse_z_ref[...]
    copy.wait()

    def start(group, n):
        return pl.multiple_of(corner_ref[2 * group + 1, box * n] * slots, SUB)

    def place(group, carry):
        values = recv_ref[group, :depth, :]
        for n in range(count):
            shift = lax.rem(corner_ref[2 * group, box * n] - box * n + grid, grid)
            moved = pltpu.roll(jnp.where(owner == n, values, jnp.zeros_like(values)), shift, 1)
            field_ref[pl.ds(start(group, n), depth), :] += moved.astype(F32)
        return carry

    if plan.groups == 1:
        for group in range(all_groups):
            place(group, 0)
    else:
        lax.fori_loop(0, all_groups, place, 0)
    row = iota((grid, 1), 0)
    edge_row = lax.rem(me, half) * plan.ky_block
    edges = edge_refs[0][0]
    for ref in edge_refs[1:]:
        edges = edges + ref[0]
    batch = slots
    for first in range(0, slots, batch):
        rows, spectra = [], []
        for s in range(first, first + batch, 2):
            planes = [field_ref[pl.ds(t, grid, stride=slots), :] for t in (s, s + 1)]
            planes = jnp.concatenate(planes, axis=1).astype(BF16)
            modes = dot(forward_y, jnp.concatenate([planes, planes], axis=0)).astype(BF16)
            rows += [modes[:, :grid], modes[:, grid:]]
        for s in range(first, first + batch):
            spectrum = jnp.concatenate([ref[pl.ds(s, plan.ky_block, stride=slots), :] for ref in piece_refs], axis=0)
            spectra += [spectrum, jnp.where(row == edge_row, edges[s : s + 1], spectrum)]
        rows, spectra = jnp.concatenate(rows, axis=0), jnp.concatenate(spectra, axis=0)
        modes = dot(jnp.concatenate([rows, rows], axis=1), forward_z) * jnp.concatenate([spectra, spectra], axis=1)
        back = dot(terms_of(modes, 1), inverse_z)
        for t in range(0, batch, 2):
            size = 2 * grid
            both = [back[size * u : size * (u + 1)] for u in (t, t + 1)]
            planes = dot(inverse_y, terms_of(jnp.concatenate(both, axis=1), 0))
            for side in range(2):
                result_ref[pl.ds(first + t + side, grid, stride=slots), :] = planes[:, grid * side : grid * (side + 1)]

    def cut(d, group, carry):
        number = (own ^ d) * plan.groups + group
        values = jnp.zeros((depth, grid), BF16)
        for n in range(count):
            shift = lax.rem(box * n - corner_ref[2 * number, box * n] + grid, grid)
            rows = result_ref[pl.ds(start(number, n), depth), :].astype(BF16)
            values = jnp.where(owner == n, pltpu.roll(rows, shift, 1), values)
        if d < 2:
            (own_ref, swap_ref)[d][group] = values
        else:
            send_refs[d // 2 - 1][d % 2, group] = values
        return carry

    for d in range(plan.orb):
        if plan.groups == 1:
            cut(d, 0, 0)
        else:
            lax.fori_loop(0, plan.groups, functools.partial(cut, d), 0)


def gather_kernel(swap_ref, *refs):
    out_ref = refs[-1]
    out_ref[0] = swap_ref[...]
    for number, ref in enumerate(refs[:-1]):
        out_ref[number + 1] = ref[1]


def terms_kernel(plan, where_ref, *refs):
    box, grid, count, slots, pln = plan.box, plan.grid, plan.per_group, plan.slots, plan.pln
    chips = plan.orb // 2
    own_ref, other_ref, *chip_refs = refs[: chips + 1]
    psi_any, wave_ref, inner_ref, outer_ref, back_ref, *refs = refs[chips + 1 :]

    def tile(d, rows):
        if d % 2:
            return other_ref[d // 2, 0, rows]
        return chip_refs[d // 2 - 1][0, 0, rows] if d else own_ref[0, rows]

    out_refs = refs[:pln]
    psi_ref, stage_ref, result_ref, sem = refs[pln:]
    group = pl.program_id(0)
    copy = pltpu.make_async_copy(psi_any.at[group], psi_ref, sem)
    copy.start()
    owner = lane_owner((1, grid), box)
    own = where_ref[0] // pln
    rows = [wave_ref[0, pl.ds(pl.multiple_of((own ^ d) * slots, SUB), slots), :] for d in range(plan.orb)]
    wave = jnp.concatenate(split(jnp.concatenate(rows, axis=0).T), axis=1)
    inner, outer, back = inner_ref[...], outer_ref[...], back_ref[...]
    copy.wait()
    for pair in range(box // 2):
        tiles = [tile(d, pl.ds(2 * slots * pair, 2 * slots)).astype(F32) for d in range(plan.orb)]
        columns = [jnp.concatenate([t[slots * side : slots * (side + 1)] for t in tiles], axis=0) for side in range(2)]
        both = jnp.concatenate(columns, axis=1).astype(BF16)
        out = dot(wave, jnp.concatenate([both, both], axis=0))
        for side, b in enumerate((2 * pair, 2 * pair + 1)):
            mine = out[:, grid * side : grid * (side + 1)]
            potential = jnp.zeros((box, grid), F32)
            for n in range(count):
                potential = jnp.where(owner == n, mine[box * n : box * (n + 1)], potential)
            stage_ref[b] = potential * psi_ref[b]
    span = SUB * box
    second = side_by_side(inner, [stage_ref[SUB * t : SUB * (t + 1)].reshape(span, grid) for t in range(box // SUB)])
    second = jnp.concatenate(second, axis=0).reshape(box, box // SUB, SUB, grid)
    third = side_by_side(outer, [second[:, t].reshape(span, grid) for t in range(box // SUB)])
    for t in range(box // SUB):
        stage_ref[:, SUB * t : SUB * (t + 1), :] = third[t].reshape(box, SUB, grid)
    values = terms_of(stage_ref[...].reshape(box * box, grid), 1)
    out = dot(back, values, ((1,), (1,)))
    part = plan.box_part * count
    for p in range(pln):
        result_ref[p] = out[part * p : part * (p + 1)]
    me = lax.rem(where_ref[0], pln)
    out_refs[0][0] = result_ref[me]
    for step in range(1, pln):
        out_refs[step][0] = result_ref[lax.rem(me + step, pln)].astype(BF16)


def sum_kernel(plan, *refs):
    out_ref = refs[plan.pln]
    total = refs[0][0]
    for ref in refs[1 : plan.pln]:
        total = total + ref[0].astype(F32)
    section = plan.box * plan.box
    count = plan.per_group
    for j in range(plan.box_part):
        out_ref[0, :, section * j : section * (j + 1)] = total[count * j : count * (j + 1)].astype(out_ref.dtype)


def per_device(plan, orbitals, occupations, box_offsets, kernel_spectrum):
    orb, pln, half, slots = plan.orb, plan.pln, plan.half, plan.slots
    groups, count, box, grid = plan.groups, plan.per_group, plan.box, plan.grid
    plane_index = lax.axis_index("pln")
    where = (lax.axis_index("orb") * pln + plane_index).astype(jnp.int32)[None]
    smem = pl.BlockSpec(memory_space=pltpu.SMEM)
    anywhere = pl.BlockSpec(memory_space=pl.ANY)
    vmem = pl.BlockSpec(memory_space=pltpu.VMEM)
    dma = pltpu.SemaphoreType.DMA
    coefs = orbitals.reshape(groups, count, orbitals.shape[1])
    by_ky = jnp.transpose(kernel_spectrum, (1, 2, 0))
    area = plan.area
    padded = area + 2 * SUB
    tables = [plan.depth, plan.inner, plan.outer]
    piece = jax.ShapeDtypeStruct((plan.ky_block, slots, grid), F32)
    edge = jax.ShapeDtypeStruct((1, slots, grid), F32)
    send, psi, wave, *pieces = pl.pallas_call(
        functools.partial(density_kernel, plan),
        in_specs=[smem, smem, smem] + [anywhere] * 6,
        out_specs=[anywhere] * (3 + 2 * half),
        out_shape=[
            jax.ShapeDtypeStruct((orb, groups, padded, grid), BF16),
            jax.ShapeDtypeStruct((groups, box, box, grid), F32),
            jax.ShapeDtypeStruct((groups, plan.rows, grid), F32),
            *[piece] * half,
            *[edge] * half,
        ],
        scratch_shapes=[
            pltpu.VMEM(coefs.shape, BF16),
            *[pltpu.VMEM(t.shape, t.dtype) for t in tables],
            pltpu.VMEM((plan.rows, grid), F32),
            pltpu.VMEM((plan.rows, grid), F32),
            pltpu.VMEM((grid, box * box), F32),
            pltpu.VMEM((box, box, grid), F32),
            pltpu.VMEM((orb, padded, grid), BF16),
            pltpu.VMEM((half, plan.ky_block, slots, plan.doubled), F32),
            pltpu.VMEM((half, slots, plan.doubled), F32),
            pltpu.VMEM((half, plan.ky_block, slots, grid), F32),
            pltpu.VMEM((half, slots, grid), F32),
            dma((2 * half,)),
            dma((2 * half,)),
            dma((12,)),
        ],
        compiler_params=pltpu.CompilerParams(vmem_limit_bytes=LARGE),
        name="density",
    )(where, box_offsets, occupations, coefs, *tables, plan.wave, by_ky)
    received = lax.all_to_all(send, "orb", split_axis=0, concat_axis=0, tiled=True)
    received = received.reshape(orb * groups, padded, grid)
    for step in range(1, half):
        pairs = [(g * half + i, g * half + (i + step) % half) for g in range(2) for i in range(half)]
        pieces[step] = lax.ppermute(pieces[step], "pln", pairs)
    for step in reversed(range(half)):
        pieces[half + step] = lax.ppermute(pieces[half + step], "pln", [(0, half + step), (half, step)])
    pieces[:half] = [p.reshape(plan.ky_block * slots, grid) for p in pieces[:half]]

    small = pltpu.CompilerParams(vmem_limit_bytes=SMALL)
    span = SUB * box
    shapes = [(plan.doubled, 2 * grid), (2 * grid, plan.doubled), (grid, 3 * plan.doubled), (3 * plan.doubled, grid)]
    shapes += [(span, 3 * span), (span, 3 * span), (grid, 3 * grid)]
    tables = pl.pallas_call(
        functools.partial(tables_kernel, plan),
        in_specs=[smem, anywhere],
        out_specs=[vmem] * (len(shapes) + 1),
        out_shape=[*[jax.ShapeDtypeStruct(shape, BF16) for shape in shapes], jax.ShapeDtypeStruct(pieces[0].shape, F32)],
        scratch_shapes=[dma((1,))],
        compiler_params=small,
        name="tables",
    )(where, pieces[0])
    pieces[0] = tables[7]
    chips = orb // 2
    single = jax.ShapeDtypeStruct((groups, area, grid), BF16)
    send = pl.pallas_call(
        functools.partial(solve_kernel, plan),
        in_specs=[smem] + [vmem] * (5 + 2 * half),
        out_specs=[vmem] * (1 + chips),
        out_shape=[single] * 2 + [jax.ShapeDtypeStruct((2, groups, area, grid), BF16)] * (chips - 1),
        scratch_shapes=[
            pltpu.VMEM((grid * slots, grid), F32),
            pltpu.VMEM((grid * slots, grid), F32),
            pltpu.VMEM((2 * orb * groups, grid), jnp.int32),
            pltpu.SMEM((2 * orb * groups, grid), jnp.int32),
            dma,
        ],
        compiler_params=small,
        name="solve",
    )(where, received, *pieces, *tables[:4])
    own, swap, *send = send
    core_pairs = [(o, o ^ 1) for o in range(orb)]
    arrived = [None] * (chips - 1)
    for e in reversed(range(1, chips)):
        arrived[e - 1] = lax.ppermute(send[e - 1], "orb", [(o, o ^ (2 * e)) for o in range(orb)])
    gathered = pl.pallas_call(
        gather_kernel,
        in_specs=[vmem] * chips,
        out_specs=vmem,
        out_shape=jax.ShapeDtypeStruct((chips, groups, area, grid), BF16),
        compiler_params=small,
        name="gather",
    )(swap, *arrived)
    other = lax.ppermute(gathered, "orb", core_pairs)
    part = plan.box_part * count
    finished = pl.pallas_call(
        functools.partial(terms_kernel, plan),
        grid=(groups,),
        in_specs=[
            smem,
            pl.BlockSpec((1, area, grid), lambda g: (g, 0, 0)),
            pl.BlockSpec((chips, 1, area, grid), lambda g: (0, g, 0, 0)),
            *[pl.BlockSpec((1, 1, area, grid), lambda g: (0, g, 0, 0))] * (chips - 1),
            anywhere,
            pl.BlockSpec((1, plan.rows, grid), lambda g: (g, 0, 0)),
            vmem,
            vmem,
            vmem,
        ],
        out_specs=[pl.BlockSpec((1, part, box * box), lambda g: (g, 0, 0))] * pln,
        out_shape=[jax.ShapeDtypeStruct((groups, part, box * box), BF16 if step else F32) for step in range(pln)],
        scratch_shapes=[
            pltpu.VMEM((box, box, grid), F32),
            pltpu.VMEM((box, box, grid), F32),
            pltpu.VMEM((pln, part, box * box), F32),
            dma,
        ],
        compiler_params=small,
        name="terms",
    )(where, own, other, *arrived, psi, wave, *tables[4:7])
    finished = list(finished)
    for step in range(1, pln):
        finished[step] = lax.ppermute(finished[step], "pln", [(p, (p + step) % pln) for p in range(pln)])
    cells = plan.box_part * box * box
    result = pl.pallas_call(
        functools.partial(sum_kernel, plan),
        grid=(groups,),
        in_specs=[pl.BlockSpec((1, part, box * box), lambda g: (g, 0, 0))] * pln,
        out_specs=pl.BlockSpec((1, count, cells), lambda g: (g, 0, 0)),
        out_shape=jax.ShapeDtypeStruct((groups, count, cells), BF16),
        compiler_params=small,
        name="sum",
    )(*finished)
    return result.reshape(groups * count, cells)


def solution(mesh):
    in_specs = (P("orb", None), P("orb"), P("orb", None), P(None, "pln", "orb"))
    out_specs = P("orb", "pln")

    def whole(orbitals, occupations, box_offsets, kernel_spectrum):
        plan = Plan(mesh, orbitals.shape, kernel_spectrum.shape)
        return jax.shard_map(
            functools.partial(per_device, plan), mesh=mesh, in_specs=in_specs, out_specs=out_specs, check_vma=False
        )(orbitals, occupations, box_offsets, kernel_spectrum)

    return whole
```

```python
import functools
import math

import jax
import jax.numpy as jnp
import numpy as np
from jax import lax
from jax.experimental import pallas as pl
from jax.experimental.pallas import tpu as pltpu
from jax.sharding import PartitionSpec as P

MAGIC_TAPS = (
    8.433424733352934e-07,
    -1.290557201342061e-05,
    8.76298447621056e-05,
    -0.00030158038132690465,
    0.001747237136729939,
    -0.009420470302010804,
    0.023738214637249424,
    0.0612625895831208,
    0.9940415697834004,
    -0.06048952891969835,
    -0.021030251609303816,
    0.013372634148547948,
    -0.0034412814449349387,
    0.0004944322768868992,
    -5.185986881173433e-05,
    2.7273449291197967e-06,
)
F32 = jnp.float32
BF16 = jnp.bfloat16
SUB = 8
LARGE = 60 * 1024 * 1024
SMALL = 32 * 1024 * 1024


def magic_filter(box):
    table = np.zeros((box, box))
    for row in range(box):
        for tap in range(-8, 8):
            if 0 <= row + tap < box:
                table[row, row + tap] = MAGIC_TAPS[tap + 8]
    return table.astype(np.float32).astype(np.float64)


def cas(product, doubled):
    angle = 2.0 * math.pi * (product % doubled) / doubled
    return np.cos(angle) + np.sin(angle)


def halves(table):
    high = np.asarray(table, np.float32).astype(jnp.bfloat16)
    low = (np.asarray(table, np.float64) - high.astype(np.float64)).astype(jnp.bfloat16)
    return high, low


def split(values):
    high = values.astype(BF16)
    low = (values - high.astype(F32)).astype(BF16)
    return high, low


def dot(left, right, dims=((1,), (0,))):
    return lax.dot_general(left, right, (dims, ((), ())), preferred_element_type=F32)


def terms_of(values, axis):
    high, low = split(values)
    return jnp.concatenate([high, high, low], axis=axis)


def stacked(table, axis):
    high, low = halves(table)
    return np.concatenate([high, low, high], axis=axis)


SINE = (1.0, -1.0 / 6, 1.0 / 120, -1.0 / 5040, 1.0 / 362880)
COSINE = (1.0, -1.0 / 2, 1.0 / 24, -1.0 / 720, 1.0 / 40320)


def turn(steps, doubled):
    quarter = doubled // 4
    place = (steps + quarter // 2) & (doubled - 1)
    quadrant = place // quarter
    angle = (place - quadrant * quarter - quarter // 2).astype(F32) * (2.0 * math.pi / doubled)
    square = angle * angle
    cosine, sine = COSINE[-1], SINE[-1]
    for even, odd in zip(COSINE[-2::-1], SINE[-2::-1]):
        cosine, sine = cosine * square + even, sine * square + odd
    return quadrant, cosine, sine * angle


def cosine_table(steps, doubled):
    quadrant, cosine, sine = turn(steps, doubled)
    value = jnp.where((quadrant & 1) == 0, cosine, -sine)
    return jnp.where(quadrant < 2, value, -value)


def cas_table(steps, doubled):
    quadrant, cosine, sine = turn(steps, doubled)
    value = jnp.where((quadrant & 1) == 0, cosine + sine, cosine - sine)
    return jnp.where(quadrant < 2, value, -value)


def iota(shape, axis):
    return lax.broadcasted_iota(jnp.int32, shape, axis)


def stack_terms(table, axis):
    high, low = split(table)
    return jnp.concatenate([high, low, high], axis=axis)


def tap_table(step):
    value = jnp.zeros(step.shape, F32)
    for tap in range(-8, 8):
        value = jnp.where(step == tap, np.float32(MAGIC_TAPS[tap + 8]), value)
    return value


def inner_back_table(box):
    span = SUB * box
    one = tap_table(iota((box, span), 0) - (iota((box, span), 1) & (box - 1)))
    whole = jnp.concatenate([one] * SUB, axis=0)
    return jnp.where(iota((span, span), 0) // box == iota((span, span), 1) // box, whole, 0.0)


def outer_back_table(box):
    span = SUB * box
    row, column = iota((span, span), 0), iota((span, span), 1)
    value = tap_table(row // SUB - column // SUB)
    return jnp.where((row & (SUB - 1)) == (column & (SUB - 1)), value, 0.0)


def depth_back_table(plan):
    grid, box, count = plan.grid, plan.box, plan.per_group
    row, column = iota((grid, grid), 0), iota((grid, grid), 1)
    value = tap_table(row // count - (column & (box - 1)))
    return jnp.where((row & (count - 1)) == column // box, value, 0.0)


def mode_table(plan, me, shape, axis):
    grid, doubled, half = plan.grid, plan.doubled, plan.half
    line = tuple(doubled if dim == axis else 1 for dim in range(2))
    group, index = me // half, lax.rem(me, half)
    mode = iota(line, axis)
    within = mode & (grid - 1)
    block = (index - within // plan.ky_block + half) & (half - 1)
    step = block * plan.ky_block + (within & (plan.ky_block - 1))
    edge = (mode >= grid) & (step == 0)
    frequency = jnp.where(edge, ((1 - group) * grid), group * grid + step)
    quarter = jnp.where((mode >= grid) & (step != 0), doubled // 4, 0)
    weight = jnp.where(step == 0, 1.0, 2.0)
    return cosine_table(frequency * iota(shape, 1 - axis) - quarter, doubled), weight


def depth_mode_table(plan, shape, axis):
    grid, doubled = plan.grid, plan.doubled
    place = iota(shape, axis)
    frequency = jnp.where(place < grid, place, grid - place)
    return jnp.where(place == grid, 0.0, cas_table(frequency * iota(shape, 1 - axis), doubled))


def side_by_side(table, parts):
    results = []
    for first, second in zip(parts[::2], parts[1::2]):
        width = first.shape[1]
        out = dot(table, terms_of(jnp.concatenate([first, second], axis=1), 0))
        results += [out[:, :width], out[:, width:]]
    return results


class Plan:
    def __init__(self, mesh, orbital_shape, kernel_shape):
        self.orb = mesh.shape["orb"]
        self.pln = mesh.shape["pln"]
        self.doubled = doubled = kernel_shape[0]
        self.grid = grid = doubled // 2
        self.box = box = round(orbital_shape[1] ** (1 / 3))
        self.per_group = grid // box
        self.groups = orbital_shape[0] // self.orb // self.per_group
        self.ky_block = kernel_shape[1] // self.pln
        self.kx_block = kernel_shape[2] // self.orb
        self.slots = SUB * -(-self.kx_block // (SUB * self.pln))
        self.half = self.pln // 2
        self.rows = self.orb * self.slots
        self.area = box * self.slots
        self.box_part = box // self.pln
        magic = magic_filter(box)
        eye = np.eye(SUB)
        depth = np.zeros((box, self.per_group, self.per_group, box))
        for n in range(self.per_group):
            depth[:, n, n, :] = magic.T
        depth = depth.reshape(grid, grid)
        self.depth = np.concatenate(halves(depth), axis=0)
        self.inner = stacked(np.kron(eye, magic), 1)
        self.outer = stacked(np.kron(magic, eye), 1)
        places = np.arange(grid)
        wave = np.zeros((self.pln, self.orb, self.slots, grid))
        for p in range(self.pln):
            for s in range(self.slots):
                within = p * self.slots + s
                if within < self.kx_block:
                    k = self.kx_block * np.arange(self.orb) + within
                    wave[p, :, s, :] = cas(k[:, None] * places[None, :], doubled)
        self.wave = wave.reshape(self.pln, self.rows, grid).astype(np.float32)
        self.quarter = box // 4


def lane_owner(shape, box):
    return lax.broadcasted_iota(jnp.int32, shape, len(shape) - 1) // box


def start_copies(sems, first, *pairs):
    copies = []
    for number, (source, target) in enumerate(pairs):
        copy = pltpu.make_async_copy(source, target, sems.at[first + number])
        copy.start()
        copies.append(copy)
    return copies


def wait_copies(copies):
    for copy in copies:
        copy.wait()


def density_kernel(
    plan, where_ref, corner_ref, weight_ref, coef_any, depth_any, inner_any, outer_any, wave_any, spectrum_any,
    send_any, psi_any, wave_out_any, *refs,
):
    half = plan.half
    piece_anys = refs[: 2 * half]
    coef_ref, depth_ref, inner_ref, outer_ref, wave_ref, own_wave_ref, stage_ref, psi_ref, send_ref = refs[2 * half : -7]
    block_ref, edge_ref, block_out_ref, edge_out_ref, spectrum_sems, out_sems, sems = refs[-7:]
    box, grid, count, slots = plan.box, plan.grid, plan.per_group, plan.slots
    section = box * box
    span = SUB * box
    me = lax.rem(where_ref[0], plan.pln)
    coef_copy = pltpu.make_async_copy(coef_any, coef_ref, sems.at[0])
    coef_copy.start()
    fetched = start_copies(
        sems, 1, (depth_any, depth_ref), (inner_any, inner_ref), (outer_any, outer_ref), (wave_any.at[me], wave_ref)
    )
    spectrum = spectrum_copies(plan, me, spectrum_any, block_ref, edge_ref, spectrum_sems)
    for copy in spectrum:
        copy.start()
    owner = lane_owner((1, grid), box)
    owner_pair = jnp.concatenate([owner, owner], axis=1)
    coef_copy.wait()
    wait_copies(fetched[:1])
    for group in range(plan.groups):
        for p in range(box):
            stage_ref[count * p : count * (p + 1), :] = coef_ref[group, :, section * p : section * (p + 1)].astype(F32)
        coef = stage_ref[...].astype(BF16)
        first = dot(jnp.concatenate([coef, coef], axis=0), depth_ref[...], ((0,), (0,)))
        if group == 0:
            wait_copies(fetched[1:])
        inner, outer = inner_ref[...], outer_ref[...]
        second = side_by_side(inner, [first[span * t : span * (t + 1)] for t in range(box // SUB)])
        second = jnp.concatenate(second, axis=0).reshape(box, box // SUB, SUB, grid)
        third = side_by_side(outer, [second[:, t].reshape(span, grid) for t in range(box // SUB)])
        for t in range(box // SUB):
            psi_ref[:, SUB * t : SUB * (t + 1), :] = third[t].reshape(box, SUB, grid)
        sent = start_copies(sems, 5, (psi_ref, psi_any.at[group]))
        whole_wave = wave_ref[...]
        wave = jnp.zeros_like(whole_wave)
        weight = jnp.zeros((1, grid), F32)
        wave_terms = []
        kind = iota((2 * SUB, 1), 0)
        corner = jnp.zeros((2 * SUB, grid), F32)
        for n in range(count):
            number = group * count + n
            every = jnp.zeros_like(whole_wave)
            for block in range(count):
                shift = lax.rem(box * block - corner_ref[number, 2] + grid, grid)
                every = jnp.where(owner == block, pltpu.roll(whole_wave, shift, 1), every)
            high, low = split(every)
            wave_terms.append(jnp.where((owner & 1) == 0, high.astype(F32), low.astype(F32)).astype(BF16))
            wave = jnp.where(owner == n, every, wave)
            weight = jnp.where(owner == n, weight_ref[number], weight)
            place = jnp.where(kind == 0, corner_ref[number, 0], corner_ref[number, 1])
            corner = jnp.where(owner == n, place.astype(F32), corner)
        own_wave_ref[...] = wave
        sent += start_copies(sems, 6, (own_wave_ref, wave_out_any.at[group]))
        for o in range(plan.orb):
            send_ref[o, plan.area :, :] = corner.astype(send_ref.dtype)
        wave_terms = jnp.concatenate(wave_terms, axis=0)
        if group == 0:
            wait_copies(spectrum)
            folded = fold_spectrum(plan, piece_anys, block_ref, edge_ref, block_out_ref, edge_out_ref, out_sems)
        rows = pl.ds(plan.area, 2 * SUB)
        sent += start_copies(sems, 7, (send_ref.at[:, rows, :], send_any.at[:, group, rows, :]))
        per_part = plan.quarter // 2
        for pair in range(box // 2):
            columns = [psi_ref[b] * psi_ref[b] * weight for b in (2 * pair, 2 * pair + 1)]
            up, down = split(jnp.concatenate(columns, axis=1))
            out = dot(wave_terms, jnp.concatenate([up, up, down, down], axis=0))
            mine = out[: plan.rows]
            for n in range(1, count):
                mine = jnp.where(owner_pair == n, out[plan.rows * n : plan.rows * (n + 1)], mine)
            for o in range(plan.orb):
                part = mine[slots * o : slots * (o + 1)]
                tile = jnp.concatenate([part[:, :grid], part[:, grid:]], axis=0)
                send_ref[o, 2 * slots * pair : 2 * slots * (pair + 1), :] = tile.astype(send_ref.dtype)
            if pair % per_part == per_part - 1:
                part = pair // per_part
                rows = pl.ds(plan.quarter * slots * part, plan.quarter * slots)
                sent += start_copies(sems, 8 + part, (send_ref.at[:, rows, :], send_any.at[:, group, rows, :]))
        wait_copies(sent)
    wait_copies(folded)


def spectrum_copies(plan, me, spectrum_any, block_ref, edge_ref, sems):
    half, slots = plan.half, plan.slots
    group, index = me // half, lax.rem(me, half)

    def fetch(target, source, buffer, number):
        first = jnp.minimum(target * slots, max(plan.kx_block - slots, 0))
        first = pl.multiple_of(first, SUB)
        return pltpu.make_async_copy(source.at[:, pl.ds(first, slots), :], buffer, sems.at[number])

    copies = []
    for step in range(half):
        copies.append(fetch(group * half + lax.rem(index + step, half), spectrum_any, block_ref.at[step], step))
    for step in range(half):
        target = (1 - group) * half + step
        copies.append(fetch(target, spectrum_any.at[pl.ds(0, 1)], edge_ref.at[pl.ds(step, 1)], half + step))
    return copies


def fold_spectrum(plan, piece_anys, block_ref, edge_ref, block_out_ref, edge_out_ref, sems):
    half, grid = plan.half, plan.grid
    odd = (iota((1, 1, grid), 2) & 1) == 1

    def fold(values):
        last = values[..., grid : grid + 1]
        return values[..., :grid] + jnp.where(odd, last, -last)

    for step in range(half):
        block_out_ref[step] = fold(block_ref[step])
    edge_out_ref[...] = fold(edge_ref[...])
    pairs = [(block_out_ref.at[step], piece_anys[step]) for step in range(half)]
    pairs += [(edge_out_ref.at[pl.ds(step, 1)], piece_anys[plan.pln - 1 - step]) for step in range(half)]
    return start_copies(sems, 0, *pairs)


def tables_kernel(plan, where_ref, piece_any, *refs):
    forward_y_ref, forward_z_ref, inverse_y_ref, inverse_z_ref, inner_ref, outer_ref, back_ref = refs[:7]
    piece_ref, sems = refs[7:]
    grid, doubled, me = plan.grid, plan.doubled, lax.rem(where_ref[0], plan.pln)
    copies = start_copies(sems, 0, (piece_any, piece_ref))
    forward, _ = mode_table(plan, me, (doubled, grid), 0)
    forward_y_ref[...] = jnp.concatenate(split(forward), axis=1)
    forward_z_ref[...] = jnp.concatenate(split(depth_mode_table(plan, (grid, doubled), 1)), axis=0)
    inverse, weight = mode_table(plan, me, (grid, doubled), 1)
    inverse_y_ref[...] = stack_terms(inverse * (weight * (1.0 / doubled**3)), 1)
    inverse_z_ref[...] = stack_terms(depth_mode_table(plan, (doubled, grid), 0), 0)
    inner_ref[...] = stack_terms(inner_back_table(plan.box), 1)
    outer_ref[...] = stack_terms(outer_back_table(plan.box), 1)
    back_ref[...] = stack_terms(depth_back_table(plan), 1)
    wait_copies(copies)


def solve_kernel(plan, where_ref, recv_ref, *refs):
    half, slots, grid, box, count = plan.half, plan.slots, plan.grid, plan.box, plan.per_group
    piece_refs, edge_refs = refs[:half], refs[half : 2 * half]
    forward_y_ref, forward_z_ref, inverse_y_ref, inverse_z_ref = refs[2 * half : 2 * half + 4]
    chips = plan.orb // 2
    own_ref, swap_ref, *send_refs = refs[2 * half + 4 : 2 * half + 5 + chips]
    field_ref, result_ref, table_ref, corner_ref, sem = refs[2 * half + 5 + chips :]
    me, own = lax.rem(where_ref[0], plan.pln), where_ref[0] // plan.pln
    depth = plan.area
    all_groups = plan.orb * plan.groups
    owner = lane_owner((1, grid), box)
    for group in range(all_groups):
        tile = recv_ref[group, depth : depth + 2 * SUB, :].astype(F32).astype(jnp.int32)
        table_ref[2 * group : 2 * group + 2, :] = tile[:2]
    copy = pltpu.make_async_copy(table_ref, corner_ref, sem)
    copy.start()
    field_ref[...] = jnp.zeros_like(field_ref)
    forward_y, forward_z = forward_y_ref[...], forward_z_ref[...]
    inverse_y, inverse_z = inverse_y_ref[...], inverse_z_ref[...]
    copy.wait()

    def start(group, n):
        return pl.multiple_of(corner_ref[2 * group + 1, box * n] * slots, SUB)

    def place(group, carry):
        values = recv_ref[group, :depth, :]
        for n in range(count):
            shift = lax.rem(corner_ref[2 * group, box * n] - box * n + grid, grid)
            moved = pltpu.roll(jnp.where(owner == n, values, jnp.zeros_like(values)), shift, 1)
            field_ref[pl.ds(start(group, n), depth), :] += moved.astype(F32)
        return carry

    if plan.groups == 1:
        for group in range(all_groups):
            place(group, 0)
    else:
        lax.fori_loop(0, all_groups, place, 0)
    row = iota((grid, 1), 0)
    edge_row = lax.rem(me, half) * plan.ky_block
    edges = edge_refs[0][0]
    for ref in edge_refs[1:]:
        edges = edges + ref[0]
    batch = slots
    for first in range(0, slots, batch):
        rows, spectra = [], []
        for s in range(first, first + batch, 2):
            planes = [field_ref[pl.ds(t, grid, stride=slots), :] for t in (s, s + 1)]
            planes = jnp.concatenate(planes, axis=1).astype(BF16)
            modes = dot(forward_y, jnp.concatenate([planes, planes], axis=0)).astype(BF16)
            rows += [modes[:, :grid], modes[:, grid:]]
        for s in range(first, first + batch):
            spectrum = jnp.concatenate([ref[pl.ds(s, plan.ky_block, stride=slots), :] for ref in piece_refs], axis=0)
            spectra += [spectrum, jnp.where(row == edge_row, edges[s : s + 1], spectrum)]
        rows, spectra = jnp.concatenate(rows, axis=0), jnp.concatenate(spectra, axis=0)
        modes = dot(jnp.concatenate([rows, rows], axis=1), forward_z) * jnp.concatenate([spectra, spectra], axis=1)
        back = dot(terms_of(modes, 1), inverse_z)
        for t in range(0, batch, 2):
            size = 2 * grid
            both = [back[size * u : size * (u + 1)] for u in (t, t + 1)]
            planes = dot(inverse_y, terms_of(jnp.concatenate(both, axis=1), 0))
            for side in range(2):
                result_ref[pl.ds(first + t + side, grid, stride=slots), :] = planes[:, grid * side : grid * (side + 1)]

    def cut(d, group, carry):
        number = (own ^ d) * plan.groups + group
        values = jnp.zeros((depth, grid), BF16)
        for n in range(count):
            shift = lax.rem(box * n - corner_ref[2 * number, box * n] + grid, grid)
            rows = result_ref[pl.ds(start(number, n), depth), :].astype(BF16)
            values = jnp.where(owner == n, pltpu.roll(rows, shift, 1), values)
        if d < 2:
            (own_ref, swap_ref)[d][group] = values
        else:
            send_refs[d // 2 - 1][d % 2, group] = values
        return carry

    for d in range(plan.orb):
        if plan.groups == 1:
            cut(d, 0, 0)
        else:
            lax.fori_loop(0, plan.groups, functools.partial(cut, d), 0)


def gather_kernel(swap_ref, *refs):
    out_ref = refs[-1]
    out_ref[0] = swap_ref[...]
    for number, ref in enumerate(refs[:-1]):
        out_ref[number + 1] = ref[1]


def terms_kernel(plan, where_ref, *refs):
    box, grid, count, slots, pln = plan.box, plan.grid, plan.per_group, plan.slots, plan.pln
    chips = plan.orb // 2
    own_ref, other_ref, *chip_refs = refs[: chips + 1]
    psi_any, wave_ref, inner_ref, outer_ref, back_ref, *refs = refs[chips + 1 :]

    def tile(d, rows):
        if d % 2:
            return other_ref[d // 2, 0, rows]
        return chip_refs[d // 2 - 1][0, 0, rows] if d else own_ref[0, rows]

    out_refs = refs[:pln]
    psi_ref, stage_ref, result_ref, sem = refs[pln:]
    group = pl.program_id(0)
    copy = pltpu.make_async_copy(psi_any.at[group], psi_ref, sem)
    copy.start()
    owner = lane_owner((1, grid), box)
    own = where_ref[0] // pln
    rows = [wave_ref[0, pl.ds(pl.multiple_of((own ^ d) * slots, SUB), slots), :] for d in range(plan.orb)]
    wave = jnp.concatenate(split(jnp.concatenate(rows, axis=0).T), axis=1)
    inner, outer, back = inner_ref[...], outer_ref[...], back_ref[...]
    copy.wait()
    for pair in range(box // 2):
        tiles = [tile(d, pl.ds(2 * slots * pair, 2 * slots)).astype(F32) for d in range(plan.orb)]
        columns = [jnp.concatenate([t[slots * side : slots * (side + 1)] for t in tiles], axis=0) for side in range(2)]
        both = jnp.concatenate(columns, axis=1).astype(BF16)
        out = dot(wave, jnp.concatenate([both, both], axis=0))
        for side, b in enumerate((2 * pair, 2 * pair + 1)):
            mine = out[:, grid * side : grid * (side + 1)]
            potential = jnp.zeros((box, grid), F32)
            for n in range(count):
                potential = jnp.where(owner == n, mine[box * n : box * (n + 1)], potential)
            stage_ref[b] = potential * psi_ref[b]
    span = SUB * box
    second = side_by_side(inner, [stage_ref[SUB * t : SUB * (t + 1)].reshape(span, grid) for t in range(box // SUB)])
    second = jnp.concatenate(second, axis=0).reshape(box, box // SUB, SUB, grid)
    third = side_by_side(outer, [second[:, t].reshape(span, grid) for t in range(box // SUB)])
    for t in range(box // SUB):
        stage_ref[:, SUB * t : SUB * (t + 1), :] = third[t].reshape(box, SUB, grid)
    values = terms_of(stage_ref[...].reshape(box * box, grid), 1)
    out = dot(back, values, ((1,), (1,)))
    part = plan.box_part * count
    for p in range(pln):
        result_ref[p] = out[part * p : part * (p + 1)]
    me = lax.rem(where_ref[0], pln)
    out_refs[0][0] = result_ref[me]
    for step in range(1, pln):
        out_refs[step][0] = result_ref[lax.rem(me + step, pln)].astype(BF16)


def sum_kernel(plan, *refs):
    out_ref = refs[plan.pln]
    total = refs[0][0]
    for ref in refs[1 : plan.pln]:
        total = total + ref[0].astype(F32)
    section = plan.box * plan.box
    count = plan.per_group
    for j in range(plan.box_part):
        out_ref[0, :, section * j : section * (j + 1)] = total[count * j : count * (j + 1)].astype(out_ref.dtype)


def per_device(plan, orbitals, occupations, box_offsets, kernel_spectrum):
    orb, pln, half, slots = plan.orb, plan.pln, plan.half, plan.slots
    groups, count, box, grid = plan.groups, plan.per_group, plan.box, plan.grid
    plane_index = lax.axis_index("pln")
    where = (lax.axis_index("orb") * pln + plane_index).astype(jnp.int32)[None]
    smem = pl.BlockSpec(memory_space=pltpu.SMEM)
    anywhere = pl.BlockSpec(memory_space=pl.ANY)
    vmem = pl.BlockSpec(memory_space=pltpu.VMEM)
    dma = pltpu.SemaphoreType.DMA
    coefs = orbitals.reshape(groups, count, orbitals.shape[1])
    by_ky = jnp.transpose(kernel_spectrum, (1, 2, 0))
    area = plan.area
    padded = area + 2 * SUB
    tables = [plan.depth, plan.inner, plan.outer]
    piece = jax.ShapeDtypeStruct((plan.ky_block, slots, grid), F32)
    edge = jax.ShapeDtypeStruct((1, slots, grid), F32)
    send, psi, wave, *pieces = pl.pallas_call(
        functools.partial(density_kernel, plan),
        in_specs=[smem, smem, smem] + [anywhere] * 6,
        out_specs=[anywhere] * (3 + 2 * half),
        out_shape=[
            jax.ShapeDtypeStruct((orb, groups, padded, grid), BF16),
            jax.ShapeDtypeStruct((groups, box, box, grid), F32),
            jax.ShapeDtypeStruct((groups, plan.rows, grid), F32),
            *[piece] * half,
            *[edge] * half,
        ],
        scratch_shapes=[
            pltpu.VMEM(coefs.shape, BF16),
            *[pltpu.VMEM(t.shape, t.dtype) for t in tables],
            pltpu.VMEM((plan.rows, grid), F32),
            pltpu.VMEM((plan.rows, grid), F32),
            pltpu.VMEM((grid, box * box), F32),
            pltpu.VMEM((box, box, grid), F32),
            pltpu.VMEM((orb, padded, grid), BF16),
            pltpu.VMEM((half, plan.ky_block, slots, plan.doubled), F32),
            pltpu.VMEM((half, slots, plan.doubled), F32),
            pltpu.VMEM((half, plan.ky_block, slots, grid), F32),
            pltpu.VMEM((half, slots, grid), F32),
            dma((2 * half,)),
            dma((2 * half,)),
            dma((12,)),
        ],
        compiler_params=pltpu.CompilerParams(vmem_limit_bytes=LARGE),
        name="density",
    )(where, box_offsets, occupations, coefs, *tables, plan.wave, by_ky)
    received = lax.all_to_all(send, "orb", split_axis=0, concat_axis=0, tiled=True)
    received = received.reshape(orb * groups, padded, grid)
    for step in range(1, half):
        pairs = [(g * half + i, g * half + (i + step) % half) for g in range(2) for i in range(half)]
        pieces[step] = lax.ppermute(pieces[step], "pln", pairs)
    for step in reversed(range(half)):
        place = pln - 1 - step
        pieces[place] = lax.ppermute(pieces[place], "pln", [(0, half + step), (half, step)])
    pieces[:half] = [p.reshape(plan.ky_block * slots, grid) for p in pieces[:half]]

    small = pltpu.CompilerParams(vmem_limit_bytes=SMALL)
    span = SUB * box
    shapes = [(plan.doubled, 2 * grid), (2 * grid, plan.doubled), (grid, 3 * plan.doubled), (3 * plan.doubled, grid)]
    shapes += [(span, 3 * span), (span, 3 * span), (grid, 3 * grid)]
    tables = pl.pallas_call(
        functools.partial(tables_kernel, plan),
        in_specs=[smem, anywhere],
        out_specs=[vmem] * (len(shapes) + 1),
        out_shape=[*[jax.ShapeDtypeStruct(shape, BF16) for shape in shapes], jax.ShapeDtypeStruct(pieces[0].shape, F32)],
        scratch_shapes=[dma((1,))],
        compiler_params=small,
        name="tables",
    )(where, pieces[0])
    pieces[0] = tables[7]
    chips = orb // 2
    single = jax.ShapeDtypeStruct((groups, area, grid), BF16)
    send = pl.pallas_call(
        functools.partial(solve_kernel, plan),
        in_specs=[smem] + [vmem] * (5 + 2 * half),
        out_specs=[vmem] * (1 + chips),
        out_shape=[single] * 2 + [jax.ShapeDtypeStruct((2, groups, area, grid), BF16)] * (chips - 1),
        scratch_shapes=[
            pltpu.VMEM((grid * slots, grid), F32),
            pltpu.VMEM((grid * slots, grid), F32),
            pltpu.VMEM((2 * orb * groups, grid), jnp.int32),
            pltpu.SMEM((2 * orb * groups, grid), jnp.int32),
            dma,
        ],
        compiler_params=small,
        name="solve",
    )(where, received, *pieces, *tables[:4])
    own, swap, *send = send
    core_pairs = [(o, o ^ 1) for o in range(orb)]
    arrived = [None] * (chips - 1)
    for e in reversed(range(1, chips)):
        arrived[e - 1] = lax.ppermute(send[e - 1], "orb", [(o, o ^ (2 * e)) for o in range(orb)])
    gathered = pl.pallas_call(
        gather_kernel,
        in_specs=[vmem] * chips,
        out_specs=vmem,
        out_shape=jax.ShapeDtypeStruct((chips, groups, area, grid), BF16),
        compiler_params=small,
        name="gather",
    )(swap, *arrived)
    other = lax.ppermute(gathered, "orb", core_pairs)
    part = plan.box_part * count
    finished = pl.pallas_call(
        functools.partial(terms_kernel, plan),
        grid=(groups,),
        in_specs=[
            smem,
            pl.BlockSpec((1, area, grid), lambda g: (g, 0, 0)),
            pl.BlockSpec((chips, 1, area, grid), lambda g: (0, g, 0, 0)),
            *[pl.BlockSpec((1, 1, area, grid), lambda g: (0, g, 0, 0))] * (chips - 1),
            anywhere,
            pl.BlockSpec((1, plan.rows, grid), lambda g: (g, 0, 0)),
            vmem,
            vmem,
            vmem,
        ],
        out_specs=[pl.BlockSpec((1, part, box * box), lambda g: (g, 0, 0))] * pln,
        out_shape=[jax.ShapeDtypeStruct((groups, part, box * box), BF16 if step else F32) for step in range(pln)],
        scratch_shapes=[
            pltpu.VMEM((box, box, grid), F32),
            pltpu.VMEM((box, box, grid), F32),
            pltpu.VMEM((pln, part, box * box), F32),
            dma,
        ],
        compiler_params=small,
        name="terms",
    )(where, own, other, *arrived, psi, wave, *tables[4:7])
    finished = list(finished)
    for step in range(1, pln):
        finished[step] = lax.ppermute(finished[step], "pln", [(p, (p + step) % pln) for p in range(pln)])
    cells = plan.box_part * box * box
    result = pl.pallas_call(
        functools.partial(sum_kernel, plan),
        grid=(groups,),
        in_specs=[pl.BlockSpec((1, part, box * box), lambda g: (g, 0, 0))] * pln,
        out_specs=pl.BlockSpec((1, count, cells), lambda g: (g, 0, 0)),
        out_shape=jax.ShapeDtypeStruct((groups, count, cells), BF16),
        compiler_params=small,
        name="sum",
    )(*finished)
    return result.reshape(groups * count, cells)


def solution(mesh):
    in_specs = (P("orb", None), P("orb"), P("orb", None), P(None, "pln", "orb"))
    out_specs = P("orb", "pln")

    def whole(orbitals, occupations, box_offsets, kernel_spectrum):
        plan = Plan(mesh, orbitals.shape, kernel_spectrum.shape)
        return jax.shard_map(
            functools.partial(per_device, plan), mesh=mesh, in_specs=in_specs, out_specs=out_specs, check_vma=False
        )(orbitals, occupations, box_offsets, kernel_spectrum)

    return whole
```
